128 devices in a mesh: chan: 64 (over z, y, x), row: 2 (over core).
Axes of the slice: x: 4, y: 4, z: 4, core: 2. Of those that a mesh axis runs over, the one named last changes fastest.
Arguments:
- generator: bfloat16 [64, 1280, 1280], P('chan', 'row'), may hold values from -0.25155765 to 0.25155765, as said below
- magnus_old: bfloat16 [64, 1280, 1280], P('chan', 'row'), may hold values from -0.25155765 to 0.25155765, as said below
- hamiltonian: bfloat16 [64, 1280, 1280], P('chan', 'row'), may hold values from -9 to 9, as said below
- chan_of_slot: int32 [64], P('chan'), may hold values from 0 to 63, each once
- chan_dims: int32 [64], replicated, may hold values from 160 to 1280, as said below
- pp_factor: float32 [64, 1280], replicated, may hold values from -1 to 1, as said below
- cc_factor: float32 [64, 1280], P('chan'), may hold values from -1 to 1, as said below
- send_table: int32 [64, 64, 3], P('chan'), may hold values from 0 to 160, as said below
- recv_table: int32 [64, 160], P('chan'), may hold values from 0 to 191, as said below
- pandya_weight: float32 [64, 160], P('chan'), may hold values from 0.5 to 2
Outputs:
- magnus_new: bfloat16 [64, 1280, 1280], P('chan', 'row')
- flowed: bfloat16 [64, 1280, 1280], P('chan', 'row')
The draws below stay inside these ranges and needn't reach their ends.
Inputs may be any that keep to these rules, and one draw needn't show every extreme that they name: `generator`: antisymmetric in its last two dimensions. `magnus_old`: antisymmetric in its last two dimensions. `hamiltonian`: symmetric in its last two dimensions. `chan_dims`: live order of each channel; one channel has exactly 1280. `pp_factor`: every entry is -1, 0 or 1. `cc_factor`: every entry is -1, 0 or 1. send_table[p, d, l] is the local tile that group p sends to group d in slot l; 160 marks an empty slot; each local tile is sent exactly once; every group fills all 3 slots towards some peer. recv_table[d, v] = p * 3 + l names a filled slot of send_table[p, d, l]; every group receives exactly 160 tiles, each filled slot once.
All inputs are finite; a program needn't handle non-finite values.
Results may differ from the reference program's by a relative error of at most 0.0065.
Values may be sent and summed in bfloat16 or wider, within the bound.
A program may use at most 128 MiB of HBM per device.

```python
import jax
import jax.numpy as jnp
from jax import lax

M = 1280
TR = 40
COLT = 128
CH_DEV = 1
CH = 64
TILES_DEV = 160
SLOTS = 3
N_CHAN = 64
N_ROW = 2


def spread_offsets():
    tile_ids = jnp.arange(TILES_DEV, dtype=jnp.int32)
    if TILES_DEV >= N_CHAN:
        return tile_ids % N_CHAN
    lower = 1 + tile_ids * (N_CHAN - 1) // TILES_DEV
    upper = (tile_ids + 1) * (N_CHAN - 1) // TILES_DEV
    return jnp.where(tile_ids <= TILES_DEV // 2, lower, upper).astype(jnp.int32)


def pandya_plan(key):
    key_offsets, key_orders, key_places = jax.random.split(key, 3)
    offsets = spread_offsets()[jax.random.permutation(key_offsets, TILES_DEV)].astype(jnp.int32)
    orders = jax.vmap(lambda part_key: jax.random.permutation(part_key, TILES_DEV))(jax.random.split(key_orders, N_CHAN)).astype(jnp.int32)
    anchor = jnp.broadcast_to(jnp.arange(N_CHAN, dtype=jnp.int32)[:, None], (N_CHAN, TILES_DEV))
    local_ids = jnp.broadcast_to(jnp.arange(TILES_DEV, dtype=jnp.int32)[None, :], (N_CHAN, TILES_DEV))
    target = (anchor + offsets[orders]) % N_CHAN
    same_target = target[:, :, None] == target[:, None, :]
    earlier = local_ids[:, :, None] > local_ids[:, None, :]
    slot_index = jnp.sum((same_target & earlier).astype(jnp.int32), axis=2)
    send_plan = jnp.full((N_CHAN, N_CHAN, SLOTS), TILES_DEV, jnp.int32).at[anchor, target, slot_index].set(local_ids)
    target_flat = target.reshape(-1)
    order_key = (anchor * SLOTS + slot_index).reshape(-1)
    same_flat = target_flat[:, None] == target_flat[None, :]
    before = order_key[None, :] < order_key[:, None]
    arrival_rank = jnp.sum((same_flat & before).astype(jnp.int32), axis=1)
    places = jax.vmap(lambda part_key: jax.random.permutation(part_key, TILES_DEV))(jax.random.split(key_places, N_CHAN)).astype(jnp.int32)
    position = places[target_flat, arrival_rank]
    recv_plan = jnp.zeros((N_CHAN, TILES_DEV), jnp.int32).at[target_flat, position].set(order_key)
    return (send_plan, recv_plan)


def draw_send_table(key, part):
    plans = pandya_plan(key)
    return plans[0]


def draw_recv_table(key, part):
    plans = pandya_plan(key)
    return plans[1]


def paired_matrix(key, sign, scale):
    base = jnp.clip(jax.random.normal(key, (CH, M, M), jnp.float32), -6.0, 6.0)
    return ((base + sign * jnp.swapaxes(base, 1, 2)) * 0.5 ** 0.5 * scale).astype(jnp.bfloat16)


def draw_generator(key, part):
    key = jax.random.fold_in(key, 21)
    return paired_matrix(key, -1.0, M ** (-0.5))


def draw_magnus_old(key, part):
    key = jax.random.fold_in(key, 22)
    return paired_matrix(key, -1.0, M ** (-0.5))


def draw_hamiltonian(key, part):
    key = jax.random.fold_in(key, 23)
    return paired_matrix(key, 1.0, 1.0)


def draw_chan_dims(key, part):
    key = jax.random.fold_in(key, 11)
    key_sizes, key_largest = jax.random.split(key)
    choice_pick = jax.random.randint(key_sizes, (CH,), 0, 64)
    lowest = M // 8
    order_sizes = lowest + (M - lowest) * choice_pick * choice_pick // 3969
    largest_at = jax.random.randint(key_largest, (), 0, CH)
    return jnp.where(jnp.arange(CH) == largest_at, M, order_sizes).astype(jnp.int32)


def draw_pp_factor(key, part):
    key = jax.random.fold_in(key, 12)
    choice_pick = jax.random.randint(key, (CH, M), 0, 8)
    values = jnp.where(choice_pick < 5, 1.0, jnp.where(choice_pick < 6, -1.0, 0.0))
    return values.astype(jnp.float32)


def draw_cc_factor(key, part):
    key = jax.random.fold_in(key, 13)
    choice_pick = jax.random.randint(key, (CH, M), 0, 4)
    values = jnp.where(choice_pick == 0, -1.0, jnp.where(choice_pick == 1, 1.0, 0.0))
    return values.astype(jnp.float32)


def block_scale(own_key, dims, shards, smallest, top_value):
    level, own = 1.0, jax.random.fold_in(own_key, 6)
    for dim, blocks in shards:
        draws = jnp.exp(jax.random.uniform(jax.random.fold_in(own, dim), (blocks,), jnp.float32, smallest / len(shards), top_value / len(shards)))
        level = level * jnp.repeat(draws, dims[dim] // blocks).reshape([-1 if axis == dim else 1 for axis in range(len(dims))])
    return level


def setup_inputs(seed: int = 0) -> dict:
    key_of = jax.random.split(jax.random.key(seed), 11)
    generator = draw_generator(jax.random.fold_in(key_of[10], 71), 0)
    magnus_old = draw_magnus_old(jax.random.fold_in(key_of[10], 71), 0)
    hamiltonian = draw_hamiltonian(jax.random.fold_in(key_of[10], 71), 0)
    chan_of_slot = jax.random.permutation(key_of[3], CH).astype(jnp.int32)
    chan_dims = draw_chan_dims(jax.random.fold_in(key_of[10], 71), 0)
    pp_factor = draw_pp_factor(jax.random.fold_in(key_of[10], 71), 0)
    cc_factor = draw_cc_factor(jax.random.fold_in(key_of[10], 71), 0)
    send_table = draw_send_table(jax.random.fold_in(key_of[10], 71), 0)
    recv_table = draw_recv_table(jax.random.fold_in(key_of[10], 71), 0)
    pandya_weight = jnp.clip(0.5 + 1.5 * jax.random.uniform(key_of[9], (N_CHAN, TILES_DEV), jnp.float32) ** block_scale(key_of[9], (N_CHAN, TILES_DEV), ((0, 64),), -0.2, 0.2), 0.5, 2.0)
    return dict(generator=generator, magnus_old=magnus_old, hamiltonian=hamiltonian, chan_of_slot=chan_of_slot, chan_dims=chan_dims, pp_factor=pp_factor, cc_factor=cc_factor, send_table=send_table, recv_table=recv_table, pandya_weight=pandya_weight)


STEP_SIZE = 0.5


def to_tiles(matrix):
    strip_rows = M // N_ROW
    tile_grid = matrix.reshape(N_CHAN, CH_DEV, N_ROW, strip_rows // TR, TR, M // COLT, COLT)
    tile_grid = tile_grid.transpose(0, 2, 1, 3, 5, 4, 6)
    return tile_grid.reshape(N_CHAN, N_ROW, TILES_DEV, TR, COLT)


def from_tiles(tile_stack):
    strip_rows = M // N_ROW
    tile_grid = tile_stack.reshape(N_CHAN, N_ROW, CH_DEV, strip_rows // TR, M // COLT, TR, COLT)
    tile_grid = tile_grid.transpose(0, 2, 1, 3, 5, 4, 6)
    return tile_grid.reshape(CH, M, M)


def commutator(left_side, right_side, factor):
    def single(operands):
        left_one, right_one, factor_one = operands
        left_wide = left_one.astype(jnp.float32)
        right_wide = right_one.astype(jnp.float32)
        forward = jnp.dot(left_wide * factor_one[None, :], right_wide)
        backward = jnp.dot(right_wide * factor_one[None, :], left_wide)
        return forward - backward

    return lax.map(single, (left_side, right_side, factor))


def reference(generator, magnus_old, hamiltonian, chan_of_slot, chan_dims, pp_factor, cc_factor, send_table, recv_table, pandya_weight):
    magnus_new = (magnus_old.astype(jnp.float32) + STEP_SIZE * generator.astype(jnp.float32)).astype(jnp.bfloat16)
    limits = chan_dims[chan_of_slot]
    positions = jnp.arange(M, dtype=jnp.int32)
    inside = positions[None, :] < limits[:, None]
    live_mask = inside[:, :, None] & inside[:, None, :]
    zero_half = jnp.zeros((), jnp.bfloat16)
    magnus_live = jnp.where(live_mask, magnus_new, zero_half)
    hamilton_live = jnp.where(live_mask, hamiltonian, zero_half)
    pp_part = commutator(magnus_live, hamilton_live, pp_factor[chan_of_slot])

    source_group = recv_table // SLOTS
    source_slot = recv_table % SLOTS
    target_group = jnp.broadcast_to(jnp.arange(N_CHAN, dtype=jnp.int32)[:, None], recv_table.shape)
    source_tile = send_table[source_group, target_group, source_slot]
    flat_index = (source_group * TILES_DEV + source_tile).reshape(-1).astype(jnp.int32)
    tile_scale = pandya_weight[:, None, :, None, None]

    def regroup(matrix):
        stacked = to_tiles(matrix).transpose(0, 2, 1, 3, 4).reshape(N_CHAN * TILES_DEV, N_ROW, TR, COLT)
        moved_tiles = stacked[flat_index].reshape(N_CHAN, TILES_DEV, N_ROW, TR, COLT).transpose(0, 2, 1, 3, 4)
        return from_tiles((tile_scale * moved_tiles.astype(jnp.float32)).astype(jnp.bfloat16))

    magnus_cross = regroup(magnus_live)
    hamilton_cross = regroup(hamilton_live)
    cross_part = commutator(magnus_cross, hamilton_cross, cc_factor)
    weighted = (tile_scale * to_tiles(cross_part)).astype(jnp.bfloat16)
    weighted = weighted.transpose(0, 2, 1, 3, 4).reshape(N_CHAN * TILES_DEV, N_ROW, TR, COLT)
    returned = jnp.zeros_like(weighted).at[flat_index].set(weighted)
    ph_part = from_tiles(returned.reshape(N_CHAN, TILES_DEV, N_ROW, TR, COLT).transpose(0, 2, 1, 3, 4))
    combined = hamilton_live.astype(jnp.float32) + pp_part + ph_part.astype(jnp.float32)
    flowed = jnp.where(live_mask, combined, jnp.zeros((), jnp.float32)).astype(jnp.bfloat16)
    return magnus_new, flowed
```

```python
import functools

import jax
import jax.numpy as jnp
from jax import lax
from jax.experimental import pallas as pl
from jax.experimental.pallas import tpu as pltpu
from jax.sharding import PartitionSpec as P

TR = 40
COLT = 128
SLOTS = 3
STEP_SIZE = 0.5
PEERS = 64
MULT = 37
MESH = pl.DeviceIdType.MESH
F32 = jnp.float32
BF16 = jnp.bfloat16

ROWS = 640
WIDTH = 1280
BLOCKS = WIDTH // COLT
PAIRS = ROWS // (2 * TR)
TILES = (ROWS // TR) * BLOCKS
PAIR = 2 * TR
BACK = 128
CHUNK = 256


def spin(me, step, sign):
    off = lax.rem(step * MULT, PEERS)
    x = lax.rem(lax.rem(me, 4) + 4 + sign * lax.rem(off, 4), 4)
    y = lax.rem(lax.rem(lax.div(me, 4), 4) + 4 + sign * lax.rem(lax.div(off, 4), 4), 4)
    z = lax.rem(lax.div(me, 16) + 4 + sign * lax.div(off, 16), 4)
    return (z * 4 + y) * 4 + x


def rows_at(start, size, unit):
    return pl.ds(pl.multiple_of(start, unit), size)


def kernel(
    gen, mag, ham, slot_ref, dims_ref, pp_ref, cc_ref, send_ref, recv_ref, weight_ref,
    new_out, flow_out,
    gen_v, mag_v, ham_v, pp_v, stack, sbuf, near, far, right, left, base, cross, tsend, trecv, unpacked,
    inv_v, inv_s,
    in_sem, pp_sem, inv_sem, out_sem, new_sem, self_sem, send_sem, recv_sem, hand_sem, take_sem,
    strip_send, strip_recv, bsend_sem, brecv_sem, bself_sem,
):
    me = lax.axis_index("chan")
    row = lax.axis_index("row")
    other = 1 - row

    def load(i, start):
        for n, (src, dst) in enumerate(((gen, gen_v), (mag, mag_v), (ham, ham_v))):
            at = rows_at(i * PAIR, PAIR, 16)
            copy = pltpu.make_async_copy(src.at[0, at], dst.at[at], in_sem.at[n, i])
            copy.start() if start else copy.wait()

    for i in range(PAIRS):
        load(i, True)
    pp_copy = pltpu.make_async_copy(pp_ref, pp_v, pp_sem)
    pp_copy.start()
    barrier = pltpu.get_barrier_semaphore()

    def greet(step, _):
        pl.semaphore_signal(
            barrier, inc=1, device_id={"chan": spin(me, step, 1)}, device_id_type=MESH
        )
        return 0

    lax.fori_loop(1, PEERS, greet, 0)
    pl.semaphore_signal(barrier, inc=1, device_id={"row": other}, device_id_type=MESH)

    limit = dims_ref[slot_ref[0]]

    def live(i, k):
        row_ids = row * ROWS + i * PAIR + lax.broadcasted_iota(jnp.int32, (PAIR, COLT), 0)
        col_ids = k * COLT + lax.broadcasted_iota(jnp.int32, (PAIR, COLT), 1)
        return (row_ids < limit) & (col_ids < limit)

    def prologue(i, _):
        load(i, False)
        at = rows_at(i * PAIR, PAIR, 16)
        for k in range(BLOCKS):
            col = pl.ds(k * COLT, COLT)
            new = (mag_v[at, col].astype(F32) + STEP_SIZE * gen_v[at, col].astype(F32)).astype(BF16)
            mag_v[at, col] = new
            mask = live(i, k)
            m = jnp.where(mask, new.astype(F32), 0.0)
            h = jnp.where(mask, ham_v[at, col].astype(F32), 0.0)
            for half in range(2):
                cut = slice(half * TR, (half + 1) * TR)
                tile = (2 * i + half) * BLOCKS + k
                stack[tile] = jnp.concatenate([m[cut], h[cut]], axis=0).astype(BF16)
        return 0

    lax.fori_loop(0, PAIRS, prologue, 0)
    new_copy = pltpu.make_async_copy(mag_v, new_out.at[0], new_sem)
    new_copy.start()
    pl.semaphore_wait(barrier, PEERS)

    def pick(to):
        for l in range(SLOTS):
            tile = jnp.minimum(send_ref[0, to, l], TILES - 1)
            sbuf[to * SLOTS + l] = stack[tile]

    def message(step):
        to = spin(me, step, 1)
        return pltpu.make_async_remote_copy(
            sbuf.at[pl.ds(to * SLOTS, SLOTS)],
            near.at[pl.ds(me * SLOTS, SLOTS)],
            send_sem.at[step],
            recv_sem.at[step],
            device_id={"chan": to},
            device_id_type=MESH,
        )

    def arrival(step):
        fr = spin(me, step, -1)
        return pltpu.make_async_remote_copy(
            sbuf.at[pl.ds(fr * SLOTS, SLOTS)],
            near.at[pl.ds(fr * SLOTS, SLOTS)],
            send_sem.at[step],
            recv_sem.at[step],
            device_id={"chan": fr},
            device_id_type=MESH,
        )

    def handed(step):
        at = pl.ds(spin(me, step, -1) * SLOTS, SLOTS)
        return pltpu.make_async_remote_copy(
            near.at[at], far.at[at], hand_sem.at[step], take_sem.at[step],
            device_id={"row": other}, device_id_type=MESH,
        )

    def send_out(step, _):
        pick(spin(me, step, 1))
        message(step).start()
        return 0

    lax.fori_loop(1, PEERS, send_out, 0)
    pick(me)
    mine = pltpu.make_async_copy(
        sbuf.at[pl.ds(me * SLOTS, SLOTS)], near.at[pl.ds(me * SLOTS, SLOTS)], self_sem
    )
    mine.start()

    pp_copy.wait()
    chosen = lax.broadcasted_iota(jnp.int32, pp_v.shape, 0) == slot_ref[0]
    factor = jnp.sum(jnp.where(chosen, pp_v[...], 0.0), axis=0, keepdims=True)

    def strips(i, _):
        at = rows_at(i * PAIR, PAIR, 16)
        for k in range(BLOCKS):
            col = pl.ds(k * COLT, COLT)
            mask = live(i, k)
            m = jnp.where(mask, mag_v[at, col].astype(F32), 0.0)
            h = jnp.where(mask, ham_v[at, col].astype(F32), 0.0)
            f = factor[:, k * COLT : (k + 1) * COLT]
            right[rows_at(row * ROWS + i * PAIR, PAIR, 16), col] = h.astype(BF16)
            right[rows_at(WIDTH + row * ROWS + i * PAIR, PAIR, 16), col] = m.astype(BF16)
            left[at, col] = (m * f).astype(BF16)
            left[at, pl.ds(WIDTH + k * COLT, COLT)] = (h * -f).astype(BF16)
            base[rows_at(k * ROWS + i * PAIR, PAIR, 8), :] = h
        return 0

    lax.fori_loop(0, PAIRS, strips, 0)

    def strip(which, r):
        at = rows_at(which * WIDTH + r * ROWS, ROWS, 16)
        return pltpu.make_async_remote_copy(
            right.at[at], right.at[at], strip_send.at[which], strip_recv.at[which],
            device_id={"row": other}, device_id_type=MESH,
        )

    for which in range(2):
        strip(which, row).start()
    mine.wait()
    handed(0).start()

    place = lax.broadcasted_iota(jnp.int32, (8, COLT), 0) * COLT + lax.broadcasted_iota(
        jnp.int32, (8, COLT), 1
    )

    def invert_recv(v, table):
        return jnp.where(place == recv_ref[0, v], v, table)

    def invert_send(d, table):
        for l in range(SLOTS):
            table = jnp.where(place == send_ref[0, d, l], d * SLOTS + l, table)
        return table

    blank = jnp.zeros((8, COLT), jnp.int32)
    inv_v[0] = lax.fori_loop(0, TILES, invert_recv, blank)
    inv_v[1] = lax.fori_loop(0, PEERS, invert_send, blank)
    inv_copy = pltpu.make_async_copy(inv_v, inv_s, inv_sem)
    inv_copy.start()

    for which in range(2):
        strip(which, other).wait_recv()
        strip(which, row).wait_send()

    def pp_product(n, _):
        col = pl.ds(pl.multiple_of(n * CHUNK, CHUNK), CHUNK)
        part = jnp.dot(left[...], right[:, col], preferred_element_type=F32)
        for half in range(CHUNK // COLT):
            at = rows_at((n * (CHUNK // COLT) + half) * ROWS, ROWS, 8)
            base[at, :] += part[:, half * COLT : (half + 1) * COLT]
        return 0

    lax.fori_loop(0, WIDTH // CHUNK, pp_product, 0)
    inv_copy.wait()

    def hand_on(step, _):
        arrival(step).wait_recv()
        handed(step).start()
        return 0

    lax.fori_loop(1, PEERS, hand_on, 0)

    def settle(tiles, r, own):
        def body(i, _):
            at = rows_at(r * ROWS + i * PAIR, PAIR, 16)
            under = rows_at(WIDTH + r * ROWS + i * PAIR, PAIR, 16)
            for k in range(BLOCKS):
                col = pl.ds(k * COLT, COLT)
                parts = []
                for half in range(2):
                    v = (2 * i + half) * BLOCKS + k
                    tile = tiles[recv_ref[0, v]]
                    parts.append(weight_ref[0, v] * tile.astype(F32))
                m = jnp.concatenate([parts[0][:TR], parts[1][:TR]], axis=0)
                h = jnp.concatenate([parts[0][TR:], parts[1][TR:]], axis=0)
                right[at, col] = h.astype(BF16)
                right[under, col] = m.astype(BF16)
                if own:
                    f = cc_ref[:, k * COLT : (k + 1) * COLT]
                    here = rows_at(i * PAIR, PAIR, 16)
                    left[here, col] = (m * f).astype(BF16)
                    left[here, pl.ds(WIDTH + k * COLT, COLT)] = (h * -f).astype(BF16)
            return 0

        lax.fori_loop(0, PAIRS, body, 0)

    settle(near, row, True)

    def take(step, _):
        handed(step).wait_recv()
        return 0

    lax.fori_loop(0, PEERS, take, 0)
    settle(far, other, False)

    def cc_product(n, _):
        col = pl.ds(pl.multiple_of(n * CHUNK, CHUNK), CHUNK)
        part = jnp.dot(left[...], right[:, col], preferred_element_type=F32)
        for half in range(CHUNK // COLT):
            for a in range(ROWS // TR):
                tile = a * BLOCKS + n * (CHUNK // COLT) + half
                cross[tile] = part[a * TR : (a + 1) * TR, half * COLT : (half + 1) * COLT]
        return 0

    lax.fori_loop(0, WIDTH // CHUNK, cc_product, 0)

    def pick_back(to):
        parts = []
        for l in range(SLOTS):
            slot = to * SLOTS + l
            v = inv_s[0, lax.div(slot, COLT), lax.rem(slot, COLT)]
            parts.append(weight_ref[0, v] * cross[v])
        parts.append(jnp.zeros((BACK - SLOTS * TR, COLT), F32))
        tsend[rows_at(to * BACK, BACK, 16), :] = jnp.concatenate(parts, axis=0).astype(BF16)

    def back(step):
        to = spin(me, step, 1)
        return pltpu.make_async_remote_copy(
            tsend.at[rows_at(to * BACK, BACK, 16)],
            trecv.at[rows_at(me * BACK, BACK, 16)],
            bsend_sem.at[step],
            brecv_sem.at[step],
            device_id={"chan": to},
            device_id_type=MESH,
        )

    def back_arrival(step):
        fr = spin(me, step, -1)
        return pltpu.make_async_remote_copy(
            tsend.at[rows_at(fr * BACK, BACK, 16)],
            trecv.at[rows_at(fr * BACK, BACK, 16)],
            bsend_sem.at[step],
            brecv_sem.at[step],
            device_id={"chan": fr},
            device_id_type=MESH,
        )

    def send_back(step, _):
        pick_back(spin(me, step, 1))
        back(step).start()
        return 0

    lax.fori_loop(1, PEERS, send_back, 0)
    pick_back(me)
    home = pltpu.make_async_copy(
        tsend.at[rows_at(me * BACK, BACK, 16)], trecv.at[rows_at(me * BACK, BACK, 16)], bself_sem
    )
    home.start()

    def unpack(fr):
        rows = trecv[rows_at(fr * BACK, BACK, 16), :].astype(F32)
        for l in range(SLOTS):
            unpacked[fr * SLOTS + l] = rows[l * TR : (l + 1) * TR]

    home.wait()
    unpack(me)

    def take_back(step, _):
        back_arrival(step).wait_recv()
        unpack(spin(me, step, -1))
        return 0

    lax.fori_loop(1, PEERS, take_back, 0)

    def out_copy(i):
        at = rows_at(i * PAIR, PAIR, 16)
        return pltpu.make_async_copy(gen_v.at[at], flow_out.at[0, at], out_sem.at[i])

    def finish(i, _):
        at = rows_at(i * PAIR, PAIR, 16)
        for k in range(BLOCKS):
            parts = []
            for half in range(2):
                u = (2 * i + half) * BLOCKS + k
                slot = inv_s[1, lax.div(u, COLT), lax.rem(u, COLT)]
                parts.append(unpacked[slot])
            total = base[rows_at(k * ROWS + i * PAIR, PAIR, 8), :] + jnp.concatenate(parts, axis=0)
            gen_v[at, pl.ds(k * COLT, COLT)] = jnp.where(live(i, k), total, 0.0).astype(BF16)
        out_copy(i).start()
        return 0

    lax.fori_loop(0, PAIRS, finish, 0)

    def drain(step, _):
        message(step).wait_send()
        handed(step).wait_send()
        back(step).wait_send()
        return 0

    lax.fori_loop(1, PEERS, drain, 0)
    handed(0).wait_send()
    new_copy.wait()
    for i in range(PAIRS):
        out_copy(i).wait()


def per_device(*args):
    strip = jax.ShapeDtypeStruct(args[0].shape, BF16)
    hbm = pl.BlockSpec(memory_space=pltpu.HBM)
    smem = pl.BlockSpec(memory_space=pltpu.SMEM)
    vmem = pl.BlockSpec(memory_space=pltpu.VMEM)
    dma = pltpu.SemaphoreType.DMA
    return pl.pallas_call(
        kernel,
        out_shape=(strip, strip),
        in_specs=[hbm, hbm, hbm, smem, smem, hbm, vmem, smem, smem, smem],
        out_specs=(hbm, hbm),
        scratch_shapes=[
            pltpu.VMEM((ROWS, WIDTH), BF16),
            pltpu.VMEM((ROWS, WIDTH), BF16),
            pltpu.VMEM((ROWS, WIDTH), BF16),
            pltpu.VMEM((PEERS, WIDTH), F32),
            pltpu.VMEM((TILES, PAIR, COLT), BF16),
            pltpu.VMEM((PEERS * SLOTS, PAIR, COLT), BF16),
            pltpu.VMEM((PEERS * SLOTS, PAIR, COLT), BF16),
            pltpu.VMEM((PEERS * SLOTS, PAIR, COLT), BF16),
            pltpu.VMEM((2 * WIDTH, WIDTH), BF16),
            pltpu.VMEM((ROWS, 2 * WIDTH), BF16),
            pltpu.VMEM((BLOCKS * ROWS, COLT), F32),
            pltpu.VMEM((TILES, TR, COLT), F32),
            pltpu.VMEM((PEERS * BACK, COLT), BF16),
            pltpu.VMEM((PEERS * BACK, COLT), BF16),
            pltpu.VMEM((PEERS * SLOTS, TR, COLT), F32),
            pltpu.VMEM((2, 8, COLT), jnp.int32),
            pltpu.SMEM((2, 8, COLT), jnp.int32),
            dma((3, PAIRS)),
            dma,
            dma,
            dma((PAIRS,)),
            dma,
            dma,
            dma((PEERS,)),
            dma((PEERS,)),
            dma((PEERS,)),
            dma((PEERS,)),
            dma((2,)),
            dma((2,)),
            dma((PEERS,)),
            dma((PEERS,)),
            dma,
        ],
        compiler_params=pltpu.CompilerParams(
            collective_id=0, has_side_effects=True, vmem_limit_bytes=58 << 20
        ),
    )(*args)


def solution(mesh):
    return jax.shard_map(
        per_device,
        mesh=mesh,
        in_specs=(
            P("chan", "row", None),
            P("chan", "row", None),
            P("chan", "row", None),
            P("chan"),
            P(),
            P(),
            P("chan", None),
            P("chan", None, None),
            P("chan", None),
            P("chan", None),
        ),
        out_specs=(P("chan", "row", None), P("chan", "row", None)),
        check_vma=False,
    )
```

```python
import functools

import jax
import jax.numpy as jnp
from jax import lax
from jax.experimental import pallas as pl
from jax.experimental.pallas import tpu as pltpu
from jax.sharding import PartitionSpec as P

TR = 40
COLT = 128
SLOTS = 3
STEP_SIZE = 0.5
PEERS = 64
MULT = 37
MESH = pl.DeviceIdType.MESH
F32 = jnp.float32
BF16 = jnp.bfloat16

ROWS = 640
WIDTH = 1280
BLOCKS = WIDTH // COLT
PAIRS = ROWS // (2 * TR)
TILES = (ROWS // TR) * BLOCKS
PAIR = 2 * TR
BACK = 128


def spin(me, step, sign):
    off = lax.rem(step * MULT, PEERS)
    x = lax.rem(lax.rem(me, 4) + 4 + sign * lax.rem(off, 4), 4)
    y = lax.rem(lax.rem(lax.div(me, 4), 4) + 4 + sign * lax.rem(lax.div(off, 4), 4), 4)
    z = lax.rem(lax.div(me, 16) + 4 + sign * lax.div(off, 16), 4)
    return (z * 4 + y) * 4 + x


def rows_at(start, size, unit):
    return pl.ds(pl.multiple_of(start, unit), size)


def kernel(
    gen, mag, ham, slot_ref, dims_in, pp_in, cc_in, send_in, recv_in, weight_in,
    flow_out,
    dims_ref, pp_v, cc_ref, send_ref, recv_ref, weight_ref, small_sem,
    gen_v, mag_v, ham_v, stack, sbuf, near, far, right, left, base, cross, tsend, trecv, unpacked,
    inv_v, inv_s,
    in_sem, inv_sem, out_sem, self_sem, send_sem, recv_sem, hand_sem, take_sem,
    strip_send, strip_recv, bsend_sem, brecv_sem, bself_sem,
):
    me = lax.axis_index("chan")
    row = lax.axis_index("row")
    other = 1 - row

    def load(i, start):
        for n, (src, dst) in enumerate(((gen, gen_v), (mag, mag_v), (ham, ham_v))):
            at = rows_at(i * PAIR, PAIR, 16)
            copy = pltpu.make_async_copy(src.at[0, at], dst.at[at], in_sem.at[n, i])
            copy.start() if start else copy.wait()

    for i in range(PAIRS):
        load(i, True)
    small = [
        pltpu.make_async_copy(src, dst, small_sem.at[n])
        for n, (src, dst) in enumerate(
            (
                (dims_in, dims_ref),
                (send_in, send_ref),
                (recv_in, recv_ref),
                (weight_in, weight_ref),
                (cc_in, cc_ref),
                (pp_in, pp_v),
            )
        )
    ]
    for copy in small:
        copy.start()
    barrier = pltpu.get_barrier_semaphore()

    def greet(step, _):
        pl.semaphore_signal(
            barrier, inc=1, device_id={"chan": spin(me, step, 1)}, device_id_type=MESH
        )
        return 0

    lax.fori_loop(1, PEERS, greet, 0)
    pl.semaphore_signal(barrier, inc=1, device_id={"row": other}, device_id_type=MESH)

    for copy in small[:2]:
        copy.wait()
    limit = dims_ref[slot_ref[0]]

    def live(i, k):
        row_ids = row * ROWS + i * PAIR + lax.broadcasted_iota(jnp.int32, (PAIR, COLT), 0)
        col_ids = k * COLT + lax.broadcasted_iota(jnp.int32, (1, COLT), 1)
        return row_ids < jnp.where(col_ids < limit, limit, 0)

    def prologue(i, _):
        load(i, False)
        at = rows_at(i * PAIR, PAIR, 16)
        for k in range(BLOCKS):
            col = pl.ds(k * COLT, COLT)
            new = (mag_v[at, col].astype(F32) + STEP_SIZE * gen_v[at, col].astype(F32)).astype(BF16)
            mag_v[at, col] = new
            mask = live(i, k)
            m = jnp.where(mask, new.astype(F32), 0.0)
            h = jnp.where(mask, ham_v[at, col].astype(F32), 0.0)
            for half in range(2):
                cut = slice(half * TR, (half + 1) * TR)
                tile = (2 * i + half) * BLOCKS + k
                stack[tile] = jnp.concatenate([m[cut], h[cut]], axis=0).astype(BF16)
        return 0

    lax.fori_loop(0, PAIRS, prologue, 0)
    pl.semaphore_wait(barrier, PEERS)

    def pick(to):
        for l in range(SLOTS):
            tile = jnp.minimum(send_ref[l, 0, to], TILES - 1)
            sbuf[to * SLOTS + l] = stack[tile]

    def message(step):
        to = spin(me, step, 1)
        return pltpu.make_async_remote_copy(
            sbuf.at[pl.ds(to * SLOTS, SLOTS)],
            near.at[pl.ds(me * SLOTS, SLOTS)],
            send_sem,
            recv_sem.at[step],
            device_id={"chan": to},
            device_id_type=MESH,
        )

    def arrival(step):
        fr = spin(me, step, -1)
        return pltpu.make_async_remote_copy(
            sbuf.at[pl.ds(fr * SLOTS, SLOTS)],
            near.at[pl.ds(fr * SLOTS, SLOTS)],
            send_sem,
            recv_sem.at[step],
            device_id={"chan": fr},
            device_id_type=MESH,
        )

    def handed(step):
        at = pl.ds(spin(me, step, -1) * SLOTS, SLOTS)
        return pltpu.make_async_remote_copy(
            near.at[at], far.at[at], hand_sem, take_sem,
            device_id={"row": other}, device_id_type=MESH,
        )

    def send_out(step, _):
        pick(spin(me, step, 1))
        message(step).start()
        return 0

    lax.fori_loop(1, PEERS, send_out, 0)
    pick(me)
    mine = pltpu.make_async_copy(
        sbuf.at[pl.ds(me * SLOTS, SLOTS)], near.at[pl.ds(me * SLOTS, SLOTS)], self_sem
    )
    mine.start()

    for copy in small[2:]:
        copy.wait()
    chosen = lax.broadcasted_iota(jnp.int32, pp_v.shape, 0) == slot_ref[0]
    factor = jnp.sum(jnp.where(chosen, pp_v[...], 0.0), axis=0, keepdims=True)

    def strips(i, _):
        at = rows_at(i * PAIR, PAIR, 16)
        for k in range(BLOCKS):
            col = pl.ds(k * COLT, COLT)
            mask = live(i, k)
            m = jnp.where(mask, mag_v[at, col].astype(F32), 0.0)
            h = jnp.where(mask, ham_v[at, col].astype(F32), 0.0)
            f = factor[:, k * COLT : (k + 1) * COLT]
            right[rows_at(row * ROWS + i * PAIR, PAIR, 16), col] = h.astype(BF16)
            right[rows_at(WIDTH + row * ROWS + i * PAIR, PAIR, 16), col] = m.astype(BF16)
            left[at, col] = (m * f).astype(BF16)
            left[at, pl.ds(WIDTH + k * COLT, COLT)] = (h * -f).astype(BF16)
            base[rows_at(k * ROWS + i * PAIR, PAIR, 8), :] = h
        return 0

    lax.fori_loop(0, PAIRS, strips, 0)

    def strip(which, r):
        at = rows_at(which * WIDTH + r * ROWS, ROWS, 16)
        return pltpu.make_async_remote_copy(
            right.at[at], right.at[at], strip_send.at[which], strip_recv.at[which],
            device_id={"row": other}, device_id_type=MESH,
        )

    for which in range(2):
        strip(which, row).start()
    mine.wait()
    handed(0).start()

    place = lax.broadcasted_iota(jnp.int32, (8, COLT), 0) * COLT + lax.broadcasted_iota(
        jnp.int32, (8, COLT), 1
    )

    def invert_recv(v, table):
        return jnp.where(place == recv_ref[0, v], v, table)

    def invert_send(d, table):
        for l in range(SLOTS):
            table = jnp.where(place == send_ref[l, 0, d], d * SLOTS + l, table)
        return table

    blank = jnp.zeros((8, COLT), jnp.int32)
    inv_v[0] = lax.fori_loop(0, TILES, invert_recv, blank)
    inv_v[1] = lax.fori_loop(0, PEERS, invert_send, blank)
    inv_copy = pltpu.make_async_copy(inv_v, inv_s, inv_sem)
    inv_copy.start()

    for which in range(2):
        strip(which, other).wait_recv()
        strip(which, row).wait_send()

    part = jnp.dot(left[...], right[...], preferred_element_type=F32)
    for k in range(BLOCKS):
        base[pl.ds(k * ROWS, ROWS), :] += part[:, k * COLT : (k + 1) * COLT]
    inv_copy.wait()

    def hand_on(step, _):
        arrival(step).wait_recv()
        handed(step).start()
        return 0

    lax.fori_loop(1, PEERS, hand_on, 0)

    def settle(tiles, r, own):
        def body(i, _):
            at = rows_at(r * ROWS + i * PAIR, PAIR, 16)
            under = rows_at(WIDTH + r * ROWS + i * PAIR, PAIR, 16)
            for k in range(BLOCKS):
                col = pl.ds(k * COLT, COLT)
                parts = []
                for half in range(2):
                    v = (2 * i + half) * BLOCKS + k
                    tile = tiles[recv_ref[0, v]]
                    parts.append(weight_ref[0, v] * tile.astype(F32))
                m = jnp.concatenate([parts[0][:TR], parts[1][:TR]], axis=0)
                h = jnp.concatenate([parts[0][TR:], parts[1][TR:]], axis=0)
                right[at, col] = h.astype(BF16)
                right[under, col] = m.astype(BF16)
                if own:
                    f = cc_ref[:, k * COLT : (k + 1) * COLT]
                    here = rows_at(i * PAIR, PAIR, 16)
                    left[here, col] = (m * f).astype(BF16)
                    left[here, pl.ds(WIDTH + k * COLT, COLT)] = (h * -f).astype(BF16)
            return 0

        lax.fori_loop(0, PAIRS, body, 0)

    settle(near, row, True)

    all_handed = pltpu.make_async_remote_copy(
        near, far, hand_sem, take_sem, device_id={"row": other}, device_id_type=MESH
    )
    all_handed.wait_recv()
    settle(far, other, False)

    part = jnp.dot(left[...], right[...], preferred_element_type=F32)
    for a in range(ROWS // TR):
        for k in range(BLOCKS):
            cross[a * BLOCKS + k] = part[a * TR : (a + 1) * TR, k * COLT : (k + 1) * COLT]

    def pick_back(to):
        parts = []
        for l in range(SLOTS):
            slot = to * SLOTS + l
            v = inv_s[0, lax.div(slot, COLT), lax.rem(slot, COLT)]
            parts.append(weight_ref[0, v] * cross[v])
        parts.append(jnp.zeros((BACK - SLOTS * TR, COLT), F32))
        tsend[rows_at(to * BACK, BACK, 16), :] = jnp.concatenate(parts, axis=0).astype(BF16)

    def back(step):
        to = spin(me, step, 1)
        return pltpu.make_async_remote_copy(
            tsend.at[rows_at(to * BACK, BACK, 16)],
            trecv.at[rows_at(me * BACK, BACK, 16)],
            bsend_sem,
            brecv_sem.at[step],
            device_id={"chan": to},
            device_id_type=MESH,
        )

    def back_arrival(step):
        fr = spin(me, step, -1)
        return pltpu.make_async_remote_copy(
            tsend.at[rows_at(fr * BACK, BACK, 16)],
            trecv.at[rows_at(fr * BACK, BACK, 16)],
            bsend_sem,
            brecv_sem.at[step],
            device_id={"chan": fr},
            device_id_type=MESH,
        )

    def send_back(step, _):
        pick_back(spin(me, step, 1))
        back(step).start()
        return 0

    lax.fori_loop(1, PEERS, send_back, 0)
    pick_back(me)
    home = pltpu.make_async_copy(
        tsend.at[rows_at(me * BACK, BACK, 16)], trecv.at[rows_at(me * BACK, BACK, 16)], bself_sem
    )
    home.start()

    def unpack(fr):
        rows = trecv[rows_at(fr * BACK, BACK, 16), :].astype(F32)
        for l in range(SLOTS):
            unpacked[fr * SLOTS + l] = rows[l * TR : (l + 1) * TR]

    home.wait()
    unpack(me)

    def take_back(step, _):
        back_arrival(step).wait_recv()
        unpack(spin(me, step, -1))
        return 0

    lax.fori_loop(1, PEERS, take_back, 0)

    def out_copy(i):
        at = rows_at(i * PAIR, PAIR, 16)
        return pltpu.make_async_copy(gen_v.at[at], flow_out.at[0, at], out_sem.at[i])

    def finish(i, _):
        at = rows_at(i * PAIR, PAIR, 16)
        for k in range(BLOCKS):
            parts = []
            for half in range(2):
                u = (2 * i + half) * BLOCKS + k
                slot = inv_s[1, lax.div(u, COLT), lax.rem(u, COLT)]
                parts.append(unpacked[slot])
            back_part = jnp.where(live(i, k), jnp.concatenate(parts, axis=0), 0.0)
            total = base[rows_at(k * ROWS + i * PAIR, PAIR, 8), :] + back_part
            gen_v[at, pl.ds(k * COLT, COLT)] = total.astype(BF16)
        out_copy(i).start()
        return 0

    lax.fori_loop(0, PAIRS, finish, 0)

    out_total = pl.ds(0, (PEERS - 1) * SLOTS)
    pltpu.make_async_remote_copy(
        sbuf.at[out_total], near.at[out_total], send_sem, recv_sem.at[0],
        device_id={"row": other}, device_id_type=MESH,
    ).wait_send()
    all_handed.wait_send()
    back_total = pl.ds(0, (PEERS - 1) * BACK)
    pltpu.make_async_remote_copy(
        tsend.at[back_total], trecv.at[back_total], bsend_sem, brecv_sem.at[0],
        device_id={"row": other}, device_id_type=MESH,
    ).wait_send()
    for i in range(PAIRS):
        out_copy(i).wait()


def per_device(gen, mag, ham, slot, dims, pp, cc, send, recv, weight):
    strip = jax.ShapeDtypeStruct(gen.shape, BF16)
    magnus_new = (mag.astype(F32) + STEP_SIZE * gen.astype(F32)).astype(BF16)
    args = (gen, mag, ham, slot, dims, pp, cc, send.transpose(2, 0, 1), recv, weight)
    hbm = pl.BlockSpec(memory_space=pltpu.HBM)
    dma = pltpu.SemaphoreType.DMA
    flowed = pl.pallas_call(
        kernel,
        out_shape=strip,
        in_specs=[hbm] * 3 + [pl.BlockSpec(memory_space=pltpu.SMEM)] + [hbm] * 6,
        out_specs=hbm,
        scratch_shapes=[
            pltpu.SMEM(dims.shape, jnp.int32),
            pltpu.VMEM(pp.shape, F32),
            pltpu.VMEM(cc.shape, F32),
            pltpu.SMEM(args[7].shape, jnp.int32),
            pltpu.SMEM(recv.shape, jnp.int32),
            pltpu.SMEM(weight.shape, F32),
            dma((6,)),
            pltpu.VMEM((ROWS, WIDTH), BF16),
            pltpu.VMEM((ROWS, WIDTH), BF16),
            pltpu.VMEM((ROWS, WIDTH), BF16),
            pltpu.VMEM((TILES, PAIR, COLT), BF16),
            pltpu.VMEM((PEERS * SLOTS, PAIR, COLT), BF16),
            pltpu.VMEM((PEERS * SLOTS, PAIR, COLT), BF16),
            pltpu.VMEM((PEERS * SLOTS, PAIR, COLT), BF16),
            pltpu.VMEM((2 * WIDTH, WIDTH), BF16),
            pltpu.VMEM((ROWS, 2 * WIDTH), BF16),
            pltpu.VMEM((BLOCKS * ROWS, COLT), F32),
            pltpu.VMEM((TILES, TR, COLT), F32),
            pltpu.VMEM((PEERS * BACK, COLT), BF16),
            pltpu.VMEM((PEERS * BACK, COLT), BF16),
            pltpu.VMEM((PEERS * SLOTS, TR, COLT), F32),
            pltpu.VMEM((2, 8, COLT), jnp.int32),
            pltpu.SMEM((2, 8, COLT), jnp.int32),
            dma((3, PAIRS)),
            dma,
            dma((PAIRS,)),
            dma,
            dma,
            dma((PEERS,)),
            dma,
            dma,
            dma((2,)),
            dma((2,)),
            dma,
            dma((PEERS,)),
            dma,
        ],
        compiler_params=pltpu.CompilerParams(
            collective_id=0, has_side_effects=True, vmem_limit_bytes=58 << 20
        ),
    )(*args)
    return magnus_new, flowed


def solution(mesh):
    return jax.shard_map(
        per_device,
        mesh=mesh,
        in_specs=(
            P("chan", "row", None),
            P("chan", "row", None),
            P("chan", "row", None),
            P("chan"),
            P(),
            P(),
            P("chan", None),
            P("chan", None, None),
            P("chan", None),
            P("chan", None),
        ),
        out_specs=(P("chan", "row", None), P("chan", "row", None)),
        check_vma=False,
    )
```

```python
import functools

import jax
import jax.numpy as jnp
from jax import lax
from jax.experimental import pallas as pl
from jax.experimental.pallas import tpu as pltpu
from jax.sharding import PartitionSpec as P

TR = 40
COLT = 128
SLOTS = 3
STEP_SIZE = 0.5
PEERS = 64
MULT = 37
MESH = pl.DeviceIdType.MESH
F32 = jnp.float32
BF16 = jnp.bfloat16

ROWS = 640
WIDTH = 1280
BLOCKS = WIDTH // COLT
PAIRS = ROWS // (2 * TR)
TILES = (ROWS // TR) * BLOCKS
PAIR = 2 * TR


def spin(me, step, sign):
    off = lax.rem(step * MULT, PEERS)
    x = lax.rem(lax.rem(me, 4) + 4 + sign * lax.rem(off, 4), 4)
    y = lax.rem(lax.rem(lax.div(me, 4), 4) + 4 + sign * lax.rem(lax.div(off, 4), 4), 4)
    z = lax.rem(lax.div(me, 16) + 4 + sign * lax.div(off, 16), 4)
    return (z * 4 + y) * 4 + x


def rows_at(start, size, unit):
    return pl.ds(pl.multiple_of(start, unit), size)


def kernel(
    gen, mag, ham, slot_ref, dims_in, pp_in, cc_in, send_in, recv_in, weight_in,
    flow_out,
    dims_ref, pp_v, cc_ref, send_ref, recv_ref, weight_ref, small_sem,
    gen_v, mag_v, ham_v, stack, sbuf, near, far, right, left, base, cross, tsend, trecv,
    inv_v, inv_s,
    in_sem, inv_sem, out_sem, self_sem, send_sem, recv_sem, hand_sem, take_sem,
    strip_send, strip_recv, bsend_sem, brecv_sem, bself_sem,
):
    me = lax.axis_index("chan")
    row = lax.axis_index("row")
    other = 1 - row

    def load(i, start):
        for n, (src, dst) in enumerate(((gen, gen_v), (mag, mag_v), (ham, ham_v))):
            at = rows_at(i * PAIR, PAIR, 16)
            copy = pltpu.make_async_copy(src.at[0, at], dst.at[at], in_sem.at[n, i])
            copy.start() if start else copy.wait()

    for i in range(PAIRS):
        load(i, True)
    small = [
        pltpu.make_async_copy(src, dst, small_sem.at[n])
        for n, (src, dst) in enumerate(
            (
                (dims_in, dims_ref),
                (send_in, send_ref),
                (recv_in, recv_ref),
                (weight_in, weight_ref),
                (cc_in, cc_ref),
                (pp_in, pp_v),
            )
        )
    ]
    for copy in small:
        copy.start()
    barrier = pltpu.get_barrier_semaphore()

    def greet(step, _):
        pl.semaphore_signal(
            barrier, inc=1, device_id={"chan": lax.rem(me + step, PEERS)}, device_id_type=MESH
        )
        return 0

    lax.fori_loop(1, PEERS, greet, 0)
    pl.semaphore_signal(barrier, inc=1, device_id={"row": other}, device_id_type=MESH)

    for copy in small[:2]:
        copy.wait()
    limit = dims_ref[slot_ref[0]]

    def live(i, k):
        row_ids = row * ROWS + i * PAIR + lax.broadcasted_iota(jnp.int32, (PAIR, COLT), 0)
        col_ids = k * COLT + lax.broadcasted_iota(jnp.int32, (1, COLT), 1)
        return row_ids < jnp.where(col_ids < limit, limit, 0)

    def prologue(i, _):
        load(i, False)
        at = rows_at(i * PAIR, PAIR, 16)
        for k in range(BLOCKS):
            col = pl.ds(k * COLT, COLT)
            new = (mag_v[at, col].astype(F32) + STEP_SIZE * gen_v[at, col].astype(F32)).astype(BF16)
            mag_v[at, col] = new
            mask = live(i, k)
            m = jnp.where(mask, new.astype(F32), 0.0)
            h = jnp.where(mask, ham_v[at, col].astype(F32), 0.0)
            for half in range(2):
                cut = slice(half * TR, (half + 1) * TR)
                tile = (2 * i + half) * BLOCKS + k
                stack[tile] = jnp.concatenate([m[cut], h[cut]], axis=0).astype(BF16)
        return 0

    lax.fori_loop(0, PAIRS, prologue, 0)
    pl.semaphore_wait(barrier, PEERS)

    def pick(to):
        for l in range(SLOTS):
            tile = jnp.minimum(send_ref[l, 0, to], TILES - 1)
            sbuf[to * SLOTS + l] = stack[tile]

    def message(step):
        to = spin(me, step, 1)
        return pltpu.make_async_remote_copy(
            sbuf.at[pl.ds(to * SLOTS, SLOTS)],
            near.at[pl.ds(me * SLOTS, SLOTS)],
            send_sem,
            recv_sem.at[step],
            device_id={"chan": to},
            device_id_type=MESH,
        )

    def arrival(step):
        fr = spin(me, step, -1)
        return pltpu.make_async_remote_copy(
            sbuf.at[pl.ds(fr * SLOTS, SLOTS)],
            near.at[pl.ds(fr * SLOTS, SLOTS)],
            send_sem,
            recv_sem.at[step],
            device_id={"chan": fr},
            device_id_type=MESH,
        )

    def handed(step):
        at = pl.ds(spin(me, step, -1) * SLOTS, SLOTS)
        return pltpu.make_async_remote_copy(
            near.at[at], far.at[at], hand_sem, take_sem,
            device_id={"row": other}, device_id_type=MESH,
        )

    def send_out(step, _):
        pick(spin(me, step, 1))
        message(step).start()
        return 0

    lax.fori_loop(1, PEERS, send_out, 0)
    pick(me)
    mine = pltpu.make_async_copy(
        sbuf.at[pl.ds(me * SLOTS, SLOTS)], near.at[pl.ds(me * SLOTS, SLOTS)], self_sem
    )
    mine.start()

    for copy in small[2:]:
        copy.wait()
    chosen = lax.broadcasted_iota(jnp.int32, pp_v.shape, 0) == slot_ref[0]
    factor = jnp.sum(jnp.where(chosen, pp_v[...], 0.0), axis=0, keepdims=True)

    def strips(i, _):
        at = rows_at(i * PAIR, PAIR, 16)
        for k in range(BLOCKS):
            col = pl.ds(k * COLT, COLT)
            mask = live(i, k)
            m = jnp.where(mask, mag_v[at, col].astype(F32), 0.0)
            h = jnp.where(mask, ham_v[at, col].astype(F32), 0.0)
            f = factor[:, k * COLT : (k + 1) * COLT]
            right[rows_at(row * ROWS + i * PAIR, PAIR, 16), col] = h.astype(BF16)
            right[rows_at(WIDTH + row * ROWS + i * PAIR, PAIR, 16), col] = m.astype(BF16)
            left[at, col] = (m * f).astype(BF16)
            left[at, pl.ds(WIDTH + k * COLT, COLT)] = (h * -f).astype(BF16)
            base[rows_at(k * ROWS + i * PAIR, PAIR, 8), :] = h
        return 0

    lax.fori_loop(0, PAIRS, strips, 0)

    def strip(which, r):
        at = rows_at(which * WIDTH + r * ROWS, ROWS, 16)
        return pltpu.make_async_remote_copy(
            right.at[at], right.at[at], strip_send.at[which], strip_recv.at[which],
            device_id={"row": other}, device_id_type=MESH,
        )

    for which in range(2):
        strip(which, row).start()
    mine.wait()
    handed(0).start()

    place = lax.broadcasted_iota(jnp.int32, (8, COLT), 0) * COLT + lax.broadcasted_iota(
        jnp.int32, (8, COLT), 1
    )

    def invert_recv(v, table):
        return jnp.where(place == recv_ref[0, v], v, table)

    def invert_send(d, table):
        for l in range(SLOTS):
            table = jnp.where(place == send_ref[l, 0, d], d * SLOTS + l, table)
        return table

    blank = jnp.zeros((8, COLT), jnp.int32)
    inv_v[0] = lax.fori_loop(0, TILES, invert_recv, blank)
    inv_v[1] = lax.fori_loop(0, PEERS, invert_send, blank)
    inv_copy = pltpu.make_async_copy(inv_v, inv_s, inv_sem)
    inv_copy.start()

    for which in range(2):
        strip(which, other).wait_recv()
        strip(which, row).wait_send()

    part = jnp.dot(left[...], right[...], preferred_element_type=F32)
    for k in range(BLOCKS):
        base[pl.ds(k * ROWS, ROWS), :] += part[:, k * COLT : (k + 1) * COLT]
    inv_copy.wait()

    def hand_on(step, _):
        arrival(step).wait_recv()
        handed(step).start()
        return 0

    lax.fori_loop(1, PEERS, hand_on, 0)

    def settle(tiles, r, own):
        def body(i, _):
            at = rows_at(r * ROWS + i * PAIR, PAIR, 16)
            under = rows_at(WIDTH + r * ROWS + i * PAIR, PAIR, 16)
            for k in range(BLOCKS):
                col = pl.ds(k * COLT, COLT)
                parts = []
                for half in range(2):
                    v = (2 * i + half) * BLOCKS + k
                    tile = tiles[recv_ref[0, v]]
                    parts.append(weight_ref[0, v] * tile.astype(F32))
                m = jnp.concatenate([parts[0][:TR], parts[1][:TR]], axis=0)
                h = jnp.concatenate([parts[0][TR:], parts[1][TR:]], axis=0)
                right[at, col] = h.astype(BF16)
                right[under, col] = m.astype(BF16)
                if own:
                    f = cc_ref[:, k * COLT : (k + 1) * COLT]
                    here = rows_at(i * PAIR, PAIR, 16)
                    left[here, col] = (m * f).astype(BF16)
                    left[here, pl.ds(WIDTH + k * COLT, COLT)] = (h * -f).astype(BF16)
            return 0

        lax.fori_loop(0, PAIRS, body, 0)

    settle(near, row, True)

    all_handed = pltpu.make_async_remote_copy(
        near, far, hand_sem, take_sem, device_id={"row": other}, device_id_type=MESH
    )
    all_handed.wait_recv()
    settle(far, other, False)

    part = jnp.dot(left[...], right[...], preferred_element_type=F32)
    for a in range(ROWS // TR):
        for k in range(BLOCKS):
            cross[a * BLOCKS + k] = part[a * TR : (a + 1) * TR, k * COLT : (k + 1) * COLT]

    def pick_back(to):
        for l in range(SLOTS):
            slot = to * SLOTS + l
            v = inv_s[0, lax.div(slot, COLT), lax.rem(slot, COLT)]
            tsend[slot] = (weight_ref[0, v] * cross[v]).astype(BF16)

    def back(step):
        to = spin(me, step, 1)
        return pltpu.make_async_remote_copy(
            tsend.at[pl.ds(to * SLOTS, SLOTS)],
            trecv.at[pl.ds(me * SLOTS, SLOTS)],
            bsend_sem,
            brecv_sem.at[step],
            device_id={"chan": to},
            device_id_type=MESH,
        )

    def back_arrival(step):
        fr = spin(me, step, -1)
        return pltpu.make_async_remote_copy(
            tsend.at[pl.ds(fr * SLOTS, SLOTS)],
            trecv.at[pl.ds(fr * SLOTS, SLOTS)],
            bsend_sem,
            brecv_sem.at[step],
            device_id={"chan": fr},
            device_id_type=MESH,
        )

    def send_back(step, _):
        pick_back(spin(me, step, 1))
        back(step).start()
        return 0

    lax.fori_loop(1, PEERS, send_back, 0)
    pick_back(me)
    home = pltpu.make_async_copy(
        tsend.at[pl.ds(me * SLOTS, SLOTS)], trecv.at[pl.ds(me * SLOTS, SLOTS)], bself_sem
    )
    home.start()

    home.wait()

    def take_back(step, _):
        back_arrival(step).wait_recv()
        return 0

    lax.fori_loop(1, PEERS, take_back, 0)

    def out_copy(i):
        at = rows_at(i * PAIR, PAIR, 16)
        return pltpu.make_async_copy(gen_v.at[at], flow_out.at[0, at], out_sem.at[i])

    def finish(i, _):
        at = rows_at(i * PAIR, PAIR, 16)
        for k in range(BLOCKS):
            parts = []
            for half in range(2):
                u = (2 * i + half) * BLOCKS + k
                slot = inv_s[1, lax.div(u, COLT), lax.rem(u, COLT)]
                parts.append(trecv[slot].astype(F32))
            back_part = jnp.where(live(i, k), jnp.concatenate(parts, axis=0), 0.0)
            total = base[rows_at(k * ROWS + i * PAIR, PAIR, 8), :] + back_part
            gen_v[at, pl.ds(k * COLT, COLT)] = total.astype(BF16)
        out_copy(i).start()
        return 0

    lax.fori_loop(0, PAIRS, finish, 0)

    out_total = pl.ds(0, (PEERS - 1) * SLOTS)
    pltpu.make_async_remote_copy(
        sbuf.at[out_total], near.at[out_total], send_sem, recv_sem.at[0],
        device_id={"row": other}, device_id_type=MESH,
    ).wait_send()
    all_handed.wait_send()
    back_total = out_total
    pltpu.make_async_remote_copy(
        tsend.at[back_total], trecv.at[back_total], bsend_sem, brecv_sem.at[0],
        device_id={"row": other}, device_id_type=MESH,
    ).wait_send()
    for i in range(PAIRS):
        out_copy(i).wait()


def per_device(gen, mag, ham, slot, dims, pp, cc, send, recv, weight):
    strip = jax.ShapeDtypeStruct(gen.shape, BF16)
    magnus_new = (mag.astype(F32) + STEP_SIZE * gen.astype(F32)).astype(BF16)
    args = (gen, mag, ham, slot, dims, pp, cc, send.transpose(2, 0, 1), recv, weight)
    hbm = pl.BlockSpec(memory_space=pltpu.HBM)
    dma = pltpu.SemaphoreType.DMA
    flowed = pl.pallas_call(
        kernel,
        out_shape=strip,
        in_specs=[hbm] * 3 + [pl.BlockSpec(memory_space=pltpu.SMEM)] + [hbm] * 6,
        out_specs=hbm,
        scratch_shapes=[
            pltpu.SMEM(dims.shape, jnp.int32),
            pltpu.VMEM(pp.shape, F32),
            pltpu.VMEM(cc.shape, F32),
            pltpu.SMEM(args[7].shape, jnp.int32),
            pltpu.SMEM(recv.shape, jnp.int32),
            pltpu.SMEM(weight.shape, F32),
            dma((6,)),
            pltpu.VMEM((ROWS, WIDTH), BF16),
            pltpu.VMEM((ROWS, WIDTH), BF16),
            pltpu.VMEM((ROWS, WIDTH), BF16),
            pltpu.VMEM((TILES, PAIR, COLT), BF16),
            pltpu.VMEM((PEERS * SLOTS, PAIR, COLT), BF16),
            pltpu.VMEM((PEERS * SLOTS, PAIR, COLT), BF16),
            pltpu.VMEM((PEERS * SLOTS, PAIR, COLT), BF16),
            pltpu.VMEM((2 * WIDTH, WIDTH), BF16),
            pltpu.VMEM((ROWS, 2 * WIDTH), BF16),
            pltpu.VMEM((BLOCKS * ROWS, COLT), F32),
            pltpu.VMEM((TILES, TR, COLT), F32),
            pltpu.VMEM((PEERS * SLOTS, TR, COLT), BF16),
            pltpu.VMEM((PEERS * SLOTS, TR, COLT), BF16),
            pltpu.VMEM((2, 8, COLT), jnp.int32),
            pltpu.SMEM((2, 8, COLT), jnp.int32),
            dma((3, PAIRS)),
            dma,
            dma((PAIRS,)),
            dma,
            dma,
            dma((PEERS,)),
            dma,
            dma,
            dma((2,)),
            dma((2,)),
            dma,
            dma((PEERS,)),
            dma,
        ],
        compiler_params=pltpu.CompilerParams(
            collective_id=0, has_side_effects=True, vmem_limit_bytes=58 << 20
        ),
    )(*args)
    return magnus_new, flowed


def solution(mesh):
    return jax.shard_map(
        per_device,
        mesh=mesh,
        in_specs=(
            P("chan", "row", None),
            P("chan", "row", None),
            P("chan", "row", None),
            P("chan"),
            P(),
            P(),
            P("chan", None),
            P("chan", None, None),
            P("chan", None),
            P("chan", None),
        ),
        out_specs=(P("chan", "row", None), P("chan", "row", None)),
        check_vma=False,
    )
```

```python
import functools

import jax
import jax.numpy as jnp
from jax import lax
from jax.experimental import pallas as pl
from jax.experimental.pallas import tpu as pltpu
from jax.sharding import PartitionSpec as P

TR = 40
COLT = 128
SLOTS = 3
STEP_SIZE = 0.5
PEERS = 64
MULT = 37
MESH = pl.DeviceIdType.MESH
F32 = jnp.float32
BF16 = jnp.bfloat16

ROWS = 640
WIDTH = 1280
BLOCKS = WIDTH // COLT
PAIRS = ROWS // (2 * TR)
TILES = (ROWS // TR) * BLOCKS
HEAD = 16
REST = TR - HEAD
PAIR = 2 * TR


def spin(me, step, sign):
    off = lax.rem(step * MULT, PEERS)
    x = lax.rem(lax.rem(me, 4) + 4 + sign * lax.rem(off, 4), 4)
    y = lax.rem(lax.rem(lax.div(me, 4), 4) + 4 + sign * lax.rem(lax.div(off, 4), 4), 4)
    z = lax.rem(lax.div(me, 16) + 4 + sign * lax.div(off, 16), 4)
    return (z * 4 + y) * 4 + x


def rows_at(start, size, unit):
    return pl.ds(pl.multiple_of(start, unit), size)


def kernel(
    gen, mag, ham, slot_ref, dims_in, pp_in, cc_in, send_in, recv_in, weight_in,
    flow_out,
    dims_ref, pp_v, cc_ref, send_ref, recv_ref, weight_ref, small_sem,
    gen_v, mag_v, ham_v, stack, sbuf, near, far, right, left, base, cross_a, cross_b, tsend_a, tsend_b, trecv_a, trecv_b,
    inv_v, inv_s,
    in_sem, inv_sem, out_sem, self_sem, send_sem, recv_sem, hand_sem, take_sem,
    strip_send, strip_recv, bsend_sem, brecv_sem, bself_sem,
):
    me = lax.axis_index("chan")
    row = lax.axis_index("row")
    other = 1 - row

    def load(i, start):
        for n, (src, dst) in enumerate(((gen, gen_v), (mag, mag_v), (ham, ham_v))):
            at = rows_at(i * PAIR, PAIR, 16)
            copy = pltpu.make_async_copy(src.at[0, at], dst.at[at], in_sem.at[n, i])
            copy.start() if start else copy.wait()

    for i in range(PAIRS):
        load(i, True)
    small = [
        pltpu.make_async_copy(src, dst, small_sem.at[n])
        for n, (src, dst) in enumerate(
            (
                (dims_in, dims_ref),
                (send_in, send_ref),
                (recv_in, recv_ref),
                (weight_in, weight_ref),
                (cc_in, cc_ref),
                (pp_in, pp_v),
            )
        )
    ]
    for copy in small:
        copy.start()
    barrier = pltpu.get_barrier_semaphore()

    def greet(step, _):
        pl.semaphore_signal(
            barrier, inc=1, device_id={"chan": lax.rem(me + step, PEERS)}, device_id_type=MESH
        )
        return 0

    lax.fori_loop(1, PEERS, greet, 0)
    pl.semaphore_signal(barrier, inc=1, device_id={"row": other}, device_id_type=MESH)

    for copy in small[:2]:
        copy.wait()
    limit = dims_ref[slot_ref[0]]

    def live(i, k):
        row_ids = row * ROWS + i * PAIR + lax.broadcasted_iota(jnp.int32, (PAIR, COLT), 0)
        col_ids = k * COLT + lax.broadcasted_iota(jnp.int32, (1, COLT), 1)
        return row_ids < jnp.where(col_ids < limit, limit, 0)

    def prologue(i, _):
        load(i, False)
        at = rows_at(i * PAIR, PAIR, 16)
        for k in range(BLOCKS):
            col = pl.ds(k * COLT, COLT)
            new = (mag_v[at, col].astype(F32) + STEP_SIZE * gen_v[at, col].astype(F32)).astype(BF16)
            mag_v[at, col] = new
            mask = live(i, k)
            m = jnp.where(mask, new.astype(F32), 0.0)
            h = jnp.where(mask, ham_v[at, col].astype(F32), 0.0)
            for half in range(2):
                cut = slice(half * TR, (half + 1) * TR)
                tile = (2 * i + half) * BLOCKS + k
                stack[tile] = jnp.concatenate([m[cut], h[cut]], axis=0).astype(BF16)
        return 0

    lax.fori_loop(0, PAIRS, prologue, 0)
    pl.semaphore_wait(barrier, PEERS)

    def pick(to):
        for l in range(SLOTS):
            tile = jnp.minimum(send_ref[l, 0, to], TILES - 1)
            sbuf[to * SLOTS + l] = stack[tile]

    def message(step):
        to = spin(me, step, 1)
        return pltpu.make_async_remote_copy(
            sbuf.at[pl.ds(to * SLOTS, SLOTS)],
            near.at[pl.ds(me * SLOTS, SLOTS)],
            send_sem,
            recv_sem.at[step],
            device_id={"chan": to},
            device_id_type=MESH,
        )

    def arrival(step):
        fr = spin(me, step, -1)
        return pltpu.make_async_remote_copy(
            sbuf.at[pl.ds(fr * SLOTS, SLOTS)],
            near.at[pl.ds(fr * SLOTS, SLOTS)],
            send_sem,
            recv_sem.at[step],
            device_id={"chan": fr},
            device_id_type=MESH,
        )

    def handed(step):
        at = pl.ds(spin(me, step, -1) * SLOTS, SLOTS)
        return pltpu.make_async_remote_copy(
            near.at[at], far.at[at], hand_sem, take_sem,
            device_id={"row": other}, device_id_type=MESH,
        )

    def send_out(step, _):
        pick(spin(me, step, 1))
        message(step).start()
        return 0

    lax.fori_loop(1, PEERS, send_out, 0)
    pick(me)
    mine = pltpu.make_async_copy(
        sbuf.at[pl.ds(me * SLOTS, SLOTS)], near.at[pl.ds(me * SLOTS, SLOTS)], self_sem
    )
    mine.start()

    for copy in small[2:]:
        copy.wait()
    chosen = lax.broadcasted_iota(jnp.int32, pp_v.shape, 0) == slot_ref[0]
    factor = jnp.sum(jnp.where(chosen, pp_v[...], 0.0), axis=0, keepdims=True)

    def strips(i, _):
        at = rows_at(i * PAIR, PAIR, 16)
        for k in range(BLOCKS):
            col = pl.ds(k * COLT, COLT)
            mask = live(i, k)
            m = jnp.where(mask, mag_v[at, col].astype(F32), 0.0)
            h = jnp.where(mask, ham_v[at, col].astype(F32), 0.0)
            f = factor[:, k * COLT : (k + 1) * COLT]
            right[rows_at(row * ROWS + i * PAIR, PAIR, 16), col] = h.astype(BF16)
            right[rows_at(WIDTH + row * ROWS + i * PAIR, PAIR, 16), col] = m.astype(BF16)
            left[at, col] = (m * f).astype(BF16)
            left[at, pl.ds(WIDTH + k * COLT, COLT)] = (h * -f).astype(BF16)
            base[rows_at(k * ROWS + i * PAIR, PAIR, 8), :] = h
        return 0

    lax.fori_loop(0, PAIRS, strips, 0)

    def strip(which, r):
        at = rows_at(which * WIDTH + r * ROWS, ROWS, 16)
        return pltpu.make_async_remote_copy(
            right.at[at], right.at[at], strip_send.at[which], strip_recv.at[which],
            device_id={"row": other}, device_id_type=MESH,
        )

    for which in range(2):
        strip(which, row).start()
    mine.wait()
    handed(0).start()

    place = lax.broadcasted_iota(jnp.int32, (8, COLT), 0) * COLT + lax.broadcasted_iota(
        jnp.int32, (8, COLT), 1
    )

    def invert_recv(v, table):
        return jnp.where(place == recv_ref[0, v], v, table)

    def invert_send(d, table):
        for l in range(SLOTS):
            table = jnp.where(place == send_ref[l, 0, d], d * SLOTS + l, table)
        return table

    blank = jnp.zeros((8, COLT), jnp.int32)
    inv_v[0] = lax.fori_loop(0, TILES, invert_recv, blank)
    inv_v[1] = lax.fori_loop(0, PEERS, invert_send, blank)
    inv_copy = pltpu.make_async_copy(inv_v, inv_s, inv_sem)
    inv_copy.start()

    for which in range(2):
        strip(which, other).wait_recv()
        strip(which, row).wait_send()

    part = jnp.dot(left[...], right[...], preferred_element_type=F32)
    for k in range(BLOCKS):
        base[pl.ds(k * ROWS, ROWS), :] += part[:, k * COLT : (k + 1) * COLT]
    inv_copy.wait()

    def hand_on(step, _):
        arrival(step).wait_recv()
        handed(step).start()
        return 0

    lax.fori_loop(1, PEERS, hand_on, 0)

    def settle(tiles, r, own):
        def body(i, _):
            at = rows_at(r * ROWS + i * PAIR, PAIR, 16)
            under = rows_at(WIDTH + r * ROWS + i * PAIR, PAIR, 16)
            for k in range(BLOCKS):
                col = pl.ds(k * COLT, COLT)
                parts = []
                for half in range(2):
                    v = (2 * i + half) * BLOCKS + k
                    tile = tiles[recv_ref[0, v]]
                    parts.append(weight_ref[0, v] * tile.astype(F32))
                m = jnp.concatenate([parts[0][:TR], parts[1][:TR]], axis=0)
                h = jnp.concatenate([parts[0][TR:], parts[1][TR:]], axis=0)
                right[at, col] = h.astype(BF16)
                right[under, col] = m.astype(BF16)
                if own:
                    f = cc_ref[:, k * COLT : (k + 1) * COLT]
                    first = rows_at(i * 2 * HEAD, 2 * HEAD, 16)
                    second = rows_at(ROWS // TR * HEAD + i * 2 * REST, 2 * REST, 16)
                    for value, place in ((m * f, k * COLT), (h * -f, WIDTH + k * COLT)):
                        side = pl.ds(place, COLT)
                        left[first, side] = jnp.concatenate(
                            [value[:HEAD], value[TR : TR + HEAD]], axis=0
                        ).astype(BF16)
                        left[second, side] = jnp.concatenate(
                            [value[HEAD:TR], value[TR + HEAD :]], axis=0
                        ).astype(BF16)
            return 0

        lax.fori_loop(0, PAIRS, body, 0)

    settle(near, row, True)

    all_handed = pltpu.make_async_remote_copy(
        near, far, hand_sem, take_sem, device_id={"row": other}, device_id_type=MESH
    )
    all_handed.wait_recv()
    settle(far, other, False)

    def product(start, size, cross):
        rows = left[start : start + size * (ROWS // TR), :]
        part = jnp.dot(rows, right[...], preferred_element_type=F32)
        for a in range(ROWS // TR):
            for k in range(BLOCKS):
                cross[a * BLOCKS + k] = part[a * size : (a + 1) * size, k * COLT : (k + 1) * COLT]

    def pick_back(to, cross, tsend):
        for l in range(SLOTS):
            slot = to * SLOTS + l
            v = inv_s[0, lax.div(slot, COLT), lax.rem(slot, COLT)]
            tsend[slot] = (weight_ref[0, v] * cross[v]).astype(BF16)

    mine_at = pl.ds(me * SLOTS, SLOTS)
    parts_back = ((0, HEAD, cross_a, tsend_a, trecv_a), (ROWS // TR * HEAD, REST, cross_b, tsend_b, trecv_b))
    homes = []
    for n, (start, size, cross, tsend, trecv) in enumerate(parts_back):
        product(start, size, cross)

        def send_back(step, _):
            to = spin(me, step, 1)
            pick_back(to, cross, tsend)
            pltpu.make_async_remote_copy(
                tsend.at[pl.ds(to * SLOTS, SLOTS)], trecv.at[mine_at], bsend_sem.at[n], brecv_sem.at[n],
                device_id={"chan": to}, device_id_type=MESH,
            ).start()
            return 0

        lax.fori_loop(1, PEERS, send_back, 0)
        pick_back(me, cross, tsend)
        homes.append(pltpu.make_async_copy(tsend.at[mine_at], trecv.at[mine_at], bself_sem.at[n]))
        homes[n].start()

    others = pl.ds(0, (PEERS - 1) * SLOTS)
    all_back = [
        pltpu.make_async_remote_copy(
            tsend.at[others], trecv.at[others], bsend_sem.at[n], brecv_sem.at[n],
            device_id={"row": other}, device_id_type=MESH,
        )
        for n, (_, _, _, tsend, trecv) in enumerate(parts_back)
    ]
    for n in range(2):
        homes[n].wait()
        all_back[n].wait_recv()

    def out_copy(i):
        at = rows_at(i * PAIR, PAIR, 16)
        return pltpu.make_async_copy(gen_v.at[at], flow_out.at[0, at], out_sem.at[i])

    def finish(i, _):
        at = rows_at(i * PAIR, PAIR, 16)
        for k in range(BLOCKS):
            parts = []
            for half in range(2):
                u = (2 * i + half) * BLOCKS + k
                slot = inv_s[1, lax.div(u, COLT), lax.rem(u, COLT)]
                parts += [trecv_a[slot].astype(F32), trecv_b[slot].astype(F32)]
            back_part = jnp.where(live(i, k), jnp.concatenate(parts, axis=0), 0.0)
            total = base[rows_at(k * ROWS + i * PAIR, PAIR, 8), :] + back_part
            gen_v[at, pl.ds(k * COLT, COLT)] = total.astype(BF16)
        out_copy(i).start()
        return 0

    lax.fori_loop(0, PAIRS, finish, 0)

    pltpu.make_async_remote_copy(
        sbuf.at[others], near.at[others], send_sem, recv_sem.at[0],
        device_id={"row": other}, device_id_type=MESH,
    ).wait_send()
    all_handed.wait_send()
    for n in range(2):
        all_back[n].wait_send()
    for i in range(PAIRS):
        out_copy(i).wait()


def per_device(gen, mag, ham, slot, dims, pp, cc, send, recv, weight):
    strip = jax.ShapeDtypeStruct(gen.shape, BF16)
    magnus_new = (mag.astype(F32) + STEP_SIZE * gen.astype(F32)).astype(BF16)
    args = (gen, mag, ham, slot, dims, pp, cc, send.transpose(2, 0, 1), recv, weight)
    hbm = pl.BlockSpec(memory_space=pltpu.HBM)
    dma = pltpu.SemaphoreType.DMA
    flowed = pl.pallas_call(
        kernel,
        out_shape=strip,
        in_specs=[hbm] * 3 + [pl.BlockSpec(memory_space=pltpu.SMEM)] + [hbm] * 6,
        out_specs=hbm,
        scratch_shapes=[
            pltpu.SMEM(dims.shape, jnp.int32),
            pltpu.VMEM(pp.shape, F32),
            pltpu.VMEM(cc.shape, F32),
            pltpu.SMEM(args[7].shape, jnp.int32),
            pltpu.SMEM(recv.shape, jnp.int32),
            pltpu.SMEM(weight.shape, F32),
            dma((6,)),
            pltpu.VMEM((ROWS, WIDTH), BF16),
            pltpu.VMEM((ROWS, WIDTH), BF16),
            pltpu.VMEM((ROWS, WIDTH), BF16),
            pltpu.VMEM((TILES, PAIR, COLT), BF16),
            pltpu.VMEM((PEERS * SLOTS, PAIR, COLT), BF16),
            pltpu.VMEM((PEERS * SLOTS, PAIR, COLT), BF16),
            pltpu.VMEM((PEERS * SLOTS, PAIR, COLT), BF16),
            pltpu.VMEM((2 * WIDTH, WIDTH), BF16),
            pltpu.VMEM((ROWS, 2 * WIDTH), BF16),
            pltpu.VMEM((BLOCKS * ROWS, COLT), F32),
            pltpu.VMEM((TILES, HEAD, COLT), F32),
            pltpu.VMEM((TILES, REST, COLT), F32),
            pltpu.VMEM((PEERS * SLOTS, HEAD, COLT), BF16),
            pltpu.VMEM((PEERS * SLOTS, REST, COLT), BF16),
            pltpu.VMEM((PEERS * SLOTS, HEAD, COLT), BF16),
            pltpu.VMEM((PEERS * SLOTS, REST, COLT), BF16),
            pltpu.VMEM((2, 8, COLT), jnp.int32),
            pltpu.SMEM((2, 8, COLT), jnp.int32),
            dma((3, PAIRS)),
            dma,
            dma((PAIRS,)),
            dma,
            dma,
            dma((PEERS,)),
            dma,
            dma,
            dma((2,)),
            dma((2,)),
            dma((2,)),
            dma((2,)),
            dma((2,)),
        ],
        compiler_params=pltpu.CompilerParams(
            collective_id=0, has_side_effects=True, vmem_limit_bytes=58 << 20
        ),
    )(*args)
    return magnus_new, flowed


def solution(mesh):
    return jax.shard_map(
        per_device,
        mesh=mesh,
        in_specs=(
            P("chan", "row", None),
            P("chan", "row", None),
            P("chan", "row", None),
            P("chan"),
            P(),
            P(),
            P("chan", None),
            P("chan", None, None),
            P("chan", None),
            P("chan", None),
        ),
        out_specs=(P("chan", "row", None), P("chan", "row", None)),
        check_vma=False,
    )
```

```python
import functools

import jax
import jax.numpy as jnp
from jax import lax
from jax.experimental import pallas as pl
from jax.experimental.pallas import tpu as pltpu
from jax.sharding import PartitionSpec as P

TR = 40
COLT = 128
SLOTS = 3
STEP_SIZE = 0.5
PEERS = 64
MULT = 37
MESH = pl.DeviceIdType.MESH
F32 = jnp.float32
BF16 = jnp.bfloat16

ROWS = 640
WIDTH = 1280
BLOCKS = WIDTH // COLT
PAIRS = ROWS // (2 * TR)
TILES = (ROWS // TR) * BLOCKS
HEAD = 24
REST = TR - HEAD
EARLY = TR + HEAD
STRIPES = ROWS // TR
HEADS = 2 * STRIPES * HEAD
LATE = HEADS + WIDTH
LOADS = 4
PAIR = 2 * TR


def spin(me, step, sign):
    off = lax.rem(step * MULT, PEERS)
    x = lax.rem(lax.rem(me, 4) + 4 + sign * lax.rem(off, 4), 4)
    y = lax.rem(lax.rem(lax.div(me, 4), 4) + 4 + sign * lax.rem(lax.div(off, 4), 4), 4)
    z = lax.rem(lax.div(me, 16) + 4 + sign * lax.div(off, 16), 4)
    return (z * 4 + y) * 4 + x


def rows_at(start, size, unit):
    return pl.ds(pl.multiple_of(start, unit), size)


def kernel(
    gen, mag, ham, slot_ref, dims_in, pp_in, cc_in, send_in, recv_in, weight_in,
    flow_out,
    dims_ref, pp_v, cc_ref, send_ref, recv_ref, weight_ref, small_sem,
    gen_v, mag_v, ham_v, stack, stack_late, sbuf, sbuf_late, near, near_late, far, far_late,
    right, left, plain, perm, base, cross_a, cross_b, tsend_a, tsend_b, trecv_a, trecv_b,
    inv_v, inv_s,
    in_sem, inv_sem, out_sem, self_sem, send_sem, recv_sem, hand_sem, take_sem,
    strip_send, strip_recv, bsend_sem, brecv_sem, bself_sem,
):
    me = lax.axis_index("chan")
    row = lax.axis_index("row")
    other = 1 - row

    def load(part, start):
        for n, (src, dst) in enumerate(((gen, gen_v), (mag, mag_v), (ham, ham_v))):
            at = rows_at(part * (ROWS // LOADS), ROWS // LOADS, 16)
            copy = pltpu.make_async_copy(src.at[0, at], dst.at[at], in_sem.at[n, part])
            copy.start() if start else copy.wait()

    for part in range(LOADS):
        load(part, True)
    small = [
        pltpu.make_async_copy(src, dst, small_sem.at[n])
        for n, (src, dst) in enumerate(
            (
                (dims_in, dims_ref),
                (send_in, send_ref),
                (recv_in, recv_ref),
                (weight_in, weight_ref),
                (cc_in, cc_ref),
                (pp_in, pp_v),
            )
        )
    ]
    for copy in small:
        copy.start()
    barrier = pltpu.get_barrier_semaphore()

    def greet(step, _):
        pl.semaphore_signal(
            barrier, inc=1, device_id={"chan": lax.rem(me + step, PEERS)}, device_id_type=MESH
        )
        return 0

    lax.fori_loop(1, PEERS, greet, 0)
    pl.semaphore_signal(barrier, inc=1, device_id={"row": other}, device_id_type=MESH)

    for copy in small[:2]:
        copy.wait()
    limit = dims_ref[slot_ref[0]]

    def live(i, k):
        row_ids = row * ROWS + i * PAIR + lax.broadcasted_iota(jnp.int32, (PAIR, COLT), 0)
        col_ids = k * COLT + lax.broadcasted_iota(jnp.int32, (1, COLT), 1)
        return row_ids < jnp.where(col_ids < limit, limit, 0)

    def cut(i):
        at = rows_at(i * PAIR, PAIR, 16)
        for k in range(BLOCKS):
            col = pl.ds(k * COLT, COLT)
            new = (mag_v[at, col].astype(F32) + STEP_SIZE * gen_v[at, col].astype(F32)).astype(BF16)
            mag_v[at, col] = new
            mask = live(i, k)
            m = jnp.where(mask, new.astype(F32), 0.0)
            h = jnp.where(mask, ham_v[at, col].astype(F32), 0.0)
            for top in (0, TR):
                tile = (2 * i + top // TR) * BLOCKS + k
                stack[tile] = jnp.concatenate(
                    [m[top : top + TR], h[top : top + HEAD]], axis=0
                ).astype(BF16)
                stack_late[tile] = h[top + HEAD : top + TR].astype(BF16)

    def prologue(part, _):
        load(part, False)
        for sub in range(PAIRS // LOADS):
            cut(part * (PAIRS // LOADS) + sub)
        return 0

    lax.fori_loop(0, LOADS, prologue, 0)
    pl.semaphore_wait(barrier, PEERS)

    waves = ((stack, sbuf, near, far), (stack_late, sbuf_late, near_late, far_late))

    def slots_of(peer):
        return pl.ds(peer * SLOTS, SLOTS)

    def pick(to, tiles, out):
        for l in range(SLOTS):
            tile = jnp.minimum(send_ref[l, 0, to], TILES - 1)
            out[to * SLOTS + l] = tiles[tile]

    def message(wave, step, to, place):
        _, out, held, _ = waves[wave]
        return pltpu.make_async_remote_copy(
            out.at[slots_of(to)], held.at[slots_of(place)], send_sem.at[wave], recv_sem.at[wave, step],
            device_id={"chan": to}, device_id_type=MESH,
        )

    def handed(wave, at):
        _, _, held, passed = waves[wave]
        return pltpu.make_async_remote_copy(
            held.at[at], passed.at[at], hand_sem.at[wave], take_sem.at[wave],
            device_id={"row": other}, device_id_type=MESH,
        )

    mine = []
    for wave, (tiles, out, held, _) in enumerate(waves):

        def send_out(step, _):
            to = spin(me, step, 1)
            pick(to, tiles, out)
            message(wave, step, to, me).start()
            return 0

        lax.fori_loop(1, PEERS, send_out, 0)
        pick(me, tiles, out)
        mine.append(
            pltpu.make_async_copy(out.at[slots_of(me)], held.at[slots_of(me)], self_sem.at[wave])
        )
        mine[wave].start()

    for copy in small[2:]:
        copy.wait()
    chosen = lax.broadcasted_iota(jnp.int32, pp_v.shape, 0) == slot_ref[0]
    factor = jnp.sum(jnp.where(chosen, pp_v[...], 0.0), axis=0, keepdims=True)

    def strips(i, _):
        at = rows_at(i * PAIR, PAIR, 16)
        for k in range(BLOCKS):
            col = pl.ds(k * COLT, COLT)
            mask = live(i, k)
            m = jnp.where(mask, mag_v[at, col].astype(F32), 0.0)
            h = jnp.where(mask, ham_v[at, col].astype(F32), 0.0)
            f = factor[:, k * COLT : (k + 1) * COLT]
            right[rows_at(row * ROWS + i * PAIR, PAIR, 16), col] = h.astype(BF16)
            right[rows_at(WIDTH + row * ROWS + i * PAIR, PAIR, 16), col] = m.astype(BF16)
            left[at, col] = (m * f).astype(BF16)
            left[at, pl.ds(WIDTH + k * COLT, COLT)] = (h * -f).astype(BF16)
            base[rows_at(k * ROWS + i * PAIR, PAIR, 8), :] = h
        return 0

    lax.fori_loop(0, PAIRS, strips, 0)

    def order(i, _):
        at = rows_at(i * PAIR, PAIR, 16)
        inside = lax.broadcasted_iota(jnp.int32, (PAIR, COLT), 0)
        second = jnp.where(inside >= TR, 1, 0)
        inside = inside - TR * second
        stripe = 2 * i + second
        target = jnp.where(
            inside < HEAD, stripe * HEAD + inside, HEADS + stripe * REST + inside - HEAD
        )
        for k in range(BLOCKS):
            ids = k * COLT + lax.broadcasted_iota(jnp.int32, (PAIR, COLT), 1)
            perm[at, pl.ds(k * COLT, COLT)] = jnp.where(target == ids, 1.0, 0.0).astype(BF16)
        return 0

    lax.fori_loop(0, WIDTH // PAIR, order, 0)

    def strip(which, r):
        at = rows_at(which * WIDTH + r * ROWS, ROWS, 16)
        return pltpu.make_async_remote_copy(
            right.at[at], right.at[at], strip_send.at[which], strip_recv.at[which],
            device_id={"row": other}, device_id_type=MESH,
        )

    for which in range(2):
        strip(which, row).start()
    for wave in range(2):
        mine[wave].wait()
        handed(wave, slots_of(me)).start()

    place = lax.broadcasted_iota(jnp.int32, (8, COLT), 0) * COLT + lax.broadcasted_iota(
        jnp.int32, (8, COLT), 1
    )

    def invert_recv(v, table):
        return jnp.where(place == recv_ref[0, v], v, table)

    def invert_send(d, table):
        for l in range(SLOTS):
            table = jnp.where(place == send_ref[l, 0, d], d * SLOTS + l, table)
        return table

    blank = jnp.zeros((8, COLT), jnp.int32)
    inv_v[0] = lax.fori_loop(0, TILES, invert_recv, blank)
    inv_v[1] = lax.fori_loop(0, PEERS, invert_send, blank)
    inv_copy = pltpu.make_async_copy(inv_v, inv_s, inv_sem)
    inv_copy.start()

    for which in range(2):
        strip(which, other).wait_recv()
        strip(which, row).wait_send()

    part = jnp.dot(left[...], right[...], preferred_element_type=F32)
    for k in range(BLOCKS):
        base[pl.ds(k * ROWS, ROWS), :] += part[:, k * COLT : (k + 1) * COLT]
    inv_copy.wait()

    def hand_on(wave):
        def body(step, _):
            fr = spin(me, step, -1)
            message(wave, step, fr, fr).wait_recv()
            handed(wave, slots_of(fr)).start()
            return 0

        lax.fori_loop(1, PEERS, body, 0)

    all_slots = pl.ds(0, PEERS * SLOTS)
    all_handed = [handed(wave, all_slots) for wave in range(2)]

    def weighted(tiles, i, k):
        ids = [(2 * i + half) * BLOCKS + k for half in range(2)]
        return [weight_ref[0, v] * tiles[recv_ref[0, v]].astype(F32) for v in ids]

    def both(parts, start, stop):
        return jnp.concatenate([parts[0][start:stop], parts[1][start:stop]], axis=0)

    def settle(tiles, r, own):
        def body(i, _):
            for k in range(BLOCKS):
                col = pl.ds(k * COLT, COLT)
                parts = weighted(tiles, i, k)
                m, h = both(parts, 0, TR), both(parts, TR, EARLY)
                right[rows_at(HEADS + r * ROWS + i * PAIR, PAIR, 16), col] = m.astype(BF16)
                right[rows_at((r * STRIPES + 2 * i) * HEAD, 2 * HEAD, 16), col] = h.astype(BF16)
                if own:
                    f = cc_ref[:, k * COLT : (k + 1) * COLT]
                    first = rows_at(i * 2 * HEAD, 2 * HEAD, 16)
                    second = rows_at(STRIPES * HEAD + i * 2 * REST, 2 * REST, 16)
                    plain[first, col] = (both(parts, 0, HEAD) * f).astype(BF16)
                    plain[second, col] = (both(parts, HEAD, TR) * f).astype(BF16)
                    left[first, pl.ds(HEADS + k * COLT, COLT)] = (h * -f).astype(BF16)
            return 0

        lax.fori_loop(0, PAIRS, body, 0)

    def settle_late(tiles, r, own):
        def body(i, _):
            for k in range(BLOCKS):
                h = both(weighted(tiles, i, k), 0, REST)
                at = rows_at(LATE + (r * STRIPES + 2 * i) * REST, 2 * REST, 16)
                right[at, pl.ds(k * COLT, COLT)] = h.astype(BF16)
                if own:
                    f = cc_ref[:, k * COLT : (k + 1) * COLT]
                    second = rows_at(STRIPES * HEAD + i * 2 * REST, 2 * REST, 16)
                    left[second, pl.ds(HEADS + k * COLT, COLT)] = (h * -f).astype(BF16)
            return 0

        lax.fori_loop(0, PAIRS, body, 0)

    def product(rows, depth, size, cross, add):
        part = jnp.dot(left[rows, depth], right[depth, :], preferred_element_type=F32)
        for a in range(STRIPES):
            for k in range(BLOCKS):
                block = part[a * size : (a + 1) * size, k * COLT : (k + 1) * COLT]
                tile = a * BLOCKS + k
                cross[tile] = cross[tile] + block if add else block

    head_rows = slice(0, STRIPES * HEAD)
    rest_rows = slice(STRIPES * HEAD, ROWS)

    hand_on(0)
    settle(near, row, True)
    all_handed[0].wait_recv()
    settle(far, other, False)
    ordered = jnp.dot(plain[...], perm[...], preferred_element_type=F32).astype(BF16)
    left[:, :HEADS] = ordered[:, :HEADS]
    left[:, LATE:] = ordered[:, HEADS:]
    product(head_rows, slice(0, LATE), HEAD, cross_a, False)
    product(rest_rows, slice(0, HEADS), REST, cross_b, False)

    hand_on(1)
    settle_late(near_late, row, True)
    all_handed[1].wait_recv()
    settle_late(far_late, other, False)

    def pick_back(to, cross, tsend):
        for l in range(SLOTS):
            slot = to * SLOTS + l
            v = inv_s[0, lax.div(slot, COLT), lax.rem(slot, COLT)]
            tsend[slot] = (weight_ref[0, v] * cross[v]).astype(BF16)

    mine_at = pl.ds(me * SLOTS, SLOTS)
    parts_back = (
        (head_rows, slice(LATE, 2 * WIDTH), HEAD, cross_a, tsend_a, trecv_a),
        (rest_rows, slice(HEADS, 2 * WIDTH), REST, cross_b, tsend_b, trecv_b),
    )
    homes = []
    for n, (rows, depth, size, cross, tsend, trecv) in enumerate(parts_back):
        product(rows, depth, size, cross, True)

        def send_back(step, _):
            to = spin(me, step, 1)
            pick_back(to, cross, tsend)
            pltpu.make_async_remote_copy(
                tsend.at[pl.ds(to * SLOTS, SLOTS)], trecv.at[mine_at], bsend_sem.at[n], brecv_sem.at[n],
                device_id={"chan": to}, device_id_type=MESH,
            ).start()
            return 0

        lax.fori_loop(1, PEERS, send_back, 0)
        pick_back(me, cross, tsend)
        homes.append(pltpu.make_async_copy(tsend.at[mine_at], trecv.at[mine_at], bself_sem.at[n]))
        homes[n].start()

    others = pl.ds(0, (PEERS - 1) * SLOTS)
    all_back = [
        pltpu.make_async_remote_copy(
            tsend.at[others], trecv.at[others], bsend_sem.at[n], brecv_sem.at[n],
            device_id={"row": other}, device_id_type=MESH,
        )
        for n, (_, _, _, _, tsend, trecv) in enumerate(parts_back)
    ]
    def out_copy(i):
        at = rows_at(i * PAIR, PAIR, 16)
        return pltpu.make_async_copy(gen_v.at[at], flow_out.at[0, at], out_sem.at[i])

    def tile_back(trecv, i, half, k):
        u = (2 * i + half) * BLOCKS + k
        return trecv[inv_s[1, lax.div(u, COLT), lax.rem(u, COLT)]].astype(F32)

    def add_heads(i, _):
        for k in range(BLOCKS):
            mask = live(i, k)
            for half in range(2):
                at = rows_at(k * ROWS + i * PAIR + half * TR, HEAD, 8)
                keep = mask[half * TR : half * TR + HEAD]
                base[at, :] += jnp.where(keep, tile_back(trecv_a, i, half, k), 0.0)
        return 0

    def finish(i, _):
        at = rows_at(i * PAIR, PAIR, 16)
        for k in range(BLOCKS):
            mask = live(i, k)
            pieces = []
            for half in range(2):
                start = k * ROWS + i * PAIR + half * TR
                keep = mask[half * TR + HEAD : (half + 1) * TR]
                pieces.append(base[rows_at(start, HEAD, 8), :])
                pieces.append(
                    base[rows_at(start + HEAD, REST, 8), :]
                    + jnp.where(keep, tile_back(trecv_b, i, half, k), 0.0)
                )
            gen_v[at, pl.ds(k * COLT, COLT)] = jnp.concatenate(pieces, axis=0).astype(BF16)
        out_copy(i).start()
        return 0

    homes[0].wait()
    all_back[0].wait_recv()
    lax.fori_loop(0, PAIRS, add_heads, 0)
    homes[1].wait()
    all_back[1].wait_recv()
    lax.fori_loop(0, PAIRS, finish, 0)

    for n, (_, out, held, _) in enumerate(waves):
        pltpu.make_async_remote_copy(
            out.at[others], held.at[others], send_sem.at[n], recv_sem.at[n, 0],
            device_id={"row": other}, device_id_type=MESH,
        ).wait_send()
        all_handed[n].wait_send()
        all_back[n].wait_send()
    for i in range(PAIRS):
        out_copy(i).wait()


def per_device(gen, mag, ham, slot, dims, pp, cc, send, recv, weight):
    strip = jax.ShapeDtypeStruct(gen.shape, BF16)
    magnus_new = (mag.astype(F32) + STEP_SIZE * gen.astype(F32)).astype(BF16)
    args = (gen, mag, ham, slot, dims, pp, cc, send.transpose(2, 0, 1), recv, weight)
    hbm = pl.BlockSpec(memory_space=pltpu.HBM)
    dma = pltpu.SemaphoreType.DMA
    flowed = pl.pallas_call(
        kernel,
        out_shape=strip,
        in_specs=[hbm] * 3 + [pl.BlockSpec(memory_space=pltpu.SMEM)] + [hbm] * 6,
        out_specs=hbm,
        scratch_shapes=[
            pltpu.SMEM(dims.shape, jnp.int32),
            pltpu.VMEM(pp.shape, F32),
            pltpu.VMEM(cc.shape, F32),
            pltpu.SMEM(args[7].shape, jnp.int32),
            pltpu.SMEM(recv.shape, jnp.int32),
            pltpu.SMEM(weight.shape, F32),
            dma((6,)),
            pltpu.VMEM((ROWS, WIDTH), BF16),
            pltpu.VMEM((ROWS, WIDTH), BF16),
            pltpu.VMEM((ROWS, WIDTH), BF16),
            pltpu.VMEM((TILES, EARLY, COLT), BF16),
            pltpu.VMEM((TILES, REST, COLT), BF16),
            pltpu.VMEM((PEERS * SLOTS, EARLY, COLT), BF16),
            pltpu.VMEM((PEERS * SLOTS, REST, COLT), BF16),
            pltpu.VMEM((PEERS * SLOTS, EARLY, COLT), BF16),
            pltpu.VMEM((PEERS * SLOTS, REST, COLT), BF16),
            pltpu.VMEM((PEERS * SLOTS, EARLY, COLT), BF16),
            pltpu.VMEM((PEERS * SLOTS, REST, COLT), BF16),
            pltpu.VMEM((2 * WIDTH, WIDTH), BF16),
            pltpu.VMEM((ROWS, 2 * WIDTH), BF16),
            pltpu.VMEM((ROWS, WIDTH), BF16),
            pltpu.VMEM((WIDTH, WIDTH), BF16),
            pltpu.VMEM((BLOCKS * ROWS, COLT), F32),
            pltpu.VMEM((TILES, HEAD, COLT), F32),
            pltpu.VMEM((TILES, REST, COLT), F32),
            pltpu.VMEM((PEERS * SLOTS, HEAD, COLT), BF16),
            pltpu.VMEM((PEERS * SLOTS, REST, COLT), BF16),
            pltpu.VMEM((PEERS * SLOTS, HEAD, COLT), BF16),
            pltpu.VMEM((PEERS * SLOTS, REST, COLT), BF16),
            pltpu.VMEM((2, 8, COLT), jnp.int32),
            pltpu.SMEM((2, 8, COLT), jnp.int32),
            dma((3, LOADS)),
            dma,
            dma((PAIRS,)),
            dma((2,)),
            dma((2,)),
            dma((2, PEERS)),
            dma((2,)),
            dma((2,)),
            dma((2,)),
            dma((2,)),
            dma((2,)),
            dma((2,)),
            dma((2,)),
        ],
        compiler_params=pltpu.CompilerParams(
            collective_id=0, has_side_effects=True, vmem_limit_bytes=58 << 20
        ),
    )(*args)
    return magnus_new, flowed


def solution(mesh):
    return jax.shard_map(
        per_device,
        mesh=mesh,
        in_specs=(
            P("chan", "row", None),
            P("chan", "row", None),
            P("chan", "row", None),
            P("chan"),
            P(),
            P(),
            P("chan", None),
            P("chan", None, None),
            P("chan", None),
            P("chan", None),
        ),
        out_specs=(P("chan", "row", None), P("chan", "row", None)),
        check_vma=False,
    )
```

```python
import functools

import jax
import jax.numpy as jnp
from jax import lax
from jax.experimental import pallas as pl
from jax.experimental.pallas import tpu as pltpu
from jax.sharding import PartitionSpec as P

TR = 40
COLT = 128
SLOTS = 3
STEP_SIZE = 0.5
PEERS = 64
MULT = 37
MESH = pl.DeviceIdType.MESH
F32 = jnp.float32
BF16 = jnp.bfloat16

ROWS = 640
WIDTH = 1280
BLOCKS = WIDTH // COLT
PAIRS = ROWS // (2 * TR)
TILES = (ROWS // TR) * BLOCKS
HEAD = 16
REST = TR - HEAD
LOADS = 4
PAIR = 2 * TR


def spin(me, step, sign):
    off = lax.rem(step * MULT, PEERS)
    x = lax.rem(lax.rem(me, 4) + 4 + sign * lax.rem(off, 4), 4)
    y = lax.rem(lax.rem(lax.div(me, 4), 4) + 4 + sign * lax.rem(lax.div(off, 4), 4), 4)
    z = lax.rem(lax.div(me, 16) + 4 + sign * lax.div(off, 16), 4)
    return (z * 4 + y) * 4 + x


def rows_at(start, size, unit):
    return pl.ds(pl.multiple_of(start, unit), size)


def kernel(
    gen, mag, ham, slot_ref, dims_in, pp_in, cc_in, send_in, recv_in, weight_in,
    new_out, flow_out,
    dims_ref, pp_v, cc_ref, send_ref, recv_ref, weight_ref, small_sem,
    gen_v, mag_v, ham_v, stack, sbuf, near, far, right, left, base, cross_a, cross_b, tsend_a, tsend_b, trecv_a, trecv_b,
    inv_v, inv_s,
    in_sem, inv_sem, self_sem, send_sem, recv_sem, hand_sem, take_sem,
    strip_send, strip_recv, bsend_sem, brecv_sem, bself_sem,
):
    me = lax.axis_index("chan")
    row = lax.axis_index("row")
    other = 1 - row

    def load(part, start):
        for n, (src, dst) in enumerate(((gen, gen_v), (mag, mag_v), (ham, ham_v))):
            at = rows_at(part * (ROWS // LOADS), ROWS // LOADS, 16)
            copy = pltpu.make_async_copy(src.at[0, at], dst.at[at], in_sem.at[n, part])
            copy.start() if start else copy.wait()

    for part in range(LOADS):
        load(part, True)
    small = [
        pltpu.make_async_copy(src, dst, small_sem.at[n])
        for n, (src, dst) in enumerate(
            (
                (dims_in, dims_ref),
                (send_in, send_ref),
                (recv_in, recv_ref),
                (weight_in, weight_ref),
                (cc_in, cc_ref),
                (pp_in, pp_v),
            )
        )
    ]
    for copy in small:
        copy.start()
    barrier = pltpu.get_barrier_semaphore()

    def greet(step, _):
        pl.semaphore_signal(
            barrier, inc=1, device_id={"chan": lax.rem(me + step, PEERS)}, device_id_type=MESH
        )
        return 0

    lax.fori_loop(1, PEERS, greet, 0)
    pl.semaphore_signal(barrier, inc=1, device_id={"row": other}, device_id_type=MESH)

    for copy in small[:2]:
        copy.wait()
    limit = dims_ref[slot_ref[0]]

    def live(i, k):
        row_ids = row * ROWS + i * PAIR + lax.broadcasted_iota(jnp.int32, (PAIR, COLT), 0)
        col_ids = k * COLT + lax.broadcasted_iota(jnp.int32, (1, COLT), 1)
        return row_ids < jnp.where(col_ids < limit, limit, 0)

    def cut(i):
        at = rows_at(i * PAIR, PAIR, 16)
        for k in range(BLOCKS):
            col = pl.ds(k * COLT, COLT)
            new = (mag_v[at, col].astype(F32) + STEP_SIZE * gen_v[at, col].astype(F32)).astype(BF16)
            new_out[0, at, col] = new
            mask = live(i, k)
            m = jnp.where(mask, new.astype(F32), 0.0)
            h = jnp.where(mask, ham_v[at, col].astype(F32), 0.0)
            for top in (0, TR):
                stack[(2 * i + top // TR) * BLOCKS + k] = jnp.concatenate(
                    [m[top : top + TR], h[top : top + TR]], axis=0
                ).astype(BF16)

    def prologue(part, _):
        load(part, False)
        for sub in range(PAIRS // LOADS):
            cut(part * (PAIRS // LOADS) + sub)
        return 0

    lax.fori_loop(0, LOADS, prologue, 0)
    pl.semaphore_wait(barrier, PEERS)

    def pick(to):
        for l in range(SLOTS):
            tile = jnp.minimum(send_ref[l, 0, to], TILES - 1)
            sbuf[to * SLOTS + l] = stack[tile]

    def message(step):
        to = spin(me, step, 1)
        return pltpu.make_async_remote_copy(
            sbuf.at[pl.ds(to * SLOTS, SLOTS)],
            near.at[pl.ds(me * SLOTS, SLOTS)],
            send_sem,
            recv_sem.at[step],
            device_id={"chan": to},
            device_id_type=MESH,
        )

    def arrival(step):
        fr = spin(me, step, -1)
        return pltpu.make_async_remote_copy(
            sbuf.at[pl.ds(fr * SLOTS, SLOTS)],
            near.at[pl.ds(fr * SLOTS, SLOTS)],
            send_sem,
            recv_sem.at[step],
            device_id={"chan": fr},
            device_id_type=MESH,
        )

    def handed(step):
        at = pl.ds(spin(me, step, -1) * SLOTS, SLOTS)
        return pltpu.make_async_remote_copy(
            near.at[at], far.at[at], hand_sem, take_sem,
            device_id={"row": other}, device_id_type=MESH,
        )

    def send_out(step, _):
        pick(spin(me, step, 1))
        message(step).start()
        return 0

    lax.fori_loop(1, PEERS, send_out, 0)
    pick(me)
    mine = pltpu.make_async_copy(
        sbuf.at[pl.ds(me * SLOTS, SLOTS)], near.at[pl.ds(me * SLOTS, SLOTS)], self_sem
    )
    mine.start()

    for copy in small[2:]:
        copy.wait()
    chosen = lax.broadcasted_iota(jnp.int32, pp_v.shape, 0) == slot_ref[0]
    factor = jnp.sum(jnp.where(chosen, pp_v[...], 0.0), axis=0, keepdims=True)

    def strips(i, _):
        at = rows_at(i * PAIR, PAIR, 16)
        for k in range(BLOCKS):
            col = pl.ds(k * COLT, COLT)
            mask = live(i, k)
            m = jnp.where(mask, new_out[0, at, col].astype(F32), 0.0)
            h = jnp.where(mask, ham_v[at, col].astype(F32), 0.0)
            f = factor[:, k * COLT : (k + 1) * COLT]
            right[rows_at(row * ROWS + i * PAIR, PAIR, 16), col] = h.astype(BF16)
            right[rows_at(WIDTH + row * ROWS + i * PAIR, PAIR, 16), col] = m.astype(BF16)
            left[at, col] = (m * f).astype(BF16)
            left[at, pl.ds(WIDTH + k * COLT, COLT)] = (h * -f).astype(BF16)
            base[rows_at(k * ROWS + i * PAIR, PAIR, 8), :] = h
        return 0

    lax.fori_loop(0, PAIRS, strips, 0)

    def strip(which, r):
        at = rows_at(which * WIDTH + r * ROWS, ROWS, 16)
        return pltpu.make_async_remote_copy(
            right.at[at], right.at[at], strip_send.at[which], strip_recv.at[which],
            device_id={"row": other}, device_id_type=MESH,
        )

    for which in range(2):
        strip(which, row).start()
    mine.wait()
    handed(0).start()

    place = lax.broadcasted_iota(jnp.int32, (8, COLT), 0) * COLT + lax.broadcasted_iota(
        jnp.int32, (8, COLT), 1
    )

    def invert_recv(v, table):
        return jnp.where(place == recv_ref[0, v], v, table)

    def invert_send(d, table):
        for l in range(SLOTS):
            table = jnp.where(place == send_ref[l, 0, d], d * SLOTS + l, table)
        return table

    blank = jnp.zeros((8, COLT), jnp.int32)
    inv_v[0] = lax.fori_loop(0, TILES, invert_recv, blank)
    inv_v[1] = lax.fori_loop(0, PEERS, invert_send, blank)
    inv_copy = pltpu.make_async_copy(inv_v, inv_s, inv_sem)
    inv_copy.start()

    for which in range(2):
        strip(which, other).wait_recv()
        strip(which, row).wait_send()

    part = jnp.dot(left[...], right[...], preferred_element_type=F32)
    for k in range(BLOCKS):
        base[pl.ds(k * ROWS, ROWS), :] += part[:, k * COLT : (k + 1) * COLT]
    inv_copy.wait()

    def hand_on(step, _):
        arrival(step).wait_recv()
        handed(step).start()
        return 0

    lax.fori_loop(1, PEERS, hand_on, 0)

    def settle(tiles, r, own):
        def body(i, _):
            at = rows_at(r * ROWS + i * PAIR, PAIR, 16)
            under = rows_at(WIDTH + r * ROWS + i * PAIR, PAIR, 16)
            for k in range(BLOCKS):
                col = pl.ds(k * COLT, COLT)
                parts = []
                for half in range(2):
                    v = (2 * i + half) * BLOCKS + k
                    tile = tiles[recv_ref[0, v]]
                    parts.append(weight_ref[0, v] * tile.astype(F32))
                m = jnp.concatenate([parts[0][:TR], parts[1][:TR]], axis=0)
                h = jnp.concatenate([parts[0][TR:], parts[1][TR:]], axis=0)
                right[at, col] = h.astype(BF16)
                right[under, col] = m.astype(BF16)
                if own:
                    f = cc_ref[:, k * COLT : (k + 1) * COLT]
                    first = rows_at(i * 2 * HEAD, 2 * HEAD, 16)
                    second = rows_at(ROWS // TR * HEAD + i * 2 * REST, 2 * REST, 16)
                    for value, place in ((m * f, k * COLT), (h * -f, WIDTH + k * COLT)):
                        side = pl.ds(place, COLT)
                        left[first, side] = jnp.concatenate(
                            [value[:HEAD], value[TR : TR + HEAD]], axis=0
                        ).astype(BF16)
                        left[second, side] = jnp.concatenate(
                            [value[HEAD:TR], value[TR + HEAD :]], axis=0
                        ).astype(BF16)
            return 0

        lax.fori_loop(0, PAIRS, body, 0)

    settle(near, row, True)

    all_handed = pltpu.make_async_remote_copy(
        near, far, hand_sem, take_sem, device_id={"row": other}, device_id_type=MESH
    )
    all_handed.wait_recv()
    settle(far, other, False)

    def product(start, size, cross):
        rows = left[start : start + size * (ROWS // TR), :]
        part = jnp.dot(rows, right[...], preferred_element_type=F32)
        for a in range(ROWS // TR):
            for k in range(BLOCKS):
                cross[a * BLOCKS + k] = part[a * size : (a + 1) * size, k * COLT : (k + 1) * COLT]

    def pick_back(to, cross, tsend):
        for l in range(SLOTS):
            slot = to * SLOTS + l
            v = inv_s[0, lax.div(slot, COLT), lax.rem(slot, COLT)]
            tsend[slot] = (weight_ref[0, v] * cross[v]).astype(BF16)

    mine_at = pl.ds(me * SLOTS, SLOTS)
    parts_back = ((0, HEAD, cross_a, tsend_a, trecv_a), (ROWS // TR * HEAD, REST, cross_b, tsend_b, trecv_b))
    homes = []
    for n, (start, size, cross, tsend, trecv) in enumerate(parts_back):
        product(start, size, cross)

        def send_back(step, _):
            to = spin(me, step, 1)
            pick_back(to, cross, tsend)
            pltpu.make_async_remote_copy(
                tsend.at[pl.ds(to * SLOTS, SLOTS)], trecv.at[mine_at], bsend_sem.at[n], brecv_sem.at[n],
                device_id={"chan": to}, device_id_type=MESH,
            ).start()
            return 0

        lax.fori_loop(1, PEERS, send_back, 0)
        pick_back(me, cross, tsend)
        homes.append(pltpu.make_async_copy(tsend.at[mine_at], trecv.at[mine_at], bself_sem.at[n]))
        homes[n].start()

    others = pl.ds(0, (PEERS - 1) * SLOTS)
    all_back = [
        pltpu.make_async_remote_copy(
            tsend.at[others], trecv.at[others], bsend_sem.at[n], brecv_sem.at[n],
            device_id={"row": other}, device_id_type=MESH,
        )
        for n, (_, _, _, tsend, trecv) in enumerate(parts_back)
    ]
    def tile_back(trecv, i, half, k):
        u = (2 * i + half) * BLOCKS + k
        return trecv[inv_s[1, lax.div(u, COLT), lax.rem(u, COLT)]].astype(F32)

    def add_heads(i, _):
        for k in range(BLOCKS):
            mask = live(i, k)
            for half in range(2):
                at = rows_at(k * ROWS + i * PAIR + half * TR, HEAD, 8)
                keep = mask[half * TR : half * TR + HEAD]
                base[at, :] += jnp.where(keep, tile_back(trecv_a, i, half, k), 0.0)
        return 0

    def finish(i, _):
        at = rows_at(i * PAIR, PAIR, 16)
        for k in range(BLOCKS):
            mask = live(i, k)
            pieces = []
            for half in range(2):
                start = k * ROWS + i * PAIR + half * TR
                keep = mask[half * TR + HEAD : (half + 1) * TR]
                pieces.append(base[rows_at(start, HEAD, 8), :])
                pieces.append(
                    base[rows_at(start + HEAD, REST, 8), :]
                    + jnp.where(keep, tile_back(trecv_b, i, half, k), 0.0)
                )
            flow_out[0, at, pl.ds(k * COLT, COLT)] = jnp.concatenate(pieces, axis=0).astype(BF16)
        return 0

    homes[0].wait()
    all_back[0].wait_recv()
    lax.fori_loop(0, PAIRS, add_heads, 0)
    homes[1].wait()
    all_back[1].wait_recv()
    lax.fori_loop(0, PAIRS, finish, 0)

    pltpu.make_async_remote_copy(
        sbuf.at[others], near.at[others], send_sem, recv_sem.at[0],
        device_id={"row": other}, device_id_type=MESH,
    ).wait_send()
    all_handed.wait_send()
    for n in range(2):
        all_back[n].wait_send()


def write_out(new, flow, new_out, flow_out, sem):
    copies = []
    for n, (src, dst) in enumerate(((new, new_out), (flow, flow_out))):
        for part in range(LOADS):
            at = pl.ds(part * (ROWS // LOADS), ROWS // LOADS)
            copies.append(pltpu.make_async_copy(src.at[0, at], dst.at[0, at], sem.at[n, part]))
    for copy in copies:
        copy.start()
    for copy in copies:
        copy.wait()


def per_device(gen, mag, ham, slot, dims, pp, cc, send, recv, weight):
    args = (gen, mag, ham, slot, dims, pp, cc, send.transpose(2, 0, 1), recv, weight)
    hbm = pl.BlockSpec(memory_space=pltpu.HBM)
    vmem = pl.BlockSpec(memory_space=pltpu.VMEM)
    dma = pltpu.SemaphoreType.DMA
    held = pl.pallas_call(
        kernel,
        out_shape=(pltpu.VMEM(gen.shape, BF16),) * 2,
        in_specs=[hbm] * 3 + [pl.BlockSpec(memory_space=pltpu.SMEM)] + [hbm] * 6,
        out_specs=(vmem, vmem),
        scratch_shapes=[
            pltpu.SMEM(dims.shape, jnp.int32),
            pltpu.VMEM(pp.shape, F32),
            pltpu.VMEM(cc.shape, F32),
            pltpu.SMEM(args[7].shape, jnp.int32),
            pltpu.SMEM(recv.shape, jnp.int32),
            pltpu.SMEM(weight.shape, F32),
            dma((6,)),
            pltpu.VMEM((ROWS, WIDTH), BF16),
            pltpu.VMEM((ROWS, WIDTH), BF16),
            pltpu.VMEM((ROWS, WIDTH), BF16),
            pltpu.VMEM((TILES, PAIR, COLT), BF16),
            pltpu.VMEM((PEERS * SLOTS, PAIR, COLT), BF16),
            pltpu.VMEM((PEERS * SLOTS, PAIR, COLT), BF16),
            pltpu.VMEM((PEERS * SLOTS, PAIR, COLT), BF16),
            pltpu.VMEM((2 * WIDTH, WIDTH), BF16),
            pltpu.VMEM((ROWS, 2 * WIDTH), BF16),
            pltpu.VMEM((BLOCKS * ROWS, COLT), F32),
            pltpu.VMEM((TILES, HEAD, COLT), F32),
            pltpu.VMEM((TILES, REST, COLT), F32),
            pltpu.VMEM((PEERS * SLOTS, HEAD, COLT), BF16),
            pltpu.VMEM((PEERS * SLOTS, REST, COLT), BF16),
            pltpu.VMEM((PEERS * SLOTS, HEAD, COLT), BF16),
            pltpu.VMEM((PEERS * SLOTS, REST, COLT), BF16),
            pltpu.VMEM((2, 8, COLT), jnp.int32),
            pltpu.SMEM((2, 8, COLT), jnp.int32),
            dma((3, LOADS)),
            dma,
            dma,
            dma,
            dma((PEERS,)),
            dma,
            dma,
            dma((2,)),
            dma((2,)),
            dma((2,)),
            dma((2,)),
            dma((2,)),
        ],
        compiler_params=pltpu.CompilerParams(
            collective_id=0, has_side_effects=True, vmem_limit_bytes=54 << 20
        ),
    )(*args)
    strip = jax.ShapeDtypeStruct(gen.shape, BF16)
    return pl.pallas_call(
        write_out,
        out_shape=(strip, strip),
        in_specs=[vmem, vmem],
        out_specs=(hbm, hbm),
        scratch_shapes=[dma((2, LOADS))],
    )(*held)


def solution(mesh):
    return jax.shard_map(
        per_device,
        mesh=mesh,
        in_specs=(
            P("chan", "row", None),
            P("chan", "row", None),
            P("chan", "row", None),
            P("chan"),
            P(),
            P(),
            P("chan", None),
            P("chan", None, None),
            P("chan", None),
            P("chan", None),
        ),
        out_specs=(P("chan", "row", None), P("chan", "row", None)),
        check_vma=False,
    )
```

```python
import functools

import jax
import jax.numpy as jnp
from jax import lax
from jax.experimental import pallas as pl
from jax.experimental.pallas import tpu as pltpu
from jax.sharding import PartitionSpec as P

TR = 40
COLT = 128
SLOTS = 3
STEP_SIZE = 0.5
PEERS = 64
MULT = 37
MESH = pl.DeviceIdType.MESH
F32 = jnp.float32
BF16 = jnp.bfloat16

ROWS = 640
WIDTH = 1280
BLOCKS = WIDTH // COLT
PAIRS = ROWS // (2 * TR)
TILES = (ROWS // TR) * BLOCKS
HEAD = 16
REST = TR - HEAD
LOADS = 4
PAIR = 2 * TR


def spin(me, step, sign):
    off = lax.rem(step * MULT, PEERS)
    x = lax.rem(lax.rem(me, 4) + 4 + sign * lax.rem(off, 4), 4)
    y = lax.rem(lax.rem(lax.div(me, 4), 4) + 4 + sign * lax.rem(lax.div(off, 4), 4), 4)
    z = lax.rem(lax.div(me, 16) + 4 + sign * lax.div(off, 16), 4)
    return (z * 4 + y) * 4 + x


def rows_at(start, size, unit):
    return pl.ds(pl.multiple_of(start, unit), size)


def kernel(
    gen, mag, ham, slot_ref, dims_in, pp_in, cc_in, send_in, recv_in, weight_in,
    new_out, flow_out,
    dims_ref, pp_v, cc_ref, send_ref, recv_ref, weight_ref, small_sem,
    gen_v, mag_v, ham_v, stack, sbuf, near, far, right, left, base, cross_a, cross_b, tsend_a, tsend_b, trecv_a, trecv_b,
    inv_v, inv_s,
    in_sem, inv_sem, self_sem, send_sem, recv_sem, hand_sem, take_sem,
    strip_send, strip_recv, bsend_sem, brecv_sem, bself_sem,
):
    me = lax.axis_index("chan")
    row = lax.axis_index("row")
    other = 1 - row

    def load(part, start):
        for n, (src, dst) in enumerate(((gen, gen_v), (mag, mag_v), (ham, ham_v))):
            at = rows_at(part * (ROWS // LOADS), ROWS // LOADS, 16)
            copy = pltpu.make_async_copy(src.at[0, at], dst.at[at], in_sem.at[n, part])
            copy.start() if start else copy.wait()

    for part in range(LOADS):
        load(part, True)
    small = [
        pltpu.make_async_copy(src, dst, small_sem.at[n])
        for n, (src, dst) in enumerate(
            (
                (dims_in, dims_ref),
                (send_in, send_ref),
                (recv_in, recv_ref),
                (weight_in, weight_ref),
                (cc_in, cc_ref),
                (pp_in, pp_v),
            )
        )
    ]
    for copy in small:
        copy.start()
    barrier = pltpu.get_barrier_semaphore()

    def greet(step, _):
        pl.semaphore_signal(
            barrier, inc=1, device_id={"chan": lax.rem(me + step, PEERS)}, device_id_type=MESH
        )
        return 0

    lax.fori_loop(1, PEERS, greet, 0)
    pl.semaphore_signal(barrier, inc=1, device_id={"row": other}, device_id_type=MESH)

    for copy in small[:2]:
        copy.wait()
    limit = dims_ref[slot_ref[0]]

    def live(i, k):
        row_ids = row * ROWS + i * PAIR + lax.broadcasted_iota(jnp.int32, (PAIR, COLT), 0)
        col_ids = k * COLT + lax.broadcasted_iota(jnp.int32, (1, COLT), 1)
        return row_ids < jnp.where(col_ids < limit, limit, 0)

    def cut(i):
        at = rows_at(i * PAIR, PAIR, 16)
        for k in range(BLOCKS):
            col = pl.ds(k * COLT, COLT)
            new = (mag_v[at, col].astype(F32) + STEP_SIZE * gen_v[at, col].astype(F32)).astype(BF16)
            new_out[0, at, col] = new
            mask = live(i, k)
            m = jnp.where(mask, new.astype(F32), 0.0)
            h = jnp.where(mask, ham_v[at, col].astype(F32), 0.0)
            for top in (0, TR):
                stack[(2 * i + top // TR) * BLOCKS + k] = jnp.concatenate(
                    [m[top : top + TR], h[top : top + TR]], axis=0
                ).astype(BF16)

    def prologue(part, _):
        load(part, False)
        for sub in range(PAIRS // LOADS):
            cut(part * (PAIRS // LOADS) + sub)
        return 0

    lax.fori_loop(0, LOADS, prologue, 0)
    pl.semaphore_wait(barrier, PEERS)

    def pick(to):
        for l in range(SLOTS):
            tile = jnp.minimum(send_ref[l, 0, to], TILES - 1)
            sbuf[to * SLOTS + l] = stack[tile]

    def message(step):
        to = spin(me, step, 1)
        return pltpu.make_async_remote_copy(
            sbuf.at[pl.ds(to * SLOTS, SLOTS)],
            near.at[pl.ds(me * SLOTS, SLOTS)],
            send_sem,
            recv_sem.at[step],
            device_id={"chan": to},
            device_id_type=MESH,
        )

    def arrival(step):
        fr = spin(me, step, -1)
        return pltpu.make_async_remote_copy(
            sbuf.at[pl.ds(fr * SLOTS, SLOTS)],
            near.at[pl.ds(fr * SLOTS, SLOTS)],
            send_sem,
            recv_sem.at[step],
            device_id={"chan": fr},
            device_id_type=MESH,
        )

    def handed(step):
        at = pl.ds(spin(me, step, -1) * SLOTS, SLOTS)
        return pltpu.make_async_remote_copy(
            near.at[at], far.at[at], hand_sem, take_sem,
            device_id={"row": other}, device_id_type=MESH,
        )

    def send_out(step, _):
        pick(spin(me, step, 1))
        message(step).start()
        return 0

    lax.fori_loop(1, PEERS, send_out, 0)
    pick(me)
    mine = pltpu.make_async_copy(
        sbuf.at[pl.ds(me * SLOTS, SLOTS)], near.at[pl.ds(me * SLOTS, SLOTS)], self_sem
    )
    mine.start()

    for copy in small[2:]:
        copy.wait()
    chosen = lax.broadcasted_iota(jnp.int32, pp_v.shape, 0) == slot_ref[0]
    factor = jnp.sum(jnp.where(chosen, pp_v[...], 0.0), axis=0, keepdims=True)

    def strips(i, _):
        at = rows_at(i * PAIR, PAIR, 16)
        for k in range(BLOCKS):
            col = pl.ds(k * COLT, COLT)
            mask = live(i, k)
            m = jnp.where(mask, new_out[0, at, col].astype(F32), 0.0)
            h = jnp.where(mask, ham_v[at, col].astype(F32), 0.0)
            f = factor[:, k * COLT : (k + 1) * COLT]
            right[rows_at(row * ROWS + i * PAIR, PAIR, 16), col] = h.astype(BF16)
            right[rows_at(WIDTH + row * ROWS + i * PAIR, PAIR, 16), col] = m.astype(BF16)
            left[at, col] = (m * f).astype(BF16)
            left[at, pl.ds(WIDTH + k * COLT, COLT)] = (h * -f).astype(BF16)
            base[rows_at(k * ROWS + i * PAIR, PAIR, 8), :] = h
        return 0

    lax.fori_loop(0, PAIRS, strips, 0)

    def strip(which, r):
        at = rows_at(which * WIDTH + r * ROWS, ROWS, 16)
        return pltpu.make_async_remote_copy(
            right.at[at], right.at[at], strip_send.at[which], strip_recv.at[which],
            device_id={"row": other}, device_id_type=MESH,
        )

    for which in range(2):
        strip(which, row).start()
    mine.wait()
    handed(0).start()

    place = lax.broadcasted_iota(jnp.int32, (8, COLT), 0) * COLT + lax.broadcasted_iota(
        jnp.int32, (8, COLT), 1
    )

    def invert_recv(v, table):
        return jnp.where(place == recv_ref[0, v], v, table)

    def invert_send(d, table):
        for l in range(SLOTS):
            table = jnp.where(place == send_ref[l, 0, d], d * SLOTS + l, table)
        return table

    blank = jnp.zeros((8, COLT), jnp.int32)
    inv_v[0] = lax.fori_loop(0, TILES, invert_recv, blank)
    inv_v[1] = lax.fori_loop(0, PEERS, invert_send, blank)
    inv_copy = pltpu.make_async_copy(inv_v, inv_s, inv_sem)
    inv_copy.start()

    for which in range(2):
        strip(which, other).wait_recv()
        strip(which, row).wait_send()

    part = jnp.dot(left[...], right[...], preferred_element_type=F32)
    for k in range(BLOCKS):
        base[pl.ds(k * ROWS, ROWS), :] += part[:, k * COLT : (k + 1) * COLT]
    inv_copy.wait()

    def hand_on(step, _):
        arrival(step).wait_recv()
        handed(step).start()
        return 0

    lax.fori_loop(1, PEERS, hand_on, 0)

    def settle(tiles, r, own):
        def body(i, _):
            at = rows_at(r * ROWS + i * PAIR, PAIR, 16)
            under = rows_at(WIDTH + r * ROWS + i * PAIR, PAIR, 16)
            for k in range(BLOCKS):
                col = pl.ds(k * COLT, COLT)
                parts = []
                for half in range(2):
                    v = (2 * i + half) * BLOCKS + k
                    tile = tiles[recv_ref[0, v]]
                    parts.append(weight_ref[0, v] * tile.astype(F32))
                m = jnp.concatenate([parts[0][:TR], parts[1][:TR]], axis=0)
                h = jnp.concatenate([parts[0][TR:], parts[1][TR:]], axis=0)
                right[at, col] = h.astype(BF16)
                right[under, col] = m.astype(BF16)
                if own:
                    f = cc_ref[:, k * COLT : (k + 1) * COLT]
                    first = rows_at(i * 2 * HEAD, 2 * HEAD, 16)
                    second = rows_at(ROWS // TR * HEAD + i * 2 * REST, 2 * REST, 16)
                    for value, place in ((m * f, k * COLT), (h * -f, WIDTH + k * COLT)):
                        side = pl.ds(place, COLT)
                        left[first, side] = jnp.concatenate(
                            [value[:HEAD], value[TR : TR + HEAD]], axis=0
                        ).astype(BF16)
                        left[second, side] = jnp.concatenate(
                            [value[HEAD:TR], value[TR + HEAD :]], axis=0
                        ).astype(BF16)
            return 0

        lax.fori_loop(0, PAIRS, body, 0)

    settle(near, row, True)

    all_handed = pltpu.make_async_remote_copy(
        near, far, hand_sem, take_sem, device_id={"row": other}, device_id_type=MESH
    )
    all_handed.wait_recv()
    settle(far, other, False)

    def product(start, size, cross):
        rows = left[start : start + size * (ROWS // TR), :]
        part = jnp.dot(rows, right[...], preferred_element_type=F32)
        for a in range(ROWS // TR):
            for k in range(BLOCKS):
                cross[a * BLOCKS + k] = part[a * size : (a + 1) * size, k * COLT : (k + 1) * COLT]

    def pick_back(to, cross, tsend):
        for l in range(SLOTS):
            slot = to * SLOTS + l
            v = inv_s[0, lax.div(slot, COLT), lax.rem(slot, COLT)]
            tsend[slot] = (weight_ref[0, v] * cross[v]).astype(BF16)

    mine_at = pl.ds(me * SLOTS, SLOTS)
    parts_back = ((0, HEAD, cross_a, tsend_a, trecv_a), (ROWS // TR * HEAD, REST, cross_b, tsend_b, trecv_b))
    homes = []
    for n, (start, size, cross, tsend, trecv) in enumerate(parts_back):
        product(start, size, cross)

        def send_back(step, _):
            to = spin(me, step, 1)
            pick_back(to, cross, tsend)
            pltpu.make_async_remote_copy(
                tsend.at[pl.ds(to * SLOTS, SLOTS)], trecv.at[mine_at], bsend_sem.at[n], brecv_sem.at[n],
                device_id={"chan": to}, device_id_type=MESH,
            ).start()
            return 0

        lax.fori_loop(1, PEERS, send_back, 0)
        pick_back(me, cross, tsend)
        homes.append(pltpu.make_async_copy(tsend.at[mine_at], trecv.at[mine_at], bself_sem.at[n]))
        homes[n].start()

    others = pl.ds(0, (PEERS - 1) * SLOTS)
    all_back = [
        pltpu.make_async_remote_copy(
            tsend.at[others], trecv.at[others], bsend_sem.at[n], brecv_sem.at[n],
            device_id={"row": other}, device_id_type=MESH,
        )
        for n, (_, _, _, tsend, trecv) in enumerate(parts_back)
    ]
    def tile_back(trecv, i, half, k):
        u = (2 * i + half) * BLOCKS + k
        return trecv[inv_s[1, lax.div(u, COLT), lax.rem(u, COLT)]].astype(F32)

    def add_heads(i, _):
        for k in range(BLOCKS):
            mask = live(i, k)
            for half in range(2):
                at = rows_at(k * ROWS + i * PAIR + half * TR, HEAD, 8)
                keep = mask[half * TR : half * TR + HEAD]
                base[at, :] += jnp.where(keep, tile_back(trecv_a, i, half, k), 0.0)
        return 0

    def finish(i, _):
        at = rows_at(i * PAIR, PAIR, 16)
        for k in range(BLOCKS):
            mask = live(i, k)
            pieces = []
            for half in range(2):
                start = k * ROWS + i * PAIR + half * TR
                keep = mask[half * TR + HEAD : (half + 1) * TR]
                pieces.append(base[rows_at(start, HEAD, 8), :])
                pieces.append(
                    base[rows_at(start + HEAD, REST, 8), :]
                    + jnp.where(keep, tile_back(trecv_b, i, half, k), 0.0)
                )
            flow_out[0, at, pl.ds(k * COLT, COLT)] = jnp.concatenate(pieces, axis=0).astype(BF16)
        return 0

    homes[0].wait()
    all_back[0].wait_recv()
    lax.fori_loop(0, PAIRS, add_heads, 0)
    homes[1].wait()
    all_back[1].wait_recv()
    lax.fori_loop(0, PAIRS, finish, 0)

    pltpu.make_async_remote_copy(
        sbuf.at[others], near.at[others], send_sem, recv_sem.at[0],
        device_id={"row": other}, device_id_type=MESH,
    ).wait_send()
    all_handed.wait_send()
    for n in range(2):
        all_back[n].wait_send()


def write_out(new, flow, new_out, flow_out, sem):
    copies = []
    for n, (src, dst) in enumerate(((new, new_out), (flow, flow_out))):
        for part in range(LOADS):
            at = pl.ds(part * (ROWS // LOADS), ROWS // LOADS)
            copies.append(pltpu.make_async_copy(src.at[0, at], dst.at[0, at], sem.at[n, part]))
    for copy in copies:
        copy.start()
    for copy in copies:
        copy.wait()


def per_device(gen, mag, ham, slot, dims, pp, cc, send, recv, weight):
    args = (gen, mag, ham, slot, dims, pp, cc, send.transpose(2, 0, 1), recv, weight)
    hbm = pl.BlockSpec(memory_space=pltpu.HBM)
    vmem = pl.BlockSpec(memory_space=pltpu.VMEM)
    dma = pltpu.SemaphoreType.DMA
    held = pl.pallas_call(
        kernel,
        out_shape=(pltpu.VMEM(gen.shape, BF16),) * 2,
        in_specs=[hbm] * 3 + [pl.BlockSpec(memory_space=pltpu.SMEM)] + [hbm] * 6,
        out_specs=(vmem, vmem),
        scratch_shapes=[
            pltpu.SMEM(dims.shape, jnp.int32),
            pltpu.VMEM(pp.shape, F32),
            pltpu.VMEM(cc.shape, F32),
            pltpu.SMEM(args[7].shape, jnp.int32),
            pltpu.SMEM(recv.shape, jnp.int32),
            pltpu.SMEM(weight.shape, F32),
            dma((6,)),
            pltpu.VMEM((ROWS, WIDTH), BF16),
            pltpu.VMEM((ROWS, WIDTH), BF16),
            pltpu.VMEM((ROWS, WIDTH), BF16),
            pltpu.VMEM((TILES, PAIR, COLT), BF16),
            pltpu.VMEM((PEERS * SLOTS, PAIR, COLT), BF16),
            pltpu.VMEM((PEERS * SLOTS, PAIR, COLT), BF16),
            pltpu.VMEM((PEERS * SLOTS, PAIR, COLT), BF16),
            pltpu.VMEM((2 * WIDTH, WIDTH), BF16),
            pltpu.VMEM((ROWS, 2 * WIDTH), BF16),
            pltpu.VMEM((BLOCKS * ROWS, COLT), F32),
            pltpu.VMEM((TILES, HEAD, COLT), F32),
            pltpu.VMEM((TILES, REST, COLT), F32),
            pltpu.VMEM((PEERS * SLOTS, HEAD, COLT), BF16),
            pltpu.VMEM((PEERS * SLOTS, REST, COLT), BF16),
            pltpu.VMEM((PEERS * SLOTS, HEAD, COLT), BF16),
            pltpu.VMEM((PEERS * SLOTS, REST, COLT), BF16),
            pltpu.VMEM((2, 8, COLT), jnp.int32),
            pltpu.SMEM((2, 8, COLT), jnp.int32),
            dma((3, LOADS)),
            dma,
            dma,
            dma,
            dma((PEERS,)),
            dma,
            dma,
            dma((2,)),
            dma((2,)),
            dma((2,)),
            dma((2,)),
            dma((2,)),
        ],
        compiler_params=pltpu.CompilerParams(
            collective_id=0, has_side_effects=True, vmem_limit_bytes=54 << 20
        ),
    )(*args)
    strip = jax.ShapeDtypeStruct(gen.shape, BF16)
    return pl.pallas_call(
        write_out,
        out_shape=(strip, strip),
        in_specs=[vmem, vmem],
        out_specs=(hbm, hbm),
        scratch_shapes=[dma((2, LOADS))],
        compiler_params=pltpu.CompilerParams(vmem_limit_bytes=6 << 20),
    )(*held)


def solution(mesh):
    return jax.shard_map(
        per_device,
        mesh=mesh,
        in_specs=(
            P("chan", "row", None),
            P("chan", "row", None),
            P("chan", "row", None),
            P("chan"),
            P(),
            P(),
            P("chan", None),
            P("chan", None, None),
            P("chan", None),
            P("chan", None),
        ),
        out_specs=(P("chan", "row", None), P("chan", "row", None)),
        check_vma=False,
    )
```

```python
import functools

import jax
import jax.numpy as jnp
from jax import lax
from jax.experimental import pallas as pl
from jax.experimental.pallas import tpu as pltpu
from jax.sharding import PartitionSpec as P

TR = 40
COLT = 128
SLOTS = 3
STEP_SIZE = 0.5
PEERS = 64
MULT = 37
MESH = pl.DeviceIdType.MESH
F32 = jnp.float32
BF16 = jnp.bfloat16

ROWS = 640
WIDTH = 1280
BLOCKS = WIDTH // COLT
PAIRS = ROWS // (2 * TR)
TILES = (ROWS // TR) * BLOCKS
HEAD = 16
REST = TR - HEAD
LOADS = 4
PAIR = 2 * TR


def spin(me, step, sign):
    off = step * MULT % PEERS
    x = lax.rem(lax.rem(me, 4) + (4 + sign * (off % 4)), 4)
    y = lax.rem(lax.rem(lax.div(me, 4), 4) + (4 + sign * (off // 4 % 4)), 4)
    z = lax.rem(lax.div(me, 16) + (4 + sign * (off // 16)), 4)
    return (z * 4 + y) * 4 + x


def rows_at(start, size, unit):
    return pl.ds(pl.multiple_of(start, unit), size)


def kernel(
    gen, mag, ham, slot_ref, dims_in, pp_in, cc_in, send_in, recv_in, weight_in,
    new_out, flow_out,
    dims_ref, pp_v, cc_ref, send_ref, recv_ref, weight_ref, small_sem,
    gen_v, mag_v, ham_v, stack, sbuf, near, far, right, left, base, cross_a, cross_b, tsend_a, tsend_b, trecv_a, trecv_b,
    inv_v, inv_s,
    in_sem, inv_sem, self_sem, send_sem, recv_sem, hand_sem, take_sem,
    strip_send, strip_recv, bsend_sem, brecv_sem, bself_sem,
):
    me = lax.axis_index("chan")
    row = lax.axis_index("row")
    other = 1 - row

    def load(part, start):
        for n, (src, dst) in enumerate(((gen, gen_v), (mag, mag_v), (ham, ham_v))):
            at = rows_at(part * (ROWS // LOADS), ROWS // LOADS, 16)
            copy = pltpu.make_async_copy(src.at[0, at], dst.at[at], in_sem.at[n, part])
            copy.start() if start else copy.wait()

    for part in range(LOADS):
        load(part, True)
    small = [
        pltpu.make_async_copy(src, dst, small_sem.at[n])
        for n, (src, dst) in enumerate(
            (
                (dims_in, dims_ref),
                (send_in, send_ref),
                (recv_in, recv_ref),
                (weight_in, weight_ref),
                (cc_in, cc_ref),
                (pp_in, pp_v),
            )
        )
    ]
    for copy in small:
        copy.start()
    barrier = pltpu.get_barrier_semaphore()

    def greet(step, _):
        pl.semaphore_signal(
            barrier, inc=1, device_id={"chan": lax.rem(me + step, PEERS)}, device_id_type=MESH
        )
        return 0

    lax.fori_loop(1, PEERS, greet, 0)
    pl.semaphore_signal(barrier, inc=1, device_id={"row": other}, device_id_type=MESH)

    for copy in small[:2]:
        copy.wait()
    limit = dims_ref[slot_ref[0]]

    def live(i, k):
        row_ids = row * ROWS + i * PAIR + lax.broadcasted_iota(jnp.int32, (PAIR, COLT), 0)
        col_ids = k * COLT + lax.broadcasted_iota(jnp.int32, (1, COLT), 1)
        return row_ids < jnp.where(col_ids < limit, limit, 0)

    def cut(i):
        at = rows_at(i * PAIR, PAIR, 16)
        for k in range(BLOCKS):
            col = pl.ds(k * COLT, COLT)
            new = (mag_v[at, col].astype(F32) + STEP_SIZE * gen_v[at, col].astype(F32)).astype(BF16)
            new_out[0, at, col] = new
            mask = live(i, k)
            m = jnp.where(mask, new.astype(F32), 0.0)
            h = jnp.where(mask, ham_v[at, col].astype(F32), 0.0)
            for top in (0, TR):
                stack[(2 * i + top // TR) * BLOCKS + k] = jnp.concatenate(
                    [m[top : top + TR], h[top : top + TR]], axis=0
                ).astype(BF16)

    def prologue(part, _):
        load(part, False)
        for sub in range(PAIRS // LOADS):
            cut(part * (PAIRS // LOADS) + sub)
        return 0

    lax.fori_loop(0, LOADS, prologue, 0)
    pl.semaphore_wait(barrier, PEERS)

    def pick(to):
        for l in range(SLOTS):
            tile = jnp.minimum(send_ref[l, 0, to], TILES - 1)
            sbuf[to * SLOTS + l] = stack[tile]

    def message(step):
        to = spin(me, step, 1)
        return pltpu.make_async_remote_copy(
            sbuf.at[pl.ds(to * SLOTS, SLOTS)],
            near.at[pl.ds(me * SLOTS, SLOTS)],
            send_sem,
            recv_sem.at[step],
            device_id={"chan": to},
            device_id_type=MESH,
        )

    def arrival(step):
        fr = spin(me, step, -1)
        return pltpu.make_async_remote_copy(
            sbuf.at[pl.ds(fr * SLOTS, SLOTS)],
            near.at[pl.ds(fr * SLOTS, SLOTS)],
            send_sem,
            recv_sem.at[step],
            device_id={"chan": fr},
            device_id_type=MESH,
        )

    def handed(step):
        at = pl.ds(spin(me, step, -1) * SLOTS, SLOTS)
        return pltpu.make_async_remote_copy(
            near.at[at], far.at[at], hand_sem, take_sem,
            device_id={"row": other}, device_id_type=MESH,
        )

    def send_out(step):
        pick(spin(me, step, 1))
        message(step).start()

    for step in range(1, PEERS):
        send_out(step)
    pick(me)
    mine = pltpu.make_async_copy(
        sbuf.at[pl.ds(me * SLOTS, SLOTS)], near.at[pl.ds(me * SLOTS, SLOTS)], self_sem
    )
    mine.start()

    for copy in small[2:]:
        copy.wait()
    chosen = lax.broadcasted_iota(jnp.int32, pp_v.shape, 0) == slot_ref[0]
    factor = jnp.sum(jnp.where(chosen, pp_v[...], 0.0), axis=0, keepdims=True)

    def strips(i, _):
        at = rows_at(i * PAIR, PAIR, 16)
        for k in range(BLOCKS):
            col = pl.ds(k * COLT, COLT)
            mask = live(i, k)
            m = jnp.where(mask, new_out[0, at, col].astype(F32), 0.0)
            h = jnp.where(mask, ham_v[at, col].astype(F32), 0.0)
            f = factor[:, k * COLT : (k + 1) * COLT]
            right[rows_at(row * ROWS + i * PAIR, PAIR, 16), col] = h.astype(BF16)
            right[rows_at(WIDTH + row * ROWS + i * PAIR, PAIR, 16), col] = m.astype(BF16)
            left[at, col] = (m * f).astype(BF16)
            left[at, pl.ds(WIDTH + k * COLT, COLT)] = (h * -f).astype(BF16)
            base[rows_at(k * ROWS + i * PAIR, PAIR, 8), :] = h
        return 0

    lax.fori_loop(0, PAIRS, strips, 0)

    def strip(which, r):
        at = rows_at(which * WIDTH + r * ROWS, ROWS, 16)
        return pltpu.make_async_remote_copy(
            right.at[at], right.at[at], strip_send.at[which], strip_recv.at[which],
            device_id={"row": other}, device_id_type=MESH,
        )

    for which in range(2):
        strip(which, row).start()
    mine.wait()
    handed(0).start()

    place = lax.broadcasted_iota(jnp.int32, (8, COLT), 0) * COLT + lax.broadcasted_iota(
        jnp.int32, (8, COLT), 1
    )

    def invert_recv(v, table):
        return jnp.where(place == recv_ref[0, v], v, table)

    def invert_send(d, table):
        for l in range(SLOTS):
            table = jnp.where(place == send_ref[l, 0, d], d * SLOTS + l, table)
        return table

    blank = jnp.zeros((8, COLT), jnp.int32)
    inv_v[0] = lax.fori_loop(0, TILES, invert_recv, blank)
    inv_v[1] = lax.fori_loop(0, PEERS, invert_send, blank)
    inv_copy = pltpu.make_async_copy(inv_v, inv_s, inv_sem)
    inv_copy.start()

    for which in range(2):
        strip(which, other).wait_recv()
        strip(which, row).wait_send()

    part = jnp.dot(left[...], right[...], preferred_element_type=F32)
    for k in range(BLOCKS):
        base[pl.ds(k * ROWS, ROWS), :] += part[:, k * COLT : (k + 1) * COLT]
    inv_copy.wait()

    def hand_on(step):
        arrival(step).wait_recv()
        handed(step).start()

    for step in range(1, PEERS):
        hand_on(step)

    def settle(tiles, r, own):
        def body(i, _):
            at = rows_at(r * ROWS + i * PAIR, PAIR, 16)
            under = rows_at(WIDTH + r * ROWS + i * PAIR, PAIR, 16)
            for k in range(BLOCKS):
                col = pl.ds(k * COLT, COLT)
                parts = []
                for half in range(2):
                    v = (2 * i + half) * BLOCKS + k
                    tile = tiles[recv_ref[0, v]]
                    parts.append(weight_ref[0, v] * tile.astype(F32))
                m = jnp.concatenate([parts[0][:TR], parts[1][:TR]], axis=0)
                h = jnp.concatenate([parts[0][TR:], parts[1][TR:]], axis=0)
                right[at, col] = h.astype(BF16)
                right[under, col] = m.astype(BF16)
                if own:
                    f = cc_ref[:, k * COLT : (k + 1) * COLT]
                    first = rows_at(i * 2 * HEAD, 2 * HEAD, 16)
                    second = rows_at(ROWS // TR * HEAD + i * 2 * REST, 2 * REST, 16)
                    for value, place in ((m * f, k * COLT), (h * -f, WIDTH + k * COLT)):
                        side = pl.ds(place, COLT)
                        left[first, side] = jnp.concatenate(
                            [value[:HEAD], value[TR : TR + HEAD]], axis=0
                        ).astype(BF16)
                        left[second, side] = jnp.concatenate(
                            [value[HEAD:TR], value[TR + HEAD :]], axis=0
                        ).astype(BF16)
            return 0

        lax.fori_loop(0, PAIRS, body, 0)

    settle(near, row, True)

    all_handed = pltpu.make_async_remote_copy(
        near, far, hand_sem, take_sem, device_id={"row": other}, device_id_type=MESH
    )
    all_handed.wait_recv()
    settle(far, other, False)

    def product(start, size, cross):
        rows = left[start : start + size * (ROWS // TR), :]
        part = jnp.dot(rows, right[...], preferred_element_type=F32)
        for a in range(ROWS // TR):
            for k in range(BLOCKS):
                cross[a * BLOCKS + k] = part[a * size : (a + 1) * size, k * COLT : (k + 1) * COLT]

    def pick_back(to, cross, tsend):
        for l in range(SLOTS):
            slot = to * SLOTS + l
            v = inv_s[0, lax.div(slot, COLT), lax.rem(slot, COLT)]
            tsend[slot] = (weight_ref[0, v] * cross[v]).astype(BF16)

    mine_at = pl.ds(me * SLOTS, SLOTS)
    parts_back = ((0, HEAD, cross_a, tsend_a, trecv_a), (ROWS // TR * HEAD, REST, cross_b, tsend_b, trecv_b))
    homes = []
    for n, (start, size, cross, tsend, trecv) in enumerate(parts_back):
        product(start, size, cross)

        def send_back(step):
            to = spin(me, step, 1)
            pick_back(to, cross, tsend)
            pltpu.make_async_remote_copy(
                tsend.at[pl.ds(to * SLOTS, SLOTS)], trecv.at[mine_at], bsend_sem.at[n], brecv_sem.at[n],
                device_id={"chan": to}, device_id_type=MESH,
            ).start()

        for step in range(1, PEERS):
            send_back(step)
        pick_back(me, cross, tsend)
        homes.append(pltpu.make_async_copy(tsend.at[mine_at], trecv.at[mine_at], bself_sem.at[n]))
        homes[n].start()

    others = pl.ds(0, (PEERS - 1) * SLOTS)
    all_back = [
        pltpu.make_async_remote_copy(
            tsend.at[others], trecv.at[others], bsend_sem.at[n], brecv_sem.at[n],
            device_id={"row": other}, device_id_type=MESH,
        )
        for n, (_, _, _, tsend, trecv) in enumerate(parts_back)
    ]
    def tile_back(trecv, i, half, k):
        u = (2 * i + half) * BLOCKS + k
        return trecv[inv_s[1, lax.div(u, COLT), lax.rem(u, COLT)]].astype(F32)

    def add_heads(i, _):
        for k in range(BLOCKS):
            mask = live(i, k)
            for half in range(2):
                at = rows_at(k * ROWS + i * PAIR + half * TR, HEAD, 8)
                keep = mask[half * TR : half * TR + HEAD]
                base[at, :] += jnp.where(keep, tile_back(trecv_a, i, half, k), 0.0)
        return 0

    def finish(i, _):
        at = rows_at(i * PAIR, PAIR, 16)
        for k in range(BLOCKS):
            mask = live(i, k)
            pieces = []
            for half in range(2):
                start = k * ROWS + i * PAIR + half * TR
                keep = mask[half * TR + HEAD : (half + 1) * TR]
                pieces.append(base[rows_at(start, HEAD, 8), :])
                pieces.append(
                    base[rows_at(start + HEAD, REST, 8), :]
                    + jnp.where(keep, tile_back(trecv_b, i, half, k), 0.0)
                )
            flow_out[0, at, pl.ds(k * COLT, COLT)] = jnp.concatenate(pieces, axis=0).astype(BF16)
        return 0

    homes[0].wait()
    all_back[0].wait_recv()
    lax.fori_loop(0, PAIRS, add_heads, 0)
    homes[1].wait()
    all_back[1].wait_recv()
    lax.fori_loop(0, PAIRS, finish, 0)

    pltpu.make_async_remote_copy(
        sbuf.at[others], near.at[others], send_sem, recv_sem.at[0],
        device_id={"row": other}, device_id_type=MESH,
    ).wait_send()
    all_handed.wait_send()
    for n in range(2):
        all_back[n].wait_send()


def write_out(new, flow, new_out, flow_out, sem):
    copies = []
    for n, (src, dst) in enumerate(((new, new_out), (flow, flow_out))):
        for part in range(LOADS):
            at = pl.ds(part * (ROWS // LOADS), ROWS // LOADS)
            copies.append(pltpu.make_async_copy(src.at[0, at], dst.at[0, at], sem.at[n, part]))
    for copy in copies:
        copy.start()
    for copy in copies:
        copy.wait()


def per_device(gen, mag, ham, slot, dims, pp, cc, send, recv, weight):
    args = (gen, mag, ham, slot, dims, pp, cc, send.transpose(2, 0, 1), recv, weight)
    hbm = pl.BlockSpec(memory_space=pltpu.HBM)
    vmem = pl.BlockSpec(memory_space=pltpu.VMEM)
    dma = pltpu.SemaphoreType.DMA
    held = pl.pallas_call(
        kernel,
        out_shape=(pltpu.VMEM(gen.shape, BF16),) * 2,
        in_specs=[hbm] * 3 + [pl.BlockSpec(memory_space=pltpu.SMEM)] + [hbm] * 6,
        out_specs=(vmem, vmem),
        scratch_shapes=[
            pltpu.SMEM(dims.shape, jnp.int32),
            pltpu.VMEM(pp.shape, F32),
            pltpu.VMEM(cc.shape, F32),
            pltpu.SMEM(args[7].shape, jnp.int32),
            pltpu.SMEM(recv.shape, jnp.int32),
            pltpu.SMEM(weight.shape, F32),
            dma((6,)),
            pltpu.VMEM((ROWS, WIDTH), BF16),
            pltpu.VMEM((ROWS, WIDTH), BF16),
            pltpu.VMEM((ROWS, WIDTH), BF16),
            pltpu.VMEM((TILES, PAIR, COLT), BF16),
            pltpu.VMEM((PEERS * SLOTS, PAIR, COLT), BF16),
            pltpu.VMEM((PEERS * SLOTS, PAIR, COLT), BF16),
            pltpu.VMEM((PEERS * SLOTS, PAIR, COLT), BF16),
            pltpu.VMEM((2 * WIDTH, WIDTH), BF16),
            pltpu.VMEM((ROWS, 2 * WIDTH), BF16),
            pltpu.VMEM((BLOCKS * ROWS, COLT), F32),
            pltpu.VMEM((TILES, HEAD, COLT), F32),
            pltpu.VMEM((TILES, REST, COLT), F32),
            pltpu.VMEM((PEERS * SLOTS, HEAD, COLT), BF16),
            pltpu.VMEM((PEERS * SLOTS, REST, COLT), BF16),
            pltpu.VMEM((PEERS * SLOTS, HEAD, COLT), BF16),
            pltpu.VMEM((PEERS * SLOTS, REST, COLT), BF16),
            pltpu.VMEM((2, 8, COLT), jnp.int32),
            pltpu.SMEM((2, 8, COLT), jnp.int32),
            dma((3, LOADS)),
            dma,
            dma,
            dma,
            dma((PEERS,)),
            dma,
            dma,
            dma((2,)),
            dma((2,)),
            dma((2,)),
            dma((2,)),
            dma((2,)),
        ],
        compiler_params=pltpu.CompilerParams(
            collective_id=0, has_side_effects=True, vmem_limit_bytes=54 << 20
        ),
    )(*args)
    strip = jax.ShapeDtypeStruct(gen.shape, BF16)
    return pl.pallas_call(
        write_out,
        out_shape=(strip, strip),
        in_specs=[vmem, vmem],
        out_specs=(hbm, hbm),
        scratch_shapes=[dma((2, LOADS))],
        compiler_params=pltpu.CompilerParams(vmem_limit_bytes=6 << 20),
    )(*held)


def solution(mesh):
    return jax.shard_map(
        per_device,
        mesh=mesh,
        in_specs=(
            P("chan", "row", None),
            P("chan", "row", None),
            P("chan", "row", None),
            P("chan"),
            P(),
            P(),
            P("chan", None),
            P("chan", None, None),
            P("chan", None),
            P("chan", None),
        ),
        out_specs=(P("chan", "row", None), P("chan", "row", None)),
        check_vma=False,
    )
```

```python
import functools

import jax
import jax.numpy as jnp
from jax import lax
from jax.experimental import pallas as pl
from jax.experimental.pallas import tpu as pltpu
from jax.sharding import PartitionSpec as P

TR = 40
COLT = 128
SLOTS = 3
STEP_SIZE = 0.5
PEERS = 64
MULT = 37
MESH = pl.DeviceIdType.MESH
F32 = jnp.float32
BF16 = jnp.bfloat16

ROWS = 640
WIDTH = 1280
BLOCKS = WIDTH // COLT
PAIRS = ROWS // (2 * TR)
TILES = (ROWS // TR) * BLOCKS
HEAD = 16
REST = TR - HEAD
LOADS = 4
PAIR = 2 * TR


def spin(me, step, sign):
    off = step * MULT % PEERS
    x = lax.rem(lax.rem(me, 4) + (4 + sign * (off % 4)), 4)
    y = lax.rem(lax.rem(lax.div(me, 4), 4) + (4 + sign * (off // 4 % 4)), 4)
    z = lax.rem(lax.div(me, 16) + (4 + sign * (off // 16)), 4)
    return (z * 4 + y) * 4 + x


def rows_at(start, size, unit):
    return pl.ds(pl.multiple_of(start, unit), size)


def kernel(
    gen, mag, ham, slot_ref, dims_in, pp_in, cc_in, send_in, recv_in, weight_in,
    new_out, flow_out,
    dims_ref, pp_v, cc_ref, send_ref, recv_ref, weight_ref, small_sem,
    gen_v, mag_v, ham_v, stack, sbuf, near, far, right, left, base, cross_a, cross_b, tsend_a, tsend_b, trecv_a, trecv_b,
    inv_v, inv_s,
    in_sem, inv_sem, self_sem, send_sem, recv_sem, hand_sem, take_sem,
    strip_send, strip_recv, bsend_sem, brecv_sem, bself_sem,
):
    me = lax.axis_index("chan")
    row = lax.axis_index("row")
    other = 1 - row

    def load(part, start):
        for n, (src, dst) in enumerate(((gen, gen_v), (mag, mag_v), (ham, ham_v))):
            at = rows_at(part * (ROWS // LOADS), ROWS // LOADS, 16)
            copy = pltpu.make_async_copy(src.at[0, at], dst.at[at], in_sem.at[n, part])
            copy.start() if start else copy.wait()

    small = [
        pltpu.make_async_copy(src, dst, small_sem.at[n])
        for n, (src, dst) in enumerate(
            (
                (dims_in, dims_ref),
                (send_in, send_ref),
                (recv_in, recv_ref),
                (weight_in, weight_ref),
                (cc_in, cc_ref),
                (pp_in, pp_v),
            )
        )
    ]
    load(0, True)
    barrier = pltpu.get_barrier_semaphore()
    pl.semaphore_signal(barrier, inc=1, device_id={"row": other}, device_id_type=MESH)
    for step in range(1, PEERS):
        pl.semaphore_signal(
            barrier, inc=1, device_id={"chan": lax.rem(me + step, PEERS)}, device_id_type=MESH
        )
    for copy in small[:2]:
        copy.start()
    for part in range(1, LOADS):
        load(part, True)
    for copy in small[2:]:
        copy.start()

    for copy in small[:2]:
        copy.wait()
    limit = dims_ref[slot_ref[0]]

    def live(i, k):
        row_ids = row * ROWS + i * PAIR + lax.broadcasted_iota(jnp.int32, (PAIR, COLT), 0)
        col_ids = k * COLT + lax.broadcasted_iota(jnp.int32, (1, COLT), 1)
        return row_ids < jnp.where(col_ids < limit, limit, 0)

    def cut(i):
        at = rows_at(i * PAIR, PAIR, 16)
        for k in range(BLOCKS):
            col = pl.ds(k * COLT, COLT)
            new = (mag_v[at, col].astype(F32) + STEP_SIZE * gen_v[at, col].astype(F32)).astype(BF16)
            new_out[0, at, col] = new
            mask = live(i, k)
            m = jnp.where(mask, new.astype(F32), 0.0)
            h = jnp.where(mask, ham_v[at, col].astype(F32), 0.0)
            for top in (0, TR):
                stack[(2 * i + top // TR) * BLOCKS + k] = jnp.concatenate(
                    [m[top : top + TR], h[top : top + TR]], axis=0
                ).astype(BF16)

    def prologue(part, _):
        load(part, False)
        for sub in range(PAIRS // LOADS):
            cut(part * (PAIRS // LOADS) + sub)
        return 0

    lax.fori_loop(0, LOADS, prologue, 0)
    pl.semaphore_wait(barrier, PEERS)

    def pick(to):
        for l in range(SLOTS):
            tile = jnp.minimum(send_ref[l, 0, to], TILES - 1)
            sbuf[to * SLOTS + l] = stack[tile]

    def message(step):
        to = spin(me, step, 1)
        return pltpu.make_async_remote_copy(
            sbuf.at[pl.ds(to * SLOTS, SLOTS)],
            near.at[pl.ds(me * SLOTS, SLOTS)],
            send_sem,
            recv_sem.at[step],
            device_id={"chan": to},
            device_id_type=MESH,
        )

    def arrival(step):
        fr = spin(me, step, -1)
        return pltpu.make_async_remote_copy(
            sbuf.at[pl.ds(fr * SLOTS, SLOTS)],
            near.at[pl.ds(fr * SLOTS, SLOTS)],
            send_sem,
            recv_sem.at[step],
            device_id={"chan": fr},
            device_id_type=MESH,
        )

    def handed(step):
        at = pl.ds(spin(me, step, -1) * SLOTS, SLOTS)
        return pltpu.make_async_remote_copy(
            near.at[at], far.at[at], hand_sem, take_sem,
            device_id={"row": other}, device_id_type=MESH,
        )

    def send_out(step):
        pick(spin(me, step, 1))
        message(step).start()

    for step in range(1, PEERS):
        send_out(step)
    pick(me)
    mine = pltpu.make_async_copy(
        sbuf.at[pl.ds(me * SLOTS, SLOTS)], near.at[pl.ds(me * SLOTS, SLOTS)], self_sem
    )
    mine.start()

    for copy in small[2:]:
        copy.wait()
    chosen = lax.broadcasted_iota(jnp.int32, pp_v.shape, 0) == slot_ref[0]
    factor = jnp.sum(jnp.where(chosen, pp_v[...], 0.0), axis=0, keepdims=True)

    def strips(i, _):
        at = rows_at(i * PAIR, PAIR, 16)
        for k in range(BLOCKS):
            col = pl.ds(k * COLT, COLT)
            mask = live(i, k)
            m = jnp.where(mask, new_out[0, at, col].astype(F32), 0.0)
            h = jnp.where(mask, ham_v[at, col].astype(F32), 0.0)
            f = factor[:, k * COLT : (k + 1) * COLT]
            right[rows_at(row * ROWS + i * PAIR, PAIR, 16), col] = h.astype(BF16)
            right[rows_at(WIDTH + row * ROWS + i * PAIR, PAIR, 16), col] = m.astype(BF16)
            left[at, col] = (m * f).astype(BF16)
            left[at, pl.ds(WIDTH + k * COLT, COLT)] = (h * -f).astype(BF16)
            base[rows_at(k * ROWS + i * PAIR, PAIR, 8), :] = h
        return 0

    lax.fori_loop(0, PAIRS, strips, 0)

    def strip(which, r):
        at = rows_at(which * WIDTH + r * ROWS, ROWS, 16)
        return pltpu.make_async_remote_copy(
            right.at[at], right.at[at], strip_send.at[which], strip_recv.at[which],
            device_id={"row": other}, device_id_type=MESH,
        )

    for which in range(2):
        strip(which, row).start()
    mine.wait()
    handed(0).start()

    place = lax.broadcasted_iota(jnp.int32, (8, COLT), 0) * COLT + lax.broadcasted_iota(
        jnp.int32, (8, COLT), 1
    )

    def invert_recv(v, table):
        return jnp.where(place == recv_ref[0, v], v, table)

    def invert_send(d, table):
        for l in range(SLOTS):
            table = jnp.where(place == send_ref[l, 0, d], d * SLOTS + l, table)
        return table

    blank = jnp.zeros((8, COLT), jnp.int32)
    inv_v[0] = lax.fori_loop(0, TILES, invert_recv, blank)
    inv_v[1] = lax.fori_loop(0, PEERS, invert_send, blank)
    inv_copy = pltpu.make_async_copy(inv_v, inv_s, inv_sem)
    inv_copy.start()

    for which in range(2):
        strip(which, other).wait_recv()
        strip(which, row).wait_send()

    part = jnp.dot(left[...], right[...], preferred_element_type=F32)
    for k in range(BLOCKS):
        base[pl.ds(k * ROWS, ROWS), :] += part[:, k * COLT : (k + 1) * COLT]
    inv_copy.wait()

    def hand_on(step):
        arrival(step).wait_recv()
        handed(step).start()

    for step in range(1, PEERS):
        hand_on(step)

    def settle(tiles, r, own):
        def body(i, _):
            at = rows_at(r * ROWS + i * PAIR, PAIR, 16)
            under = rows_at(WIDTH + r * ROWS + i * PAIR, PAIR, 16)
            for k in range(BLOCKS):
                col = pl.ds(k * COLT, COLT)
                parts = []
                for half in range(2):
                    v = (2 * i + half) * BLOCKS + k
                    tile = tiles[recv_ref[0, v]]
                    parts.append(weight_ref[0, v] * tile.astype(F32))
                m = jnp.concatenate([parts[0][:TR], parts[1][:TR]], axis=0)
                h = jnp.concatenate([parts[0][TR:], parts[1][TR:]], axis=0)
                right[at, col] = h.astype(BF16)
                right[under, col] = m.astype(BF16)
                if own:
                    f = cc_ref[:, k * COLT : (k + 1) * COLT]
                    first = rows_at(i * 2 * HEAD, 2 * HEAD, 16)
                    second = rows_at(ROWS // TR * HEAD + i * 2 * REST, 2 * REST, 16)
                    for value, place in ((m * f, k * COLT), (h * -f, WIDTH + k * COLT)):
                        side = pl.ds(place, COLT)
                        left[first, side] = jnp.concatenate(
                            [value[:HEAD], value[TR : TR + HEAD]], axis=0
                        ).astype(BF16)
                        left[second, side] = jnp.concatenate(
                            [value[HEAD:TR], value[TR + HEAD :]], axis=0
                        ).astype(BF16)
            return 0

        lax.fori_loop(0, PAIRS, body, 0)

    settle(near, row, True)

    all_handed = pltpu.make_async_remote_copy(
        near, far, hand_sem, take_sem, device_id={"row": other}, device_id_type=MESH
    )
    all_handed.wait_recv()
    settle(far, other, False)

    def product(start, size, cross):
        rows = left[start : start + size * (ROWS // TR), :]
        part = jnp.dot(rows, right[...], preferred_element_type=F32)
        for a in range(ROWS // TR):
            for k in range(BLOCKS):
                cross[a * BLOCKS + k] = part[a * size : (a + 1) * size, k * COLT : (k + 1) * COLT]

    def pick_back(to, cross, tsend):
        for l in range(SLOTS):
            slot = to * SLOTS + l
            v = inv_s[0, lax.div(slot, COLT), lax.rem(slot, COLT)]
            tsend[slot] = (weight_ref[0, v] * cross[v]).astype(BF16)

    mine_at = pl.ds(me * SLOTS, SLOTS)
    parts_back = ((0, HEAD, cross_a, tsend_a, trecv_a), (ROWS // TR * HEAD, REST, cross_b, tsend_b, trecv_b))
    homes = []
    for n, (start, size, cross, tsend, trecv) in enumerate(parts_back):
        product(start, size, cross)

        def send_back(step):
            to = spin(me, step, 1)
            pick_back(to, cross, tsend)
            pltpu.make_async_remote_copy(
                tsend.at[pl.ds(to * SLOTS, SLOTS)], trecv.at[mine_at], bsend_sem.at[n], brecv_sem.at[n],
                device_id={"chan": to}, device_id_type=MESH,
            ).start()

        for step in range(1, PEERS):
            send_back(step)
        pick_back(me, cross, tsend)
        homes.append(pltpu.make_async_copy(tsend.at[mine_at], trecv.at[mine_at], bself_sem.at[n]))
        homes[n].start()

    others = pl.ds(0, (PEERS - 1) * SLOTS)
    all_back = [
        pltpu.make_async_remote_copy(
            tsend.at[others], trecv.at[others], bsend_sem.at[n], brecv_sem.at[n],
            device_id={"row": other}, device_id_type=MESH,
        )
        for n, (_, _, _, tsend, trecv) in enumerate(parts_back)
    ]
    def tile_back(trecv, i, half, k):
        u = (2 * i + half) * BLOCKS + k
        return trecv[inv_s[1, lax.div(u, COLT), lax.rem(u, COLT)]].astype(F32)

    def add_heads(i, _):
        for k in range(BLOCKS):
            mask = live(i, k)
            for half in range(2):
                at = rows_at(k * ROWS + i * PAIR + half * TR, HEAD, 8)
                keep = mask[half * TR : half * TR + HEAD]
                base[at, :] += jnp.where(keep, tile_back(trecv_a, i, half, k), 0.0)
        return 0

    def finish(i, _):
        at = rows_at(i * PAIR, PAIR, 16)
        for k in range(BLOCKS):
            mask = live(i, k)
            pieces = []
            for half in range(2):
                start = k * ROWS + i * PAIR + half * TR
                keep = mask[half * TR + HEAD : (half + 1) * TR]
                pieces.append(base[rows_at(start, HEAD, 8), :])
                pieces.append(
                    base[rows_at(start + HEAD, REST, 8), :]
                    + jnp.where(keep, tile_back(trecv_b, i, half, k), 0.0)
                )
            flow_out[0, at, pl.ds(k * COLT, COLT)] = jnp.concatenate(pieces, axis=0).astype(BF16)
        return 0

    homes[0].wait()
    all_back[0].wait_recv()
    lax.fori_loop(0, PAIRS, add_heads, 0)
    homes[1].wait()
    all_back[1].wait_recv()
    lax.fori_loop(0, PAIRS, finish, 0)

    pltpu.make_async_remote_copy(
        sbuf.at[others], near.at[others], send_sem, recv_sem.at[0],
        device_id={"row": other}, device_id_type=MESH,
    ).wait_send()
    all_handed.wait_send()
    for n in range(2):
        all_back[n].wait_send()


def write_out(new, flow, new_out, flow_out, sem):
    copies = []
    for n, (src, dst) in enumerate(((new, new_out), (flow, flow_out))):
        for part in range(LOADS):
            at = pl.ds(part * (ROWS // LOADS), ROWS // LOADS)
            copies.append(pltpu.make_async_copy(src.at[0, at], dst.at[0, at], sem.at[n, part]))
    for copy in copies:
        copy.start()
    for copy in copies:
        copy.wait()


def per_device(gen, mag, ham, slot, dims, pp, cc, send, recv, weight):
    args = (gen, mag, ham, slot, dims, pp, cc, send.transpose(2, 0, 1), recv, weight)
    hbm = pl.BlockSpec(memory_space=pltpu.HBM)
    vmem = pl.BlockSpec(memory_space=pltpu.VMEM)
    dma = pltpu.SemaphoreType.DMA
    held = pl.pallas_call(
        kernel,
        out_shape=(pltpu.VMEM(gen.shape, BF16),) * 2,
        in_specs=[hbm] * 3 + [pl.BlockSpec(memory_space=pltpu.SMEM)] + [hbm] * 6,
        out_specs=(vmem, vmem),
        scratch_shapes=[
            pltpu.SMEM(dims.shape, jnp.int32),
            pltpu.VMEM(pp.shape, F32),
            pltpu.VMEM(cc.shape, F32),
            pltpu.SMEM(args[7].shape, jnp.int32),
            pltpu.SMEM(recv.shape, jnp.int32),
            pltpu.SMEM(weight.shape, F32),
            dma((6,)),
            pltpu.VMEM((ROWS, WIDTH), BF16),
            pltpu.VMEM((ROWS, WIDTH), BF16),
            pltpu.VMEM((ROWS, WIDTH), BF16),
            pltpu.VMEM((TILES, PAIR, COLT), BF16),
            pltpu.VMEM((PEERS * SLOTS, PAIR, COLT), BF16),
            pltpu.VMEM((PEERS * SLOTS, PAIR, COLT), BF16),
            pltpu.VMEM((PEERS * SLOTS, PAIR, COLT), BF16),
            pltpu.VMEM((2 * WIDTH, WIDTH), BF16),
            pltpu.VMEM((ROWS, 2 * WIDTH), BF16),
            pltpu.VMEM((BLOCKS * ROWS, COLT), F32),
            pltpu.VMEM((TILES, HEAD, COLT), F32),
            pltpu.VMEM((TILES, REST, COLT), F32),
            pltpu.VMEM((PEERS * SLOTS, HEAD, COLT), BF16),
            pltpu.VMEM((PEERS * SLOTS, REST, COLT), BF16),
            pltpu.VMEM((PEERS * SLOTS, HEAD, COLT), BF16),
            pltpu.VMEM((PEERS * SLOTS, REST, COLT), BF16),
            pltpu.VMEM((2, 8, COLT), jnp.int32),
            pltpu.SMEM((2, 8, COLT), jnp.int32),
            dma((3, LOADS)),
            dma,
            dma,
            dma,
            dma((PEERS,)),
            dma,
            dma,
            dma((2,)),
            dma((2,)),
            dma((2,)),
            dma((2,)),
            dma((2,)),
        ],
        compiler_params=pltpu.CompilerParams(
            collective_id=0, has_side_effects=True, vmem_limit_bytes=54 << 20
        ),
    )(*args)
    strip = jax.ShapeDtypeStruct(gen.shape, BF16)
    return pl.pallas_call(
        write_out,
        out_shape=(strip, strip),
        in_specs=[vmem, vmem],
        out_specs=(hbm, hbm),
        scratch_shapes=[dma((2, LOADS))],
        compiler_params=pltpu.CompilerParams(vmem_limit_bytes=6 << 20),
    )(*held)


def solution(mesh):
    return jax.shard_map(
        per_device,
        mesh=mesh,
        in_specs=(
            P("chan", "row", None),
            P("chan", "row", None),
            P("chan", "row", None),
            P("chan"),
            P(),
            P(),
            P("chan", None),
            P("chan", None, None),
            P("chan", None),
            P("chan", None),
        ),
        out_specs=(P("chan", "row", None), P("chan", "row", None)),
        check_vma=False,
    )
```

```python
import functools

import jax
import jax.numpy as jnp
from jax import lax
from jax.experimental import pallas as pl
from jax.experimental.pallas import tpu as pltpu
from jax.sharding import PartitionSpec as P

TR = 40
COLT = 128
SLOTS = 3
STEP_SIZE = 0.5
PEERS = 64
MULT = 37
MESH = pl.DeviceIdType.MESH
F32 = jnp.float32
BF16 = jnp.bfloat16

ROWS = 640
WIDTH = 1280
BLOCKS = WIDTH // COLT
PAIRS = ROWS // (2 * TR)
TILES = (ROWS // TR) * BLOCKS
HEAD = 16
REST = TR - HEAD
LOADS = 4
PAIR = 2 * TR


def spin(me, step, sign):
    off = step * MULT % PEERS
    x = lax.rem(lax.rem(me, 4) + (4 + sign * (off % 4)), 4)
    y = lax.rem(lax.rem(lax.div(me, 4), 4) + (4 + sign * (off // 4 % 4)), 4)
    z = lax.rem(lax.div(me, 16) + (4 + sign * (off // 16)), 4)
    return (z * 4 + y) * 4 + x


def rows_at(start, size, unit):
    return pl.ds(pl.multiple_of(start, unit), size)


def kernel(
    gen, mag, ham, slot_ref, dims_in, pp_in, cc_in, send_in, recv_in, weight_in,
    new_out, flow_out,
    dims_ref, pp_v, cc_ref, send_ref, recv_ref, weight_ref, small_sem,
    gen_v, mag_v, ham_v, stack, sbuf, near, far, right_near, right_far, left, base, cross_a, cross_b, tsend_a, tsend_b, trecv_a, trecv_b,
    inv_v, inv_s,
    in_sem, inv_sem, self_sem, send_sem, recv_sem, hand_sem, take_sem,
    strip_send, strip_recv, bsend_sem, brecv_sem, bself_sem,
):
    me = lax.axis_index("chan")
    row = lax.axis_index("row")
    other = 1 - row

    def load(part, start):
        for n, (src, dst) in enumerate(((gen, gen_v), (mag, mag_v), (ham, ham_v))):
            at = rows_at(part * (ROWS // LOADS), ROWS // LOADS, 16)
            copy = pltpu.make_async_copy(src.at[0, at], dst.at[at], in_sem.at[n, part])
            copy.start() if start else copy.wait()

    small = [
        pltpu.make_async_copy(src, dst, small_sem.at[n])
        for n, (src, dst) in enumerate(
            (
                (dims_in, dims_ref),
                (send_in, send_ref),
                (recv_in, recv_ref),
                (weight_in, weight_ref),
                (cc_in, cc_ref),
                (pp_in, pp_v),
            )
        )
    ]
    load(0, True)
    barrier = pltpu.get_barrier_semaphore()
    pl.semaphore_signal(barrier, inc=1, device_id={"row": other}, device_id_type=MESH)
    for step in range(1, PEERS):
        pl.semaphore_signal(
            barrier, inc=1, device_id={"chan": lax.rem(me + step, PEERS)}, device_id_type=MESH
        )
    for copy in small[:2]:
        copy.start()
    for part in range(1, LOADS):
        load(part, True)
    for copy in small[2:]:
        copy.start()

    for copy in small[:2]:
        copy.wait()
    limit = dims_ref[slot_ref[0]]

    def live(i, k):
        row_ids = row * ROWS + i * PAIR + lax.broadcasted_iota(jnp.int32, (PAIR, COLT), 0)
        col_ids = k * COLT + lax.broadcasted_iota(jnp.int32, (1, COLT), 1)
        return row_ids < jnp.where(col_ids < limit, limit, 0)

    def seat(which, k):
        half = k // (BLOCKS // 2)
        away = row if half == 0 else other
        start = away * WIDTH + which * ROWS + (k % (BLOCKS // 2)) * COLT
        return pl.ds(pl.multiple_of(start, COLT), COLT)

    def cut(i):
        at = rows_at(i * PAIR, PAIR, 16)
        for k in range(BLOCKS):
            col = pl.ds(k * COLT, COLT)
            new = (mag_v[at, col].astype(F32) + STEP_SIZE * gen_v[at, col].astype(F32)).astype(BF16)
            new_out[0, at, col] = new
            mask = live(i, k)
            m = jnp.where(mask, new.astype(F32), 0.0)
            h = jnp.where(mask, ham_v[at, col].astype(F32), 0.0)
            for top in (0, TR):
                stack[(2 * i + top // TR) * BLOCKS + k] = jnp.concatenate(
                    [m[top : top + TR], h[top : top + TR]], axis=0
                ).astype(BF16)

    def prologue(part, _):
        load(part, False)
        for sub in range(PAIRS // LOADS):
            cut(part * (PAIRS // LOADS) + sub)
        return 0

    lax.fori_loop(0, LOADS, prologue, 0)
    pl.semaphore_wait(barrier, PEERS)

    def pick(to):
        for l in range(SLOTS):
            tile = jnp.minimum(send_ref[l, 0, to], TILES - 1)
            sbuf[to * SLOTS + l] = stack[tile]

    def message(step):
        to = spin(me, step, 1)
        return pltpu.make_async_remote_copy(
            sbuf.at[pl.ds(to * SLOTS, SLOTS)],
            near.at[pl.ds(me * SLOTS, SLOTS)],
            send_sem,
            recv_sem.at[step],
            device_id={"chan": to},
            device_id_type=MESH,
        )

    def arrival(step):
        fr = spin(me, step, -1)
        return pltpu.make_async_remote_copy(
            sbuf.at[pl.ds(fr * SLOTS, SLOTS)],
            near.at[pl.ds(fr * SLOTS, SLOTS)],
            send_sem,
            recv_sem.at[step],
            device_id={"chan": fr},
            device_id_type=MESH,
        )

    def handed(step):
        at = pl.ds(spin(me, step, -1) * SLOTS, SLOTS)
        return pltpu.make_async_remote_copy(
            near.at[at], far.at[at], hand_sem, take_sem,
            device_id={"row": other}, device_id_type=MESH,
        )

    def send_out(step):
        pick(spin(me, step, 1))
        message(step).start()

    for step in range(1, PEERS):
        send_out(step)
    pick(me)
    mine = pltpu.make_async_copy(
        sbuf.at[pl.ds(me * SLOTS, SLOTS)], near.at[pl.ds(me * SLOTS, SLOTS)], self_sem
    )
    mine.start()

    for copy in small[2:]:
        copy.wait()
    chosen = lax.broadcasted_iota(jnp.int32, pp_v.shape, 0) == slot_ref[0]
    factor = jnp.sum(jnp.where(chosen, pp_v[...], 0.0), axis=0, keepdims=True)

    def strips(i, _):
        at = rows_at(i * PAIR, PAIR, 16)
        for k in range(BLOCKS):
            col = pl.ds(k * COLT, COLT)
            mask = live(i, k)
            m = jnp.where(mask, new_out[0, at, col].astype(F32), 0.0)
            h = jnp.where(mask, ham_v[at, col].astype(F32), 0.0)
            f = factor[:, k * COLT : (k + 1) * COLT]
            right_near[at, col] = h.astype(BF16)
            right_near[rows_at(ROWS + i * PAIR, PAIR, 16), col] = m.astype(BF16)
            left[at, seat(0, k)] = (m * f).astype(BF16)
            left[at, seat(1, k)] = (h * -f).astype(BF16)
            base[rows_at(k * ROWS + i * PAIR, PAIR, 8), :] = h
        return 0

    lax.fori_loop(0, PAIRS, strips, 0)

    strips_over = pltpu.make_async_remote_copy(
        right_near, right_far, strip_send, strip_recv,
        device_id={"row": other}, device_id_type=MESH,
    )
    strips_over.start()
    mine.wait()
    handed(0).start()

    place = lax.broadcasted_iota(jnp.int32, (8, COLT), 0) * COLT + lax.broadcasted_iota(
        jnp.int32, (8, COLT), 1
    )

    def invert_recv(v, table):
        return jnp.where(place == recv_ref[0, v], v, table)

    def invert_send(d, table):
        for l in range(SLOTS):
            table = jnp.where(place == send_ref[l, 0, d], d * SLOTS + l, table)
        return table

    blank = jnp.zeros((8, COLT), jnp.int32)
    inv_v[0] = lax.fori_loop(0, TILES, invert_recv, blank)
    inv_v[1] = lax.fori_loop(0, PEERS, invert_send, blank)
    inv_copy = pltpu.make_async_copy(inv_v, inv_s, inv_sem)
    inv_copy.start()

    def pp_product(half, right):
        part = jnp.dot(left[:, half], right[...], preferred_element_type=F32)
        for k in range(BLOCKS):
            base[pl.ds(k * ROWS, ROWS), :] += part[:, k * COLT : (k + 1) * COLT]

    near_half, far_half = slice(0, WIDTH), slice(WIDTH, 2 * WIDTH)
    pp_product(near_half, right_near)
    strips_over.wait_recv()
    pp_product(far_half, right_far)
    strips_over.wait_send()
    inv_copy.wait()

    def hand_on(step):
        arrival(step).wait_recv()
        handed(step).start()

    for step in range(1, PEERS):
        hand_on(step)

    def settle(tiles, right, own):
        def body(i, _):
            at = rows_at(i * PAIR, PAIR, 16)
            under = rows_at(ROWS + i * PAIR, PAIR, 16)
            for k in range(BLOCKS):
                col = pl.ds(k * COLT, COLT)
                parts = []
                for half in range(2):
                    v = (2 * i + half) * BLOCKS + k
                    tile = tiles[recv_ref[0, v]]
                    parts.append(weight_ref[0, v] * tile.astype(F32))
                m = jnp.concatenate([parts[0][:TR], parts[1][:TR]], axis=0)
                h = jnp.concatenate([parts[0][TR:], parts[1][TR:]], axis=0)
                right[at, col] = h.astype(BF16)
                right[under, col] = m.astype(BF16)
                if own:
                    f = cc_ref[:, k * COLT : (k + 1) * COLT]
                    first = rows_at(i * 2 * HEAD, 2 * HEAD, 16)
                    second = rows_at(ROWS // TR * HEAD + i * 2 * REST, 2 * REST, 16)
                    for value, side in ((m * f, seat(0, k)), (h * -f, seat(1, k))):
                        left[first, side] = jnp.concatenate(
                            [value[:HEAD], value[TR : TR + HEAD]], axis=0
                        ).astype(BF16)
                        left[second, side] = jnp.concatenate(
                            [value[HEAD:TR], value[TR + HEAD :]], axis=0
                        ).astype(BF16)
            return 0

        lax.fori_loop(0, PAIRS, body, 0)

    def product(part_rows, half, right, size, cross, add):
        part = jnp.dot(left[part_rows, half], right[...], preferred_element_type=F32)
        for a in range(ROWS // TR):
            for k in range(BLOCKS):
                block = part[a * size : (a + 1) * size, k * COLT : (k + 1) * COLT]
                tile = a * BLOCKS + k
                cross[tile] = cross[tile] + block if add else block

    head_rows, rest_rows = slice(0, ROWS // TR * HEAD), slice(ROWS // TR * HEAD, ROWS)
    settle(near, right_near, True)
    product(head_rows, near_half, right_near, HEAD, cross_a, False)
    all_handed = pltpu.make_async_remote_copy(
        near, far, hand_sem, take_sem, device_id={"row": other}, device_id_type=MESH
    )
    all_handed.wait_recv()
    settle(far, right_far, False)

    def pick_back(to, cross, tsend):
        for l in range(SLOTS):
            slot = to * SLOTS + l
            v = inv_s[0, lax.div(slot, COLT), lax.rem(slot, COLT)]
            tsend[slot] = (weight_ref[0, v] * cross[v]).astype(BF16)

    mine_at = pl.ds(me * SLOTS, SLOTS)
    parts_back = (
        (head_rows, HEAD, cross_a, tsend_a, trecv_a),
        (rest_rows, REST, cross_b, tsend_b, trecv_b),
    )
    homes = []
    for n, (part_rows, size, cross, tsend, trecv) in enumerate(parts_back):
        if n == 1:
            product(part_rows, near_half, right_near, size, cross, False)
        product(part_rows, far_half, right_far, size, cross, True)

        def send_back(step):
            to = spin(me, step, 1)
            pick_back(to, cross, tsend)
            pltpu.make_async_remote_copy(
                tsend.at[pl.ds(to * SLOTS, SLOTS)], trecv.at[mine_at], bsend_sem.at[n], brecv_sem.at[n],
                device_id={"chan": to}, device_id_type=MESH,
            ).start()

        for step in range(1, PEERS):
            send_back(step)
        pick_back(me, cross, tsend)
        homes.append(pltpu.make_async_copy(tsend.at[mine_at], trecv.at[mine_at], bself_sem.at[n]))
        homes[n].start()

    others = pl.ds(0, (PEERS - 1) * SLOTS)
    all_back = [
        pltpu.make_async_remote_copy(
            tsend.at[others], trecv.at[others], bsend_sem.at[n], brecv_sem.at[n],
            device_id={"row": other}, device_id_type=MESH,
        )
        for n, (_, _, _, tsend, trecv) in enumerate(parts_back)
    ]
    def tile_back(trecv, i, half, k):
        u = (2 * i + half) * BLOCKS + k
        return trecv[inv_s[1, lax.div(u, COLT), lax.rem(u, COLT)]].astype(F32)

    def add_heads(i, _):
        for k in range(BLOCKS):
            mask = live(i, k)
            for half in range(2):
                at = rows_at(k * ROWS + i * PAIR + half * TR, HEAD, 8)
                keep = mask[half * TR : half * TR + HEAD]
                base[at, :] += jnp.where(keep, tile_back(trecv_a, i, half, k), 0.0)
        return 0

    def finish(i, _):
        at = rows_at(i * PAIR, PAIR, 16)
        for k in range(BLOCKS):
            mask = live(i, k)
            pieces = []
            for half in range(2):
                start = k * ROWS + i * PAIR + half * TR
                keep = mask[half * TR + HEAD : (half + 1) * TR]
                pieces.append(base[rows_at(start, HEAD, 8), :])
                pieces.append(
                    base[rows_at(start + HEAD, REST, 8), :]
                    + jnp.where(keep, tile_back(trecv_b, i, half, k), 0.0)
                )
            flow_out[0, at, pl.ds(k * COLT, COLT)] = jnp.concatenate(pieces, axis=0).astype(BF16)
        return 0

    homes[0].wait()
    all_back[0].wait_recv()
    lax.fori_loop(0, PAIRS, add_heads, 0)
    homes[1].wait()
    all_back[1].wait_recv()
    lax.fori_loop(0, PAIRS, finish, 0)

    pltpu.make_async_remote_copy(
        sbuf.at[others], near.at[others], send_sem, recv_sem.at[0],
        device_id={"row": other}, device_id_type=MESH,
    ).wait_send()
    all_handed.wait_send()
    for n in range(2):
        all_back[n].wait_send()


def write_out(new, flow, new_out, flow_out, sem):
    copies = []
    for n, (src, dst) in enumerate(((new, new_out), (flow, flow_out))):
        for part in range(LOADS):
            at = pl.ds(part * (ROWS // LOADS), ROWS // LOADS)
            copies.append(pltpu.make_async_copy(src.at[0, at], dst.at[0, at], sem.at[n, part]))
    for copy in copies:
        copy.start()
    for copy in copies:
        copy.wait()


def per_device(gen, mag, ham, slot, dims, pp, cc, send, recv, weight):
    args = (gen, mag, ham, slot, dims, pp, cc, send.transpose(2, 0, 1), recv, weight)
    hbm = pl.BlockSpec(memory_space=pltpu.HBM)
    vmem = pl.BlockSpec(memory_space=pltpu.VMEM)
    dma = pltpu.SemaphoreType.DMA
    held = pl.pallas_call(
        kernel,
        out_shape=(pltpu.VMEM(gen.shape, BF16),) * 2,
        in_specs=[hbm] * 3 + [pl.BlockSpec(memory_space=pltpu.SMEM)] + [hbm] * 6,
        out_specs=(vmem, vmem),
        scratch_shapes=[
            pltpu.SMEM(dims.shape, jnp.int32),
            pltpu.VMEM(pp.shape, F32),
            pltpu.VMEM(cc.shape, F32),
            pltpu.SMEM(args[7].shape, jnp.int32),
            pltpu.SMEM(recv.shape, jnp.int32),
            pltpu.SMEM(weight.shape, F32),
            dma((6,)),
            pltpu.VMEM((ROWS, WIDTH), BF16),
            pltpu.VMEM((ROWS, WIDTH), BF16),
            pltpu.VMEM((ROWS, WIDTH), BF16),
            pltpu.VMEM((TILES, PAIR, COLT), BF16),
            pltpu.VMEM((PEERS * SLOTS, PAIR, COLT), BF16),
            pltpu.VMEM((PEERS * SLOTS, PAIR, COLT), BF16),
            pltpu.VMEM((PEERS * SLOTS, PAIR, COLT), BF16),
            pltpu.VMEM((WIDTH, WIDTH), BF16),
            pltpu.VMEM((WIDTH, WIDTH), BF16),
            pltpu.VMEM((ROWS, 2 * WIDTH), BF16),
            pltpu.VMEM((BLOCKS * ROWS, COLT), F32),
            pltpu.VMEM((TILES, HEAD, COLT), F32),
            pltpu.VMEM((TILES, REST, COLT), F32),
            pltpu.VMEM((PEERS * SLOTS, HEAD, COLT), BF16),
            pltpu.VMEM((PEERS * SLOTS, REST, COLT), BF16),
            pltpu.VMEM((PEERS * SLOTS, HEAD, COLT), BF16),
            pltpu.VMEM((PEERS * SLOTS, REST, COLT), BF16),
            pltpu.VMEM((2, 8, COLT), jnp.int32),
            pltpu.SMEM((2, 8, COLT), jnp.int32),
            dma((3, LOADS)),
            dma,
            dma,
            dma,
            dma((PEERS,)),
            dma,
            dma,
            dma,
            dma,
            dma((2,)),
            dma((2,)),
            dma((2,)),
        ],
        compiler_params=pltpu.CompilerParams(
            collective_id=0, has_side_effects=True, vmem_limit_bytes=54 << 20
        ),
    )(*args)
    strip = jax.ShapeDtypeStruct(gen.shape, BF16)
    return pl.pallas_call(
        write_out,
        out_shape=(strip, strip),
        in_specs=[vmem, vmem],
        out_specs=(hbm, hbm),
        scratch_shapes=[dma((2, LOADS))],
        compiler_params=pltpu.CompilerParams(vmem_limit_bytes=6 << 20),
    )(*held)


def solution(mesh):
    return jax.shard_map(
        per_device,
        mesh=mesh,
        in_specs=(
            P("chan", "row", None),
            P("chan", "row", None),
            P("chan", "row", None),
            P("chan"),
            P(),
            P(),
            P("chan", None),
            P("chan", None, None),
            P("chan", None),
            P("chan", None),
        ),
        out_specs=(P("chan", "row", None), P("chan", "row", None)),
        check_vma=False,
    )
```

```python
import functools

import jax
import jax.numpy as jnp
from jax import lax
from jax.experimental import pallas as pl
from jax.experimental.pallas import tpu as pltpu
from jax.sharding import PartitionSpec as P

TR = 40
COLT = 128
SLOTS = 3
STEP_SIZE = 0.5
PEERS = 64
MULT = 37
MESH = pl.DeviceIdType.MESH
F32 = jnp.float32
BF16 = jnp.bfloat16

ROWS = 640
WIDTH = 1280
BLOCKS = WIDTH // COLT
PAIRS = ROWS // (2 * TR)
TILES = (ROWS // TR) * BLOCKS
HEAD = 16
REST = TR - HEAD
LOADS = 4
BACK = 80
PAIR = 2 * TR


def spin(me, step, sign):
    off = step * MULT % PEERS
    x = lax.rem(lax.rem(me, 4) + (4 + sign * (off % 4)), 4)
    y = lax.rem(lax.rem(lax.div(me, 4), 4) + (4 + sign * (off // 4 % 4)), 4)
    z = lax.rem(lax.div(me, 16) + (4 + sign * (off // 16)), 4)
    return (z * 4 + y) * 4 + x


def rows_at(start, size, unit):
    return pl.ds(pl.multiple_of(start, unit), size)


def kernel(
    gen, mag, ham, slot_ref, dims_in, pp_in, cc_in, send_in, recv_in, weight_in,
    new_out, flow_out,
    dims_ref, pp_v, cc_ref, send_ref, recv_ref, weight_ref, small_sem,
    gen_v, mag_v, ham_v, stack, sbuf, near, far, right, left, base, cross_a, cross_b, tsend_a, tsend_b, trecv_a, trecv_b, unpacked,
    inv_v, inv_s,
    in_sem, inv_sem, self_sem, send_sem, recv_sem, hand_sem, take_sem,
    strip_send, strip_recv, bsend_sem, heads_sem, brecv_sem, bself_sem,
):
    me = lax.axis_index("chan")
    row = lax.axis_index("row")
    other = 1 - row

    def load(part, start):
        for n, (src, dst) in enumerate(((gen, gen_v), (mag, mag_v), (ham, ham_v))):
            at = rows_at(part * (ROWS // LOADS), ROWS // LOADS, 16)
            copy = pltpu.make_async_copy(src.at[0, at], dst.at[at], in_sem.at[n, part])
            copy.start() if start else copy.wait()

    small = [
        pltpu.make_async_copy(src, dst, small_sem.at[n])
        for n, (src, dst) in enumerate(
            (
                (dims_in, dims_ref),
                (send_in, send_ref),
                (recv_in, recv_ref),
                (weight_in, weight_ref),
                (cc_in, cc_ref),
                (pp_in, pp_v),
            )
        )
    ]
    load(0, True)
    barrier = pltpu.get_barrier_semaphore()
    pl.semaphore_signal(barrier, inc=1, device_id={"row": other}, device_id_type=MESH)
    for step in range(1, PEERS):
        pl.semaphore_signal(
            barrier, inc=1, device_id={"chan": lax.rem(me + step, PEERS)}, device_id_type=MESH
        )
    for copy in small[:2]:
        copy.start()
    for part in range(1, LOADS):
        load(part, True)
    for copy in small[2:]:
        copy.start()

    for copy in small[:2]:
        copy.wait()
    limit = dims_ref[slot_ref[0]]

    def live(i, k):
        row_ids = row * ROWS + i * PAIR + lax.broadcasted_iota(jnp.int32, (PAIR, COLT), 0)
        col_ids = k * COLT + lax.broadcasted_iota(jnp.int32, (1, COLT), 1)
        return row_ids < jnp.where(col_ids < limit, limit, 0)

    def cut(i):
        at = rows_at(i * PAIR, PAIR, 16)
        for k in range(BLOCKS):
            col = pl.ds(k * COLT, COLT)
            new = (mag_v[at, col].astype(F32) + STEP_SIZE * gen_v[at, col].astype(F32)).astype(BF16)
            new_out[0, at, col] = new
            mask = live(i, k)
            m = jnp.where(mask, new.astype(F32), 0.0)
            h = jnp.where(mask, ham_v[at, col].astype(F32), 0.0)
            for top in (0, TR):
                stack[(2 * i + top // TR) * BLOCKS + k] = jnp.concatenate(
                    [m[top : top + TR], h[top : top + TR]], axis=0
                ).astype(BF16)

    def prologue(part, _):
        load(part, False)
        for sub in range(PAIRS // LOADS):
            cut(part * (PAIRS // LOADS) + sub)
        return 0

    lax.fori_loop(0, LOADS, prologue, 0)
    pl.semaphore_wait(barrier, PEERS)

    def pick(to):
        for l in range(SLOTS):
            tile = jnp.minimum(send_ref[l, 0, to], TILES - 1)
            sbuf[to * SLOTS + l] = stack[tile]

    def message(step):
        to = spin(me, step, 1)
        return pltpu.make_async_remote_copy(
            sbuf.at[pl.ds(to * SLOTS, SLOTS)],
            near.at[pl.ds(me * SLOTS, SLOTS)],
            send_sem,
            recv_sem.at[step],
            device_id={"chan": to},
            device_id_type=MESH,
        )

    def arrival(step):
        fr = spin(me, step, -1)
        return pltpu.make_async_remote_copy(
            sbuf.at[pl.ds(fr * SLOTS, SLOTS)],
            near.at[pl.ds(fr * SLOTS, SLOTS)],
            send_sem,
            recv_sem.at[step],
            device_id={"chan": fr},
            device_id_type=MESH,
        )

    def handed(step):
        at = pl.ds(spin(me, step, -1) * SLOTS, SLOTS)
        return pltpu.make_async_remote_copy(
            near.at[at], far.at[at], hand_sem, take_sem,
            device_id={"row": other}, device_id_type=MESH,
        )

    def send_out(step):
        pick(spin(me, step, 1))
        message(step).start()

    for step in range(1, PEERS):
        send_out(step)
    pick(me)
    mine = pltpu.make_async_copy(
        sbuf.at[pl.ds(me * SLOTS, SLOTS)], near.at[pl.ds(me * SLOTS, SLOTS)], self_sem
    )
    mine.start()

    for copy in small[2:]:
        copy.wait()
    chosen = lax.broadcasted_iota(jnp.int32, pp_v.shape, 0) == slot_ref[0]
    factor = jnp.sum(jnp.where(chosen, pp_v[...], 0.0), axis=0, keepdims=True)

    def strips(i, _):
        at = rows_at(i * PAIR, PAIR, 16)
        for k in range(BLOCKS):
            col = pl.ds(k * COLT, COLT)
            mask = live(i, k)
            m = jnp.where(mask, new_out[0, at, col].astype(F32), 0.0)
            h = jnp.where(mask, ham_v[at, col].astype(F32), 0.0)
            f = factor[:, k * COLT : (k + 1) * COLT]
            right[rows_at(row * ROWS + i * PAIR, PAIR, 16), col] = h.astype(BF16)
            right[rows_at(WIDTH + row * ROWS + i * PAIR, PAIR, 16), col] = m.astype(BF16)
            left[at, col] = (m * f).astype(BF16)
            left[at, pl.ds(WIDTH + k * COLT, COLT)] = (h * -f).astype(BF16)
            base[rows_at(k * ROWS + i * PAIR, PAIR, 8), :] = h
        return 0

    lax.fori_loop(0, PAIRS, strips, 0)

    def strip(which, r):
        at = rows_at(which * WIDTH + r * ROWS, ROWS, 16)
        return pltpu.make_async_remote_copy(
            right.at[at], right.at[at], strip_send.at[which], strip_recv.at[which],
            device_id={"row": other}, device_id_type=MESH,
        )

    for which in range(2):
        strip(which, row).start()
    mine.wait()
    handed(0).start()

    place = lax.broadcasted_iota(jnp.int32, (8, COLT), 0) * COLT + lax.broadcasted_iota(
        jnp.int32, (8, COLT), 1
    )

    def invert_recv(v, table):
        return jnp.where(place == recv_ref[0, v], v, table)

    def invert_send(d, table):
        for l in range(SLOTS):
            table = jnp.where(place == send_ref[l, 0, d], d * SLOTS + l, table)
        return table

    blank = jnp.zeros((8, COLT), jnp.int32)
    inv_v[0] = lax.fori_loop(0, TILES, invert_recv, blank)
    inv_v[1] = lax.fori_loop(0, PEERS, invert_send, blank)
    inv_copy = pltpu.make_async_copy(inv_v, inv_s, inv_sem)
    inv_copy.start()

    for which in range(2):
        strip(which, other).wait_recv()
        strip(which, row).wait_send()

    part = jnp.dot(left[...], right[...], preferred_element_type=F32)
    for k in range(BLOCKS):
        base[pl.ds(k * ROWS, ROWS), :] += part[:, k * COLT : (k + 1) * COLT]
    inv_copy.wait()

    def hand_on(step):
        arrival(step).wait_recv()
        handed(step).start()

    for step in range(1, PEERS):
        hand_on(step)

    def settle(tiles, r, own):
        def body(i, _):
            at = rows_at(r * ROWS + i * PAIR, PAIR, 16)
            under = rows_at(WIDTH + r * ROWS + i * PAIR, PAIR, 16)
            for k in range(BLOCKS):
                col = pl.ds(k * COLT, COLT)
                parts = []
                for half in range(2):
                    v = (2 * i + half) * BLOCKS + k
                    tile = tiles[recv_ref[0, v]]
                    parts.append(weight_ref[0, v] * tile.astype(F32))
                m = jnp.concatenate([parts[0][:TR], parts[1][:TR]], axis=0)
                h = jnp.concatenate([parts[0][TR:], parts[1][TR:]], axis=0)
                right[at, col] = h.astype(BF16)
                right[under, col] = m.astype(BF16)
                if own:
                    f = cc_ref[:, k * COLT : (k + 1) * COLT]
                    first = rows_at(i * 2 * HEAD, 2 * HEAD, 16)
                    second = rows_at(ROWS // TR * HEAD + i * 2 * REST, 2 * REST, 16)
                    for value, place in ((m * f, k * COLT), (h * -f, WIDTH + k * COLT)):
                        side = pl.ds(place, COLT)
                        left[first, side] = jnp.concatenate(
                            [value[:HEAD], value[TR : TR + HEAD]], axis=0
                        ).astype(BF16)
                        left[second, side] = jnp.concatenate(
                            [value[HEAD:TR], value[TR + HEAD :]], axis=0
                        ).astype(BF16)
            return 0

        lax.fori_loop(0, PAIRS, body, 0)

    settle(near, row, True)

    all_handed = pltpu.make_async_remote_copy(
        near, far, hand_sem, take_sem, device_id={"row": other}, device_id_type=MESH
    )
    all_handed.wait_recv()
    settle(far, other, False)

    def product(start, size, cross):
        rows = left[start : start + size * (ROWS // TR), :]
        part = jnp.dot(rows, right[...], preferred_element_type=F32)
        for a in range(ROWS // TR):
            for k in range(BLOCKS):
                cross[a * BLOCKS + k] = part[a * size : (a + 1) * size, k * COLT : (k + 1) * COLT]

    def returned(to):
        for l in range(SLOTS):
            slot = to * SLOTS + l
            yield slot, inv_s[0, lax.div(slot, COLT), lax.rem(slot, COLT)]

    def pick_heads(to):
        for slot, v in returned(to):
            tsend_a[slot] = (weight_ref[0, v] * cross_a[v]).astype(BF16)

    def pick_rests(to):
        pieces = [weight_ref[0, v] * cross_b[v] for _, v in returned(to)]
        pieces.append(jnp.zeros((BACK - SLOTS * REST, COLT), F32))
        tsend_b[to] = jnp.concatenate(pieces, axis=0).astype(BF16)

    def back_heads(to, place):
        return pltpu.make_async_remote_copy(
            tsend_a.at[pl.ds(to * SLOTS, SLOTS)], trecv_a.at[pl.ds(place * SLOTS, SLOTS)],
            bsend_sem.at[0], heads_sem, device_id={"chan": to}, device_id_type=MESH,
        )

    def back_rests(step, to, place):
        return pltpu.make_async_remote_copy(
            tsend_b.at[to], trecv_b.at[place],
            bsend_sem.at[1], brecv_sem.at[step], device_id={"chan": to}, device_id_type=MESH,
        )

    product(0, HEAD, cross_a)
    for step in range(1, PEERS):
        to = spin(me, step, 1)
        pick_heads(to)
        back_heads(to, me).start()
    pick_heads(me)
    mine_at = pl.ds(me * SLOTS, SLOTS)
    home_heads = pltpu.make_async_copy(tsend_a.at[mine_at], trecv_a.at[mine_at], bself_sem.at[0])
    home_heads.start()

    product(ROWS // TR * HEAD, REST, cross_b)
    for step in range(1, PEERS):
        to = spin(me, step, 1)
        pick_rests(to)
        back_rests(step, to, me).start()
    pick_rests(me)
    home_rests = pltpu.make_async_copy(tsend_b.at[me], trecv_b.at[me], bself_sem.at[1])
    home_rests.start()

    others = pl.ds(0, (PEERS - 1) * SLOTS)
    all_heads = pltpu.make_async_remote_copy(
        tsend_a.at[others], trecv_a.at[others], bsend_sem.at[0], heads_sem,
        device_id={"row": other}, device_id_type=MESH,
    )
    all_rests = pltpu.make_async_remote_copy(
        tsend_b.at[pl.ds(0, PEERS - 1)], trecv_b.at[pl.ds(0, PEERS - 1)], bsend_sem.at[1],
        brecv_sem.at[0], device_id={"row": other}, device_id_type=MESH,
    )

    def unpack(fr):
        rows = trecv_b[fr].astype(F32)
        for l in range(SLOTS):
            unpacked[fr * SLOTS + l] = rows[l * REST : (l + 1) * REST]

    def tile_back(trecv, i, half, k):
        u = (2 * i + half) * BLOCKS + k
        return trecv[inv_s[1, lax.div(u, COLT), lax.rem(u, COLT)]]

    def add_heads(i, _):
        for k in range(BLOCKS):
            mask = live(i, k)
            for half in range(2):
                at = rows_at(k * ROWS + i * PAIR + half * TR, HEAD, 8)
                keep = mask[half * TR : half * TR + HEAD]
                base[at, :] += jnp.where(keep, tile_back(trecv_a, i, half, k).astype(F32), 0.0)
        return 0

    def finish(i, _):
        at = rows_at(i * PAIR, PAIR, 16)
        for k in range(BLOCKS):
            mask = live(i, k)
            pieces = []
            for half in range(2):
                start = k * ROWS + i * PAIR + half * TR
                keep = mask[half * TR + HEAD : (half + 1) * TR]
                pieces.append(base[rows_at(start, HEAD, 8), :])
                pieces.append(
                    base[rows_at(start + HEAD, REST, 8), :]
                    + jnp.where(keep, tile_back(unpacked, i, half, k), 0.0)
                )
            flow_out[0, at, pl.ds(k * COLT, COLT)] = jnp.concatenate(pieces, axis=0).astype(BF16)
        return 0

    home_heads.wait()
    all_heads.wait_recv()
    lax.fori_loop(0, PAIRS, add_heads, 0)
    home_rests.wait()
    unpack(me)
    for step in range(1, PEERS):
        fr = spin(me, step, -1)
        back_rests(step, fr, fr).wait_recv()
        unpack(fr)
    lax.fori_loop(0, PAIRS, finish, 0)

    pltpu.make_async_remote_copy(
        sbuf.at[others], near.at[others], send_sem, recv_sem.at[0],
        device_id={"row": other}, device_id_type=MESH,
    ).wait_send()
    all_handed.wait_send()
    all_heads.wait_send()
    all_rests.wait_send()


def write_out(new, flow, new_out, flow_out, sem):
    copies = []
    for n, (src, dst) in enumerate(((new, new_out), (flow, flow_out))):
        for part in range(LOADS):
            at = pl.ds(part * (ROWS // LOADS), ROWS // LOADS)
            copies.append(pltpu.make_async_copy(src.at[0, at], dst.at[0, at], sem.at[n, part]))
    for copy in copies:
        copy.start()
    for copy in copies:
        copy.wait()


def per_device(gen, mag, ham, slot, dims, pp, cc, send, recv, weight):
    args = (gen, mag, ham, slot, dims, pp, cc, send.transpose(2, 0, 1), recv, weight)
    hbm = pl.BlockSpec(memory_space=pltpu.HBM)
    vmem = pl.BlockSpec(memory_space=pltpu.VMEM)
    dma = pltpu.SemaphoreType.DMA
    held = pl.pallas_call(
        kernel,
        out_shape=(pltpu.VMEM(gen.shape, BF16),) * 2,
        in_specs=[hbm] * 3 + [pl.BlockSpec(memory_space=pltpu.SMEM)] + [hbm] * 6,
        out_specs=(vmem, vmem),
        scratch_shapes=[
            pltpu.SMEM(dims.shape, jnp.int32),
            pltpu.VMEM(pp.shape, F32),
            pltpu.VMEM(cc.shape, F32),
            pltpu.SMEM(args[7].shape, jnp.int32),
            pltpu.SMEM(recv.shape, jnp.int32),
            pltpu.SMEM(weight.shape, F32),
            dma((6,)),
            pltpu.VMEM((ROWS, WIDTH), BF16),
            pltpu.VMEM((ROWS, WIDTH), BF16),
            pltpu.VMEM((ROWS, WIDTH), BF16),
            pltpu.VMEM((TILES, PAIR, COLT), BF16),
            pltpu.VMEM((PEERS * SLOTS, PAIR, COLT), BF16),
            pltpu.VMEM((PEERS * SLOTS, PAIR, COLT), BF16),
            pltpu.VMEM((PEERS * SLOTS, PAIR, COLT), BF16),
            pltpu.VMEM((2 * WIDTH, WIDTH), BF16),
            pltpu.VMEM((ROWS, 2 * WIDTH), BF16),
            pltpu.VMEM((BLOCKS * ROWS, COLT), F32),
            pltpu.VMEM((TILES, HEAD, COLT), F32),
            pltpu.VMEM((TILES, REST, COLT), F32),
            pltpu.VMEM((PEERS * SLOTS, HEAD, COLT), BF16),
            pltpu.VMEM((PEERS, BACK, COLT), BF16),
            pltpu.VMEM((PEERS * SLOTS, HEAD, COLT), BF16),
            pltpu.VMEM((PEERS, BACK, COLT), BF16),
            pltpu.VMEM((PEERS * SLOTS, REST, COLT), F32),
            pltpu.VMEM((2, 8, COLT), jnp.int32),
            pltpu.SMEM((2, 8, COLT), jnp.int32),
            dma((3, LOADS)),
            dma,
            dma,
            dma,
            dma((PEERS,)),
            dma,
            dma,
            dma((2,)),
            dma((2,)),
            dma((2,)),
            dma,
            dma((PEERS,)),
            dma((2,)),
        ],
        compiler_params=pltpu.CompilerParams(
            collective_id=0, has_side_effects=True, vmem_limit_bytes=54 << 20
        ),
    )(*args)
    strip = jax.ShapeDtypeStruct(gen.shape, BF16)
    return pl.pallas_call(
        write_out,
        out_shape=(strip, strip),
        in_specs=[vmem, vmem],
        out_specs=(hbm, hbm),
        scratch_shapes=[dma((2, LOADS))],
        compiler_params=pltpu.CompilerParams(vmem_limit_bytes=6 << 20),
    )(*held)


def solution(mesh):
    return jax.shard_map(
        per_device,
        mesh=mesh,
        in_specs=(
            P("chan", "row", None),
            P("chan", "row", None),
            P("chan", "row", None),
            P("chan"),
            P(),
            P(),
            P("chan", None),
            P("chan", None, None),
            P("chan", None),
            P("chan", None),
        ),
        out_specs=(P("chan", "row", None), P("chan", "row", None)),
        check_vma=False,
    )
```
